32 devices in a mesh: dp: 32 (over z, y, x, core).
Axes of the slice: x: 2, y: 2, z: 4, core: 2. Of those that a mesh axis runs over, the one named last changes fastest.
Arguments:
- features: bfloat16 [23360, 40], P('dp'), may hold values from -6 to 6
- ivectors: bfloat16 [128, 100], P('dp'), may hold values from -6 to 6
- frame_mask: int32 [23360], P('dp'), may hold values from 0 to 1, as said below
- labels: int32 [23360], P('dp'), may hold values from 0 to 6015
- confidence: float32 [23360], P('dp'), may hold values from 0.25 to 1
- weights: float32 [32, 101696], P('dp'), as said below
- first_moment: float32 [32, 101696], P('dp'), may hold values from -0.0008544922 to 0.0008544922
- second_moment: float32 [32, 101696], P('dp'), may hold values from 1.532043e-10 to 2.4512687e-09
- biases: float32 [9344], replicated, may hold values from -3 to 3
- bias_first: float32 [9344], replicated, may hold values from -0.0024414062 to 0.0024414062
- bias_second: float32 [9344], replicated, may hold values from 1.3788387e-09 to 2.206142e-08
Outputs:
- new_weights: float32 [32, 101696], P('dp')
- new_first: float32 [32, 101696], P('dp')
- new_second: float32 [32, 101696], P('dp')
- new_biases: float32 [9344], replicated
- new_bias_first: float32 [9344], replicated
- new_bias_second: float32 [9344], replicated
- loss_sum: float32 [], replicated
- loss_weight: float32 [], replicated
- grad_norm: float32 [], replicated
The draws below stay inside these ranges and needn't reach their ends.
Inputs may be any that keep to these rules, and one draw needn't show every extreme that they name: `frame_mask`: in each span the frames that count form a leading run of at least one frame; some span counts all its frames. Master weights of the five matrices, scaled by their fan-in.
All inputs are finite; a program needn't handle non-finite values.
Results may differ from the reference program's by a relative error of at most 0.0066.
Values may be sent and summed in bfloat16 or wider, within the bound.
No kernel may reach another device: no remote copies, remote signals or barrier semaphores. Data moves between devices by JAX's collectives and lax.ppermute only.
A program may use at most 256 MiB of HBM per device.

```python
import math
import jax
import jax.numpy as jnp
import numpy as np
from jax import lax

FEAT = 40
IVEC = 100
HID = 1536
BOT = 160
PRE = 256
SEN = 6016
L1 = 140
L2 = 150
L3 = 300
C1 = 2
C2 = 1
C3 = 1
STEP = 10
FR_DEV = 730
FRAMES = 23360
SPANS = 128
PARAMS = 3254272
NBIAS = 9344
SHARD = 101696
N_DP = 32


def draw_frame_mask(key, part):
    key = jax.random.fold_in(key, 1)
    count = C1 + C2 + C3
    ratio = jax.random.randint(key, (N_DP, count), 60, 101)
    device = jnp.arange(N_DP, dtype=jnp.int32)[:, None]
    span = jnp.arange(count, dtype=jnp.int32)[None, :]
    length_of = jnp.where(span < C1, L1, jnp.where(span < C1 + C2, L2, L3))
    live = length_of * (N_DP + 2 * device) * ratio // (300 * N_DP)
    live = jnp.maximum(live, 1)
    live = jnp.where((device == N_DP - 1) & (span == 0), length_of, live)
    span_list = []
    place_list = []
    index = 0
    for spans, length in ((C1, L1), (C2, L2), (C3, L3)):
        for step in range(spans):
            span_list.append(np.full(length, index, np.int32))
            place_list.append(np.arange(length, dtype=np.int32))
            index = index + 1
    span_of = jnp.asarray(np.concatenate(span_list))
    place_of = jnp.asarray(np.concatenate(place_list))
    mask = (place_of[None, :] < live[:, span_of]).astype(jnp.int32)
    return mask.reshape(-1)


def draw_weights(key, part):
    key = jax.random.fold_in(key, 2)
    total = N_DP * SHARD
    raw = jax.random.normal(key, (total,), jnp.float32)
    index = jnp.arange(total, dtype=jnp.int32)
    first_end = (3 * FEAT + IVEC) * HID
    second_end = first_end + 2 * HID * BOT
    third_end = second_end + 2 * BOT * HID
    fourth_end = third_end + HID * PRE
    scale = jnp.where(index < first_end, (3 * FEAT + IVEC) ** (-0.5), jnp.where(index < second_end, (2 * HID) ** (-0.5), jnp.where(index < third_end, (2 * BOT) ** (-0.5), jnp.where(index < fourth_end, HID ** (-0.5), PRE ** (-0.5))))).astype(jnp.float32)
    return (raw * scale).reshape(N_DP, SHARD)


def with_ends(entries, key, least, largest):
    extent = entries.shape
    index_at = [jax.random.randint(jax.random.fold_in(key, axis), (), 0, extent[axis]) for axis in range(len(extent))]
    entries = entries.at[tuple(index_at)].set(least)
    longest = extent.index(max(extent))
    index_at[longest] = (index_at[longest] + 1) % extent[longest]
    return entries.at[tuple(index_at)].set(largest)


def shard_levels(key, shape, cuts, smallest, top_value):
    gain, own = 1.0, jax.random.fold_in(key, 6)
    for position, blocks in cuts:
        heights = jnp.exp(jax.random.uniform(jax.random.fold_in(own, position), (blocks,), jnp.float32, smallest / len(cuts), top_value / len(cuts)))
        gain = gain * jnp.repeat(heights, shape[position] // blocks).reshape([-1 if axis == position else 1 for axis in range(len(shape))])
    return gain


def gaussian(rng, dims, width, reach, shards=(), kind=jnp.bfloat16):
    entries = jax.random.normal(rng, dims, jnp.float32) * width
    if len(shards) > 0:
        entries = shard_levels(rng, dims, shards, -0.22, 0.18) * entries
    return jnp.clip(entries, min=-reach, max=reach).astype(kind)


def setup_inputs(seed: int = 0) -> dict:
    key_of = jax.random.split(jax.random.key(seed), 12)
    return {
        "features": gaussian(key_of[0], (FRAMES, FEAT), 1.0, 6.0, ((0, 32),)),
        "ivectors": gaussian(key_of[1], (SPANS, IVEC), 1.0, 6.0, ((0, 32),)),
        "frame_mask": draw_frame_mask(jax.random.fold_in(key_of[11], 71), 0),
        "labels": with_ends(jax.random.randint(key_of[3], (FRAMES,), 0, SEN), jax.random.fold_in(key_of[3], 1), 0, SEN - 1).astype(jnp.int32),
        "confidence": jnp.clip(jnp.exp(math.log(1.0) - 1.3862944 * jax.random.uniform(key_of[4], (FRAMES,), jnp.float32) ** shard_levels(key_of[4], (FRAMES,), ((0, 32),), -0.2, 0.2)), 0.25, 1.0),
        "weights": draw_weights(jax.random.fold_in(key_of[11], 71), 0),
        "first_moment": gaussian(key_of[6], (N_DP, SHARD), (0.11 / (PARAMS + NBIAS) ** 0.5), 0.0008544922, ((0, 32),), jnp.float32),
        "second_moment": jnp.clip(jnp.exp(math.log(2.4512687435418457e-09) - 2.7725887 * jax.random.uniform(key_of[7], (N_DP, SHARD), jnp.float32) ** shard_levels(key_of[7], (N_DP, SHARD), ((0, 32),), -0.2, 0.2)), 1.5320429647136535e-10, 2.4512687435418457e-09),
        "biases": gaussian(key_of[8], (NBIAS,), 0.2, 3.0, (), jnp.float32),
        "bias_first": gaussian(key_of[9], (NBIAS,), (0.33 / (PARAMS + NBIAS) ** 0.5), 0.0024414062, (), jnp.float32),
        "bias_second": jnp.clip(jnp.exp(jax.random.uniform(key_of[10], (NBIAS,), jnp.float32, math.log(1.3788387098756516e-09), math.log(2.2061419358010426e-08))), 1.3788387098756516e-09, 2.2061419358010426e-08),
    }


bypass_scale = 0.66
norm_eps = 0.001
learn_rate = 0.05
beta_one = 0.9
beta_two = 0.999
adam_eps = 1e-08
decay_rate = 0.01
clip_norm = 1.0

@jax.custom_vjp
def low(v):
    return lax.optimization_barrier(v.astype(jnp.bfloat16)).astype(jnp.float32)

@jax.custom_vjp
def low_back(v):
    return v

def low_keep(v):
    return (low(v), None)

def low_pass(kept, grad):
    return (grad,)

def back_keep(v):
    return (v, None)

def back_low(kept, grad):
    return (low(grad),)
low.defvjp(low_keep, low_pass)
low_back.defvjp(back_keep, back_low)

def matmul(a, b):
    return jnp.einsum('...i,ij->...j', a, b, precision=lax.Precision.HIGHEST)

def earlier(v):
    return jnp.pad(v, ((0, 0), (1, 0), (0, 0)))[:, :-1]

def later(v):
    return jnp.pad(v, ((0, 0), (0, 1), (0, 0)))[:, 1:]

def unpack(flat):
    shapes = [(3 * FEAT + IVEC, HID), (2 * HID, BOT), (2 * BOT, HID), (HID, PRE), (PRE, SEN)]
    result = []
    start = 0
    for rows, cols in shapes:
        result.append(flat[start:start + rows * cols].reshape(rows, cols))
        start = start + rows * cols
    return result

def split_bias(bias):
    return (bias[:HID], bias[HID:2 * HID], bias[2 * HID:2 * HID + PRE], bias[2 * HID + PRE:])

def normalize(h, mask):
    wide = mask[:, :, None]
    count = jnp.sum(mask)
    mean = lax.optimization_barrier(jnp.sum(wide * h, axis=(0, 1))) / count
    var = lax.optimization_barrier(jnp.sum(wide * h * h, axis=(0, 1))) / count - mean * mean
    return (h - mean) * lax.rsqrt(var + norm_eps)

def head_loss(pre, w_out, b_out, labels, weight):
    logits = low_back(matmul(pre, w_out) + b_out)
    top = lax.optimization_barrier(jnp.max(logits, axis=-1, keepdims=True))
    lse = jnp.log(lax.optimization_barrier(jnp.sum(jnp.exp(logits - top), axis=-1))) + top[..., 0]
    picked = jnp.take_along_axis(logits, labels[..., None], axis=-1)[..., 0]
    return jnp.sum(weight * (lse - picked))

def micro(mats, parts, feats, ivecs, mask, labels, weight, spans):
    w_in, w_first, w_second, w_pre, w_out = mats
    b_in, b_second, b_pre, b_out = parts
    length = feats.shape[1]
    ivec_wide = jnp.broadcast_to(ivecs[:, None, :], (ivecs.shape[0], length, IVEC))
    spliced = low(jnp.concatenate([earlier(feats), feats, later(feats), ivec_wide], axis=-1))
    act_in = low_back(matmul(spliced, w_in) + b_in)
    norm_in = normalize(jax.nn.gelu(act_in), mask)
    rounded = low(norm_in)
    factor = low_back(low(matmul(earlier(rounded), w_first[:HID]) + matmul(rounded, w_first[HID:])))
    act_mid = low_back(matmul(factor, w_second[:BOT]) + matmul(later(factor), w_second[BOT:]) + b_second)
    norm_mid = normalize(jax.nn.gelu(act_mid), mask)
    summed = low(norm_mid + bypass_scale * norm_in)
    pre = low_back(low(matmul(summed, w_pre) + b_pre))
    shape = (N_DP, spans * length)
    blocks = (pre.reshape(shape + (PRE,)), labels.reshape(shape), weight.reshape(shape))
    head = jax.checkpoint(head_loss)
    losses = lax.map(lambda item: head(item[0], w_out, b_out, item[1], item[2]), blocks)
    return jnp.sum(losses)

def reference(features, ivectors, frame_mask, labels, confidence, weights, first_moment, second_moment, biases, bias_first, bias_second):
    feats = features.astype(jnp.float32).reshape(N_DP, FR_DEV, FEAT)
    ivecs = ivectors.astype(jnp.float32).reshape(N_DP, C1 + C2 + C3, IVEC)
    masks = frame_mask.astype(jnp.float32).reshape(N_DP, FR_DEV)
    labs = labels.reshape(N_DP, FR_DEV)
    weight_all = (confidence * frame_mask.astype(jnp.float32)).reshape(N_DP, FR_DEV)
    groups = ((C1, L1), (C2, L2), (C3, L3))

    def loss_of(flat, bias):
        mats = unpack(low(flat.reshape(-1)))
        parts = split_bias(bias)
        total = jnp.float32(0.0)
        frame = 0
        span = 0
        for spans, length in groups:
            size = spans * length

            def cut(a):
                return a[:, frame:frame + size].reshape((N_DP * spans, length) + a.shape[2:])
            iv = ivecs[:, span:span + spans].reshape(N_DP * spans, IVEC)
            total = total + micro(mats, parts, cut(feats), iv, cut(masks), cut(labs), cut(weight_all), spans)
            frame = frame + size
            span = span + spans
        return total
    loss_sum, pullback = jax.vjp(loss_of, weights, biases)
    grad_w, grad_b = pullback(jnp.float32(1.0))
    grad_norm = jnp.sqrt(jnp.sum(grad_w * grad_w) + jnp.sum(grad_b * grad_b))
    scale = jnp.minimum(jnp.float32(1.0), clip_norm / grad_norm)

    def adam(value, grad, first, second, decay):
        grad = grad * scale
        first = beta_one * first + (1.0 - beta_one) * grad
        second = beta_two * second + (1.0 - beta_two) * grad * grad
        first_hat = first / (1.0 - beta_one ** STEP)
        second_hat = second / (1.0 - beta_two ** STEP)
        value = value - learn_rate * (first_hat / (jnp.sqrt(second_hat) + adam_eps) + decay * value)
        return (value, first, second)
    new_w, new_m, new_v = adam(weights, grad_w, first_moment, second_moment, decay_rate)
    new_b, new_bm, new_bv = adam(biases, grad_b, bias_first, bias_second, 0.0)
    loss_weight = jnp.sum(weight_all)
    return (new_w, new_m, new_v, new_b, new_bm, new_bv, loss_sum, loss_weight, grad_norm)
```

```python
import math

import jax
import jax.numpy as jnp
from jax import lax
from jax.experimental import pallas as pl
from jax.experimental.pallas import tpu as pltpu
from jax.sharding import PartitionSpec as P

FEAT = 40
IVEC = 100
HID = 1536
BOT = 160
PRE = 256
SEN = 6016
SPAN = (140, 140, 150, 300)
START = (0, 144, 288, 448)
ROWS = 768
SEGS = ((0, 288), (288, 448), (448, 768))
SENP = 6144
STEP = 10
NBIAS = 9344

bypass_scale = 0.66
norm_eps = 0.001
learn_rate = 0.05
beta_one = 0.9
beta_two = 0.999
adam_eps = 1e-08
decay_rate = 0.01
clip_norm = 1.0

F32 = jnp.float32
BF = jnp.bfloat16
VM = pl.BlockSpec(memory_space=pltpu.VMEM)
ANY = pl.BlockSpec(memory_space=pl.ANY)
SM = pl.BlockSpec(memory_space=pltpu.SMEM)

CHIP = 1589
BLK = 800
LAYERS = (0, 1, 3, 2)
OFF = (0, 2640, 6480, 10320, 13392)
ROWS_ALL = 16 * CHIP
TILE = 256
NT = HID // TILE
WIDE = 512
NW = SENP // WIDE
GELU_C = math.sqrt(2.0 / math.pi)


def shape(dims, kind=F32):
    return jax.ShapeDtypeStruct(dims, kind)


def params(mb=60):
    return pltpu.CompilerParams(vmem_limit_bytes=mb * 2**20)


def dot(a, b):
    return jnp.dot(a, b, preferred_element_type=F32)


def dot_nt(a, b):
    return lax.dot_general(a, b, (((1,), (1,)), ((), ())), preferred_element_type=F32)


def at(j, size):
    return pl.ds(pl.multiple_of(j * size, size), size)


def unpack_kernel(me, *refs):
    arrs = refs[:8]
    win, w1a, w1b, w2a, w2b, wp, wo = refs[8:15]
    stage, flat, tall, tall2, sem = refs[15:]
    copies = []
    for i in range(8):
        for j in range(4):
            z = lax.rem(me[0] + (4 - LAYERS[i % 4]), 4)
            y = me[1] ^ (j >> 1)
            x = me[2] ^ (j & 1)
            c = me[3] ^ (i // 4)
            d = ((z * 2 + y) * 2 + x) * 2 + c
            copy = pltpu.make_async_copy(arrs[i].at[j], stage.at[d], sem.at[i * 4 + j])
            copy.start()
            copies.append(copy)
    for copy in copies:
        copy.wait()
    for b in range(32):
        base = CHIP * (b // 2) + 794 * (b % 2)
        v = stage[b].astype(F32)
        if b % 2 == 0:
            flat[base : base + 795, :] = v[:795]
        else:
            flat[base : base + 1, :] = flat[base : base + 1, :] + v[0:1]
            flat[base + 1 : base + 795, :] = v[1:795]
    for j in range(12):
        v = flat[pl.ds(j, 224, stride=12), :]
        v = jnp.where(lax.broadcasted_iota(jnp.int32, (224, 128), 0) < 220, v, 0.0)
        win[0:224, 128 * j : 128 * j + 128] = v.astype(BF)
    win[224:256, :] = jnp.zeros((32, HID), BF)
    for j in range(12):
        v = flat[pl.ds(OFF[2] + j, 320, stride=12), :].astype(BF)
        w2a[0:160, 128 * j : 128 * j + 128] = v[:160]
        w2b[0:160, 128 * j : 128 * j + 128] = v[160:]
    w2a[160:256, :] = jnp.zeros((96, HID), BF)
    w2b[160:256, :] = jnp.zeros((96, HID), BF)
    for j in range(2):
        wp[:, 128 * j : 128 * j + 128] = flat[pl.ds(OFF[3] + j, 1536, stride=2), :].astype(BF)
    for j in range(47):
        wo[:, 128 * j : 128 * j + 128] = flat[pl.ds(OFF[4] + j, 256, stride=47), :].astype(BF)
    wo[:, 6016:] = jnp.zeros((256, 128), BF)
    lane = lax.broadcasted_iota(jnp.int32, (768, 128), 1)
    a = [flat[pl.ds(OFF[1] + q, 768, stride=5), :] for q in range(5)]

    def put(r, t0, t1):
        tall[pl.ds(r, 768, stride=4), :] = t0
        tall2[pl.ds(r, 768, stride=4), :] = jnp.where(lane < 32, t1, 0.0)

    put(0, a[0], a[1])
    for r in (1, 2, 3):
        turn = 128 - 32 * r
        low = pltpu.roll(a[r], turn, 1)
        high = pltpu.roll(a[r + 1], turn, 1)
        put(r, jnp.where(lane < turn, low, high), high)
    for out, first in ((w1a, 0), (w1b, 1536)):
        out[:, 0:128] = tall[first : first + 1536, :].astype(BF)
        out[:, 128:256] = tall2[first : first + 1536, :].astype(BF)


def unpack(me, arrs):
    outs = (
        shape((256, HID), BF),
        shape((HID, 256), BF),
        shape((HID, 256), BF),
        shape((256, HID), BF),
        shape((256, HID), BF),
        shape((HID, PRE), BF),
        shape((PRE, SENP), BF),
    )
    return pl.pallas_call(
        unpack_kernel,
        out_shape=outs,
        in_specs=[SM] + [ANY] * 8,
        out_specs=(VM,) * 7,
        scratch_shapes=[
            pltpu.VMEM((32, BLK, 128), BF),
            pltpu.VMEM((ROWS_ALL + 64, 128), F32),
            pltpu.VMEM((3072, 128), F32),
            pltpu.VMEM((3072, 128), F32),
            pltpu.SemaphoreType.DMA((32,)),
        ],
        compiler_params=params(),
        name="unpack",
    )(me, *arrs)


def pack_kernel(me, gin, g1a, g1b, g2a, g2b, gp, go, keep, send, flat, tall, tall2):
    for j in range(12):
        flat[pl.ds(j, 220, stride=12), :] = gin[0:220, 128 * j : 128 * j + 128]
    for out, first in ((g1a, 0), (g1b, 1536)):
        tall[first : first + 1536, :] = out[:, 0:128]
        tall2[first : first + 1536, :] = out[:, 128:256]
    lane = lax.broadcasted_iota(jnp.int32, (768, 128), 1)
    t0 = [tall[pl.ds(r, 768, stride=4), :] for r in range(4)]
    t1 = [tall2[pl.ds(r, 768, stride=4), :] for r in range(4)]
    flat[pl.ds(OFF[1], 768, stride=5), :] = t0[0]
    for q in (1, 2, 3):
        tail = t1[q - 1] if q == 1 else jnp.where(
            lane < 32 * (q - 1), pltpu.roll(t0[q - 1], 32 * (q - 1), 1), pltpu.roll(t1[q - 1], 32 * (q - 1), 1)
        )
        flat[pl.ds(OFF[1] + q, 768, stride=5), :] = jnp.where(
            lane < 32 * q, tail, pltpu.roll(t0[q], 32 * q, 1)
        )
    flat[pl.ds(OFF[1] + 4, 768, stride=5), :] = jnp.where(
        lane < 96, pltpu.roll(t0[3], 96, 1), pltpu.roll(t1[3], 96, 1)
    )
    for j in range(12):
        flat[pl.ds(OFF[2] + j, 160, stride=12), :] = g2a[0:160, 128 * j : 128 * j + 128]
        flat[pl.ds(OFF[2] + 1920 + j, 160, stride=12), :] = g2b[0:160, 128 * j : 128 * j + 128]
    for j in range(2):
        flat[pl.ds(OFF[3] + j, 1536, stride=2), :] = gp[:, 128 * j : 128 * j + 128]
    for j in range(47):
        flat[pl.ds(OFF[4] + j, 256, stride=47), :] = go[:, 128 * j : 128 * j + 128].astype(F32)
    for dc, out in ((0, keep), (1, send)):
        for r in range(4):
            for j in range(4):
                z = lax.rem(me[0] + r, 4)
                y = me[1] ^ (j >> 1)
                x = me[2] ^ (j & 1)
                c = me[3] ^ dc
                base = ((z * 2 + y) * 2 + x) * CHIP + c * 794
                out[r, j] = flat[pl.ds(base, BLK), :].astype(BF)


def pack(me, *grads):
    return pl.pallas_call(
        pack_kernel,
        out_shape=(shape((4, 4, BLK, 128), BF),) * 2,
        in_specs=[SM] + [VM] * 7,
        out_specs=(VM,) * 2,
        scratch_shapes=[
            pltpu.VMEM((ROWS_ALL + 64, 128), F32),
            pltpu.VMEM((3072, 128), F32),
            pltpu.VMEM((3072, 128), F32),
        ],
        compiler_params=params(),
        name="pack",
    )(me, *grads)


def gelu_parts(act):
    square = act * act
    t = jnp.tanh(GELU_C * act * (1.0 + 0.044715 * square))
    cdf = 0.5 + 0.5 * t
    slope = cdf + (0.5 * act) * (1.0 - t * t) * (GELU_C + (3 * 0.044715 * GELU_C) * square)
    return act * cdf, slope


def put_sums(st, first, v):
    for s, (a, b) in enumerate(SEGS):
        st[first + s : first + s + 1, :] = jnp.sum(v[a:b], axis=0, keepdims=True)


def norm_rows(tot, s, cols):
    count = tot[6:7, s : s + 1]
    mean = tot[s : s + 1, cols] / count
    var = tot[3 + s : 4 + s, cols] / count - mean * mean
    return mean, lax.rsqrt(var + norm_eps)


def put_stats(st, hidden, mask):
    masked = hidden * mask
    put_sums(st, 0, masked)
    put_sums(st, 3, masked * hidden)
    lane = lax.broadcasted_iota(jnp.int32, (2, TILE), 1)
    counts = [jnp.sum(mask[a:b], axis=0, keepdims=True) for a, b in SEGS]
    st[6:8, :] = jnp.where(lane == 0, counts[0], jnp.where(lane == 1, counts[1], counts[2]))


def in_kernel(spl, w, b, rowm, h, gp, st):
    act = dot(spl[...], w[...]) + b[...]
    hidden, slope = gelu_parts(act)
    h[...] = hidden
    gp[...] = slope
    put_stats(st, hidden, rowm[:, 0:1])


def layer_in(spliced, w_in, b_in, rowm):
    col = lambda rows: pl.BlockSpec((rows, TILE), lambda i: (0, i))
    full = lambda c: pl.BlockSpec((ROWS, c), lambda i: (0, 0))
    return pl.pallas_call(
        in_kernel,
        grid=(NT,),
        out_shape=(shape((ROWS, HID)), shape((ROWS, HID)), shape((8, HID))),
        in_specs=[full(256), col(256), col(1), full(8)],
        out_specs=(col(ROWS), col(ROWS), col(8)),
        compiler_params=params(),
        name="layer_in",
    )(spliced, w_in, b_in, rowm)


def mid_kernel(h, tot, w1a, w1b, w2a, w2b, b2, rowm, rounded, fac, fnext, h2, gp2, st, ua, ub):
    i = pl.program_id(0)
    valid = rowm[:, 2:3]

    @pl.when(i < NT)
    def _():
        cols = at(i, TILE)
        for s, (a, b) in enumerate(SEGS):
            mean, scale = norm_rows(tot, s, cols)
            rounded[a:b, :] = ((h[a:b, :] - mean) * scale).astype(BF)
        pa = dot(rounded[...], w1a[...])
        pb = dot(rounded[...], w1b[...])

        @pl.when(i == 0)
        def _():
            ua[...] = pa
            ub[...] = pb

        @pl.when(i > 0)
        def _():
            ua[...] += pa
            ub[...] += pb

        @pl.when(i == NT - 1)
        def _():
            f = ((ub[...] + pltpu.roll(ua[...] * valid, 1, 0)) * valid).astype(BF)
            fac[...] = f
            fnext[...] = (pltpu.roll(f.astype(F32), ROWS - 1, 0) * valid).astype(BF)

    @pl.when(i >= NT)
    def _():
        act = dot(fac[...], w2a[...]) + dot(fnext[...], w2b[...]) + b2[...]
        hidden, slope = gelu_parts(act)
        h2[...] = hidden
        gp2[...] = slope
        put_stats(st, hidden, rowm[:, 0:1])


def layer_mid(h, tot, w1a, w1b, w2a, w2b, b2, rowm):
    first = lambda i: jnp.minimum(i, NT - 1)
    second = lambda i: jnp.maximum(i - NT, 0)
    fcol = lambda rows: pl.BlockSpec((rows, TILE), lambda i: (0, first(i)))
    scol = lambda rows: pl.BlockSpec((rows, TILE), lambda i: (0, second(i)))
    frow = pl.BlockSpec((TILE, 256), lambda i: (first(i), 0))
    full = lambda r, c: pl.BlockSpec((r, c), lambda i: (0, 0))
    return pl.pallas_call(
        mid_kernel,
        grid=(2 * NT,),
        out_shape=(
            shape((ROWS, HID), BF),
            shape((ROWS, 256), BF),
            shape((ROWS, 256), BF),
            shape((ROWS, HID)),
            shape((ROWS, HID)),
            shape((8, HID)),
        ),
        in_specs=[fcol(ROWS), full(8, HID), frow, frow, scol(256), scol(256), scol(1), full(ROWS, 8)],
        out_specs=(fcol(ROWS), full(ROWS, 256), full(ROWS, 256), scol(ROWS), scol(ROWS), scol(8)),
        scratch_shapes=[pltpu.VMEM((ROWS, 256), F32)] * 2,
        compiler_params=params(),
        name="layer_mid",
    )(h, tot, w1a, w1b, w2a, w2b, b2, rowm)


def head_kernel(
    h1, tot1, h2, tot2, wp, bp, wo, bo, rowm, summed, dpre, dsum, go, gb, st, loss, lg, acc, run, run2
):
    acc[...] = jnp.zeros_like(acc)

    @pl.loop(0, NT)
    def _(j):
        cols = at(j, TILE)
        for s, (a, b) in enumerate(SEGS):
            mean1, scale1 = norm_rows(tot1, s, cols)
            mean2, scale2 = norm_rows(tot2, s, cols)
            n1 = (h1[a:b, cols] - mean1) * scale1
            n2 = (h2[a:b, cols] - mean2) * scale2
            summed[a:b, cols] = (n2 + bypass_scale * n1).astype(BF)
        acc[...] += dot(summed[:, cols], wp[cols, :])

    pre = (acc[...] + bp[...]).astype(BF)
    run[...] = jnp.full_like(run, -jnp.inf)

    @pl.loop(0, NW)
    def _(j):
        v = dot(pre, wo[:, at(j, WIDE)]) + bo[:, at(j, WIDE)]
        lg[j] = v
        m = run[...]
        for q in range(WIDE // 128):
            m = jnp.maximum(m, v[:, 128 * q : 128 * q + 128])
        run[...] = m

    top = jnp.max(run[...], axis=1, keepdims=True)
    lane = lax.broadcasted_iota(jnp.int32, (ROWS, 128), 1)
    where = rowm[:, 3:4].astype(jnp.int32) - lane
    weight = rowm[:, 1:2]
    run[...] = jnp.zeros_like(run)
    run2[...] = jnp.zeros_like(run2)

    @pl.loop(0, NW)
    def _(j):
        total = run[...]
        picked = run2[...]
        for q in range(WIDE // 128):
            v = lg[j, :, 128 * q : 128 * q + 128]
            e = jnp.exp(v - top)
            lg[j, :, 128 * q : 128 * q + 128] = e
            total = total + e
            picked = picked + jnp.where(where == j * WIDE + 128 * q, v, 0.0)
        run[...] = total
        run2[...] = picked

    total = jnp.sum(run[...], axis=1, keepdims=True)
    picked = jnp.sum(run2[...], axis=1, keepdims=True)
    lse = jnp.log(total) + top
    loss[...] = jnp.zeros((8, 128), F32) + jnp.sum(weight * (lse - picked), axis=0, keepdims=True)
    ratio = weight / total
    acc[...] = jnp.zeros_like(acc)
    pre_t = pre.astype(F32).T.astype(BF)
    ones = jnp.ones((16, ROWS), BF)

    @pl.loop(0, NW)
    def _(j):
        parts = []
        for q in range(WIDE // 128):
            e = lg[j, :, 128 * q : 128 * q + 128]
            parts.append((e * ratio - jnp.where(where == j * WIDE + 128 * q, weight, 0.0)).astype(BF))
        d = jnp.concatenate(parts, axis=1)
        acc[...] += dot_nt(d, wo[:, at(j, WIDE)])
        go[:, at(j, WIDE)] = dot(pre_t, d).astype(BF)
        gb[:, at(j, WIDE)] = dot(ones, d)[0:8]

    dp = acc[...].astype(BF)
    dpre[...] = dp

    @pl.loop(0, NT)
    def _(j):
        cols = at(j, TILE)
        ds = dot_nt(dp, wp[cols, :])
        dsum[:, cols] = ds
        for s, (a, b) in enumerate(SEGS):
            mean2, scale2 = norm_rows(tot2, s, cols)
            n2 = (h2[a:b, cols] - mean2) * scale2
            st[s : s + 1, cols] = jnp.sum(ds[a:b], axis=0, keepdims=True)
            st[3 + s : 4 + s, cols] = jnp.sum(ds[a:b] * n2, axis=0, keepdims=True)

    st[6:8, :] = jnp.zeros((2, HID), F32)


def head(h1, tot1, h2, tot2, wp, bp, wo, bo, rowm):
    return pl.pallas_call(
        head_kernel,
        out_shape=(
            shape((ROWS, HID), BF),
            shape((ROWS, PRE), BF),
            shape((ROWS, HID)),
            shape((PRE, SENP), BF),
            shape((8, SENP)),
            shape((8, HID)),
            shape((8, 128)),
        ),
        in_specs=[VM] * 9,
        out_specs=(VM,) * 7,
        scratch_shapes=[
            pltpu.VMEM((NW, ROWS, WIDE), F32),
            pltpu.VMEM((ROWS, PRE), F32),
            pltpu.VMEM((ROWS, 128), F32),
            pltpu.VMEM((ROWS, 128), F32),
        ],
        compiler_params=params(62),
        name="head",
    )(h1, tot1, h2, tot2, wp, bp, wo, bo, rowm)


def back_mid_kernel(
    h1, tot1, h2, gp2, tot2, dsum, tot3, w1a, w1b, w2a, w2b, rowm, dact, dfac, dfnext, dn, st, ua, ub
):
    i = pl.program_id(0)
    valid = rowm[:, 2:3]

    @pl.when(i < NT)
    def _():
        cols = at(i, TILE)
        for s, (a, b) in enumerate(SEGS):
            mean, scale = norm_rows(tot2, s, cols)
            along = tot3[s : s + 1, cols]
            cross = tot3[3 + s : 4 + s, cols]
            part = rowm[a:b, 0:1] / tot1[6:7, s : s + 1]
            n2 = (h2[a:b, :] - mean) * scale
            back = scale * (dsum[a:b, :] - part * (along + cross * n2))
            dact[a:b, :] = (gp2[a:b, :] * back).astype(BF)
        pa = dot_nt(dact[...], w2a[...])
        pb = dot_nt(dact[...], w2b[...])

        @pl.when(i == 0)
        def _():
            ua[...] = pa
            ub[...] = pb

        @pl.when(i > 0)
        def _():
            ua[...] += pa
            ub[...] += pb

        @pl.when(i == NT - 1)
        def _():
            f = ((ua[...] + pltpu.roll(ub[...], 1, 0)) * valid).astype(BF)
            dfac[...] = f
            dfnext[...] = (pltpu.roll(f.astype(F32), ROWS - 1, 0) * valid).astype(BF)

    @pl.when(i >= NT)
    def _():
        cols = at(i - NT, TILE)
        grad = bypass_scale * dsum[...] + dot_nt(dfac[...], w1b[...]) + dot_nt(dfnext[...], w1a[...])
        dn[...] = grad
        for s, (a, b) in enumerate(SEGS):
            mean, scale = norm_rows(tot1, s, cols)
            n1 = (h1[a:b, :] - mean) * scale
            st[s : s + 1, :] = jnp.sum(grad[a:b], axis=0, keepdims=True)
            st[3 + s : 4 + s, :] = jnp.sum(grad[a:b] * n1, axis=0, keepdims=True)
        st[6:8, :] = jnp.zeros((2, TILE), F32)


def back_mid(h1, tot1, h2, gp2, tot2, dsum, tot3, w1a, w1b, w2a, w2b, rowm):
    first = lambda i: jnp.minimum(i, NT - 1)
    second = lambda i: jnp.maximum(i - NT, 0)
    fcol = lambda rows: pl.BlockSpec((rows, TILE), lambda i: (0, first(i)))
    scol = lambda rows: pl.BlockSpec((rows, TILE), lambda i: (0, second(i)))
    both = pl.BlockSpec((ROWS, TILE), lambda i: (0, lax.rem(i, NT)))
    srow = pl.BlockSpec((TILE, 256), lambda i: (second(i), 0))
    full = lambda r, c: pl.BlockSpec((r, c), lambda i: (0, 0))
    return pl.pallas_call(
        back_mid_kernel,
        grid=(2 * NT,),
        out_shape=(
            shape((ROWS, HID), BF),
            shape((ROWS, 256), BF),
            shape((ROWS, 256), BF),
            shape((ROWS, HID)),
            shape((8, HID)),
        ),
        in_specs=[
            scol(ROWS),
            full(8, HID),
            fcol(ROWS),
            fcol(ROWS),
            full(8, HID),
            both,
            full(8, HID),
            srow,
            srow,
            fcol(256),
            fcol(256),
            full(ROWS, 8),
        ],
        out_specs=(fcol(ROWS), full(ROWS, 256), full(ROWS, 256), scol(ROWS), scol(8)),
        scratch_shapes=[pltpu.VMEM((ROWS, 256), F32)] * 2,
        compiler_params=params(),
        name="back_mid",
    )(h1, tot1, h2, gp2, tot2, dsum, tot3, w1a, w1b, w2a, w2b, rowm)


def side_kernel(summed, dpre, fac, fnext, dact, rounded, dfac, dfnext, g1a, g1b, g2a, g2b, gp, gbp, gbs):
    fac_t = fac[...].astype(F32).T.astype(BF)
    next_t = fnext[...].astype(F32).T.astype(BF)
    ones = jnp.ones((16, ROWS), BF)
    gbp[...] = dot(ones, dpre[...])[0:8]

    @pl.loop(0, NT)
    def _(j):
        cols = at(j, TILE)
        t = summed[:, cols].astype(F32).T.astype(BF)
        gp[cols, :] = dot(t, dpre[...])
        t = rounded[:, cols].astype(F32).T.astype(BF)
        g1a[cols, :] = dot(t, dfnext[...])
        g1b[cols, :] = dot(t, dfac[...])
        g2a[:, cols] = dot(fac_t, dact[:, cols])
        g2b[:, cols] = dot(next_t, dact[:, cols])
        gbs[:, cols] = dot(ones, dact[:, cols])[0:8]


def side(*args):
    return pl.pallas_call(
        side_kernel,
        out_shape=(
            shape((HID, 256)),
            shape((HID, 256)),
            shape((256, HID)),
            shape((256, HID)),
            shape((HID, PRE)),
            shape((8, PRE)),
            shape((8, HID)),
        ),
        in_specs=[VM] * 8,
        out_specs=(VM,) * 7,
        compiler_params=params(),
        name="side",
    )(*args)


def back_in_kernel(h1, gp, tot1, dn, tot4, spl_t, rowm, gin):
    i = pl.program_id(0)
    cols = at(i, TILE)
    parts = []
    for s, (a, b) in enumerate(SEGS):
        mean, scale = norm_rows(tot1, s, cols)
        along = tot4[s : s + 1, cols]
        cross = tot4[3 + s : 4 + s, cols]
        part = rowm[a:b, 0:1] / tot1[6:7, s : s + 1]
        n1 = (h1[a:b, :] - mean) * scale
        back = scale * (dn[a:b, :] - part * (along + cross * n1))
        parts.append((gp[a:b, :] * back).astype(BF))
    gin[...] = dot(spl_t[...], jnp.concatenate(parts, axis=0))


def back_in(h1, gp, tot1, dn, tot4, spl_t, rowm):
    col = lambda rows: pl.BlockSpec((rows, TILE), lambda i: (0, i))
    full = lambda r, c: pl.BlockSpec((r, c), lambda i: (0, 0))
    return pl.pallas_call(
        back_in_kernel,
        grid=(NT,),
        out_shape=shape((256, HID)),
        in_specs=[col(ROWS), col(ROWS), full(8, HID), col(ROWS), full(8, HID), full(256, ROWS), full(ROWS, 8)],
        out_specs=col(256),
        compiler_params=params(),
        name="back_in",
    )(h1, gp, tot1, dn, tot4, spl_t, rowm)


def move(x, n, mask):
    return lax.ppermute(x, "dp", [(i, i ^ mask) for i in range(n)])


def turn(x, n, layers):
    return lax.ppermute(x, "dp", [(i, (i + 8 * layers) % n) for i in range(n)])


def total(x, n):
    bit = 1
    while bit < n:
        if bit > 1 and 2 * bit < n:
            a, b, c = move(x, n, bit), move(x, n, 2 * bit), move(x, n, 3 * bit)
            x = (x + a) + (b + c)
            bit = 4 * bit
        else:
            x = x + move(x, n, bit)
            bit = 2 * bit
    return x


def fits(n, shard):
    return n == 32 and 2 * shard == CHIP * 128


def gather_blocks(shard, n, me):
    size = shard.shape[0]
    if fits(n, size):
        own = lax.dynamic_update_slice(jnp.zeros((BLK * 128,), BF), shard, (64 * me[3],)).reshape(BLK, 128)
        near, far = [], []
        for layer in LAYERS:
            v = own if layer == 0 else turn(own, n, layer)
            vx, vy = move(v, n, 2), move(v, n, 4)
            half = BLK // 2
            vxy = jnp.concatenate([move(vx[:half], n, 4), move(vy[half:], n, 2)], axis=0)
            stack = jnp.stack([v, vx, vy, vxy])
            near.append(stack)
            far.append(move(stack, n, 1))
        return near + far
    flat = lax.all_gather(shard, "dp", axis=0, tiled=True).reshape(16, CHIP, 128)
    lane = jnp.arange(128)[None, None, :]
    row = jnp.arange(795)[None, :, None]
    even = jnp.where((row == 794) & (lane >= 64), 0, flat[:, :795])
    odd = jnp.where((row == 0) & (lane < 64), 0, flat[:, 794:])
    blocks = jnp.pad(jnp.stack([even, odd], axis=1), ((0, 0), (0, 0), (0, BLK - 795), (0, 0)))
    blocks = blocks.reshape(4, 4, 2, BLK, 128)
    return [blocks[(4 - layer) % 4, :, c] for c in (0, 1) for layer in LAYERS]


def scatter_sum(keep, send, n, me, size):
    if fits(n, size):
        half = BLK // 2
        v = keep + move(send, n, 1)
        a, b = v[:, :, :half], v[:, :, half:]
        a = a[:, 0::2] + move(a[:, 1::2], n, 2)
        b = b[:, :2] + move(b[:, 2:], n, 4)
        a = a[:, 0] + move(a[:, 1], n, 4)
        b = b[:, 0] + move(b[:, 1], n, 2)
        v = jnp.concatenate([a, b], axis=1)
        out = v[0].astype(F32)
        for r in (1, 2, 3):
            out = out + turn(v[r], n, r).astype(F32)
        return lax.dynamic_slice(out.reshape(-1), (64 * me[3],), (size,))
    even = keep.reshape(16, BLK, 128)[:, :794]
    odd = send.reshape(16, BLK, 128)[:, :795]
    flat = jnp.concatenate([even, odd], axis=1).reshape(n, size)
    return lax.psum_scatter(flat.astype(F32), "dp", scatter_dimension=0, tiled=True).reshape(-1)


def adam(value, grad, first, second, decay):
    first = beta_one * first + (1.0 - beta_one) * grad
    second = beta_two * second + (1.0 - beta_two) * grad * grad
    first_hat = first / (1.0 - beta_one**STEP)
    second_hat = second / (1.0 - beta_two**STEP)
    value = value - learn_rate * (first_hat / (jnp.sqrt(second_hat) + adam_eps) + decay * value)
    return (value, first, second)


def pad_rows(v):
    parts = []
    at_row = 0
    for k, length in enumerate(SPAN):
        parts.append(v[at_row : at_row + length])
        end = START[k + 1] if k + 1 < len(START) else ROWS
        parts.append(jnp.zeros((end - START[k] - length,) + v.shape[1:], v.dtype))
        at_row = at_row + length
    return jnp.concatenate(parts, axis=0)


def on_device(
    features,
    ivectors,
    frame_mask,
    labels,
    confidence,
    weights,
    first_moment,
    second_moment,
    biases,
    bias_first,
    bias_second,
):
    n = lax.axis_size("dp")
    size = weights.shape[1]
    index = lax.axis_index("dp")
    if fits(n, size):
        me = jnp.stack([index // 8, (index // 4) % 2, (index // 2) % 2, index % 2]).astype(jnp.int32)
    else:
        me = jnp.zeros((4,), jnp.int32)
    arrs = gather_blocks(weights.astype(BF).reshape(-1), n, me)
    w_in, w1a, w1b, w2a, w2b, w_pre, w_out = unpack(me, arrs)
    b_in = biases[None, :HID]
    b_second = biases[None, HID : 2 * HID]
    b_pre = biases[None, 2 * HID : 2 * HID + PRE]
    b_out = jnp.pad(biases[None, 2 * HID + PRE :], ((0, 0), (0, SENP - SEN)), constant_values=-1e30)

    mask = frame_mask.astype(F32)
    weight = confidence * mask
    meta = jnp.stack([mask, weight, jnp.ones_like(mask), labels.astype(F32)] + [jnp.zeros_like(mask)] * 4, axis=1)
    rowm = pad_rows(meta)
    valid = rowm[:, 2:3].astype(BF)
    feats = pad_rows(features)
    gap = jnp.zeros((1, FEAT), BF)
    before = jnp.concatenate([gap, feats[:-1]], axis=0)
    after = jnp.concatenate([feats[1:], gap], axis=0)
    wide = pad_rows(jnp.concatenate([jnp.broadcast_to(ivectors[k : k + 1], (SPAN[k], IVEC)) for k in range(4)], axis=0))
    spliced = jnp.concatenate(
        [before, feats, after, wide, valid, jnp.zeros((ROWS, 256 - 3 * FEAT - IVEC - 1), BF)], axis=1
    )
    spl_t = spliced.T

    h1, gp1, st = layer_in(spliced, w_in, b_in, rowm)
    tot1 = total(st, n)
    rounded, fac, fnext, h2, gp2, st = layer_mid(h1, tot1, w1a, w1b, w2a, w2b, b_second, rowm)
    tot2 = total(st, n)
    summed, dpre, dsum, go, gbo, st, loss = head(h1, tot1, h2, tot2, w_pre, b_pre, w_out, b_out, rowm)
    tot3 = total(st, n)
    dact, dfac, dfnext, dn, st = back_mid(h1, tot1, h2, gp2, tot2, dsum, tot3, w1a, w1b, w2a, w2b, rowm)
    tot4 = total(st, n)
    g1a, g1b, g2a, g2b, gpre, gbp, gbs = side(summed, dpre, fac, fnext, dact, rounded, dfac, dfnext)
    gin = back_in(h1, gp1, tot1, dn, tot4, spl_t, rowm)
    keep, send = pack(me, gin, g1a, g1b, g2a, g2b, gpre, go)
    grad = scatter_sum(keep, send, n, me, size)

    bias_grad = jnp.concatenate([gin[220], gbs[0], gbp[0], gbo[0, :SEN]])
    extra = jnp.stack([jnp.sum(grad * grad), loss[0, 0], jnp.sum(weight)])
    last = total(jnp.concatenate([bias_grad, jnp.pad(extra, (0, 7 * 128 - 3))]).reshape(80, 128), n).reshape(-1)
    bias_sum = last[:NBIAS]
    squares, loss_sum, loss_weight = last[NBIAS], last[NBIAS + 1], last[NBIAS + 2]
    grad_norm = jnp.sqrt(squares + jnp.sum(bias_sum * bias_sum))
    scale = jnp.minimum(jnp.float32(1.0), clip_norm / grad_norm)
    new_w, new_m, new_v = adam(weights, (grad * scale)[None], first_moment, second_moment, decay_rate)
    new_b, new_bm, new_bv = adam(biases, bias_sum * scale, bias_first, bias_second, 0.0)
    return (new_w, new_m, new_v, new_b, new_bm, new_bv, loss_sum, loss_weight, grad_norm)


def solution(mesh):
    return jax.shard_map(
        on_device,
        mesh=mesh,
        in_specs=(
            P("dp", None),
            P("dp", None),
            P("dp"),
            P("dp"),
            P("dp"),
            P("dp", None),
            P("dp", None),
            P("dp", None),
            P(),
            P(),
            P(),
        ),
        out_specs=(P("dp", None), P("dp", None), P("dp", None), P(), P(), P(), P(), P(), P()),
        check_vma=False,
    )
```

```python
import math

import jax
import jax.numpy as jnp
from jax import lax
from jax.experimental import pallas as pl
from jax.experimental.pallas import tpu as pltpu
from jax.sharding import PartitionSpec as P

FEAT = 40
IVEC = 100
HID = 1536
BOT = 160
PRE = 256
SEN = 6016
SPAN = (140, 140, 150, 300)
START = (0, 144, 288, 448)
ROWS = 768
SEGS = ((0, 288), (288, 448), (448, 768))
SENP = 6144
STEP = 10
NBIAS = 9344

bypass_scale = 0.66
norm_eps = 0.001
learn_rate = 0.05
beta_one = 0.9
beta_two = 0.999
adam_eps = 1e-08
decay_rate = 0.01
clip_norm = 1.0

F32 = jnp.float32
BF = jnp.bfloat16
VM = pl.BlockSpec(memory_space=pltpu.VMEM)
SM = pl.BlockSpec(memory_space=pltpu.SMEM)
HB = pl.BlockSpec(memory_space=pltpu.HBM)

CHIP = 1589
BLK = 800
LAYERS = (0, 1, 3, 2)
OFF = (0, 2640, 6480, 10320, 13392)
ROWS_ALL = 16 * CHIP
TILE = 256
NT = HID // TILE
WIDE = 512
NW = SENP // WIDE
FLAT = ROWS_ALL + 64
FROM = 2376
HALF = BLK // 2
BIG = 512
NB = HID // BIG
GELU_C = math.sqrt(2.0 / math.pi)


def shape(dims, kind=F32):
    return jax.ShapeDtypeStruct(dims, kind)


def params(mb):
    return pltpu.CompilerParams(vmem_limit_bytes=mb * 2**20)


def here(dims, kind=F32):
    return pltpu.VMEM(dims, kind)


def kernel_call(body, outs, ins, scratch=(), mb=12, name=None, us=1.0):
    spec = {"s": SM, "v": VM, "n": VM, "h": HB}
    call = pl.pallas_call(
        body,
        out_shape=tuple(outs),
        in_specs=[spec[k] for k in ins],
        out_specs=tuple(VM for _ in outs),
        scratch_shapes=list(scratch),
        compiler_params=params(mb),
        cost_estimate=pl.CostEstimate(flops=int(us * 1e9), bytes_accessed=int(us * 3e6), transcendentals=0),
        name=name,
    )
    return lambda *args: call(
        *(pltpu.with_memory_space_constraint(v, pltpu.VMEM) if k == "n" else v for k, v in zip(ins, args))
    )


def sems(n):
    return pltpu.SemaphoreType.DMA((n,))


def vmem(dims, kind=F32):
    return pltpu.VMEM(dims, kind)


def dot(a, b):
    return jnp.dot(a, b, preferred_element_type=F32)


def dot_nt(a, b):
    return lax.dot_general(a, b, (((1,), (1,)), ((), ())), preferred_element_type=F32)


def at(j, size):
    return pl.ds(pl.multiple_of(j * size, size), size)


def block_row(d):
    return (d >> 1) * CHIP + (d & 1) * 794


def put_block(flat, d, v, start=0):
    first = block_row(d) - start
    v = v.astype(F32)
    if d % 2:
        v = pltpu.roll(v, 64, 1)
        low = lax.broadcasted_iota(jnp.int32, v.shape, 1) < 64
        flat[first : first + 1, :] = jnp.where(low[0:1], flat[first : first + 1, :], v[0:1])
        flat[first + 1 : first + 795, :] = jnp.where(low[:794], v[0:794], v[1:795])
    else:
        flat[first : first + 795, :] = v[:795]


def fetch_blocks(copies):
    for copy in copies:
        copy.start()
    for copy in copies:
        copy.wait()


def half_copies(me, srcs, first, rows, stage, sem):
    copies = []
    for core, src in enumerate(srcs):
        for i in range(rows):
            for x in (0, 1):
                for half in (0, 1):
                    y = half ^ ((first + i) & 1)
                    j = (x ^ ((me[0] >> 1) & 1)) + 2 * (y ^ ((me[0] >> 2) & 1))
                    d = 4 * i + 2 * x + ((me[0] & 1) ^ core)
                    dst = stage.at[d, pl.ds(HALF * half, HALF)]
                    copies.append(pltpu.make_async_copy(src.at[j, i] if rows > 1 else src.at[j], dst, sem.at[len(copies)]))
    return copies


def unpack_in_kernel(me, mine, other, win, last, stage, flat, sem):
    fetch_blocks(half_copies(me, (mine, other), 0, 1, stage, sem))
    for d in range(4):
        put_block(flat, d, stage[d])
    for j in range(12):
        v = flat[pl.ds(j, 224, stride=12), :]
        v = jnp.where(lax.broadcasted_iota(jnp.int32, (224, 128), 0) < 220, v, 0.0)
        win[0:224, 128 * j : 128 * j + 128] = v.astype(BF)
    win[224:256, :] = jnp.zeros((32, HID), BF)
    last[...] = flat[OFF[1] : 2 * CHIP, :]


def unpack_in(me, mine, other):
    return kernel_call(
        unpack_in_kernel,
        [here((256, HID), BF), here((2 * CHIP - OFF[1], 128))],
        "shh",
        [vmem((4, BLK, 128), BF), vmem((2 * CHIP + 14, 128)), sems(8)],
        name="unpack_in",
        us=1.5,
    )(me, mine, other)


def unpack_mid_kernel(me, last, mine, other, w1a, w1b, w2a, w2b, rest, stage, flat, tall, tall2, sem):
    copies = half_copies(me, (mine, other), 1, 3, stage, sem)
    for copy in copies:
        copy.start()
    flat[0 : 2 * CHIP - OFF[1], :] = last[...]
    for copy in copies:
        copy.wait()
    for d in range(4, 16):
        put_block(flat, d, stage[d - 4], OFF[1])
    lane = lax.broadcasted_iota(jnp.int32, (768, 128), 1)
    a = [flat[pl.ds(q, 768, stride=5), :] for q in range(5)]

    def put(r, t0, t1):
        tall[pl.ds(r, 768, stride=4), :] = t0
        tall2[pl.ds(r, 768, stride=4), :] = jnp.where(lane < 32, t1, 0.0)

    put(0, a[0], a[1])
    for r in (1, 2, 3):
        turn = 128 - 32 * r
        low = pltpu.roll(a[r], turn, 1)
        high = pltpu.roll(a[r + 1], turn, 1)
        put(r, jnp.where(lane < turn, low, high), high)
    for out, first in ((w1a, 0), (w1b, 1536)):
        out[:, 0:128] = tall[first : first + 1536, :].astype(BF)
        out[:, 128:256] = tall2[first : first + 1536, :].astype(BF)
    for j in range(12):
        v = flat[pl.ds(OFF[2] - OFF[1] + j, 320, stride=12), :].astype(BF)
        w2a[0:160, 128 * j : 128 * j + 128] = v[:160]
        w2b[0:160, 128 * j : 128 * j + 128] = v[160:]
    w2a[160:256, :] = jnp.zeros((96, HID), BF)
    w2b[160:256, :] = jnp.zeros((96, HID), BF)
    rest[...] = flat[OFF[3] - OFF[1] : 8 * CHIP - OFF[1], :]


def unpack_mid(me, *blocks):
    return kernel_call(
        unpack_mid_kernel,
        [here((HID, 256), BF)] * 2 + [here((256, HID), BF)] * 2 + [here((8 * CHIP - OFF[3], 128))],
        "snhh",
        [
            vmem((12, BLK, 128), BF),
            vmem((8 * CHIP - OFF[1] + 8, 128)),
            vmem((3072, 128)),
            vmem((3072, 128)),
            sems(24),
        ],
        mb=14,
        name="unpack_mid",
        us=5.2,
    )(me, *blocks)


def unpack_out_kernel(me, rest, mine, other, wp, wo, stage, flat, sem):
    copies = []
    for core, src in enumerate((mine, other)):
        for i in range(2):
            for j in range(4):
                d = 8 * i + ((me[0] & 7) ^ (2 * j + core))
                copies.append(pltpu.make_async_copy(src.at[j, i], stage.at[d], sem.at[len(copies)]))
    for copy in copies:
        copy.start()
    flat[0 : 8 * CHIP - OFF[3], :] = rest[...]
    for copy in copies:
        copy.wait()
    for d in range(16, 32):
        put_block(flat, d, stage[d - 16], OFF[3])
    for j in range(2):
        wp[:, 128 * j : 128 * j + 128] = flat[pl.ds(j, 1536, stride=2), :].astype(BF)
    for j in range(47):
        wo[:, 128 * j : 128 * j + 128] = flat[pl.ds(OFF[4] - OFF[3] + j, 256, stride=47), :].astype(BF)
    wo[:, 6016:] = jnp.zeros((256, 128), BF)


def unpack_out(me, *blocks):
    return kernel_call(
        unpack_out_kernel,
        [here((HID, PRE), BF), here((PRE, SENP), BF)],
        "snhh",
        [vmem((16, BLK, 128), BF), vmem((ROWS_ALL - OFF[3] + 8, 128)), sems(16)],
        mb=14,
        name="unpack_out",
        us=5.9,
    )(me, *blocks)


def put_columns(flat, first, grad, rows, width):
    for j in range(width // 128):
        flat[pl.ds(first + j, rows, stride=width // 128), :] = grad(128 * j)


def put_first(flat, first, tall, tall2):
    lane = lax.broadcasted_iota(jnp.int32, (768, 128), 1)
    t0 = [tall[pl.ds(r, 768, stride=4), :] for r in range(4)]
    t1 = [tall2[pl.ds(r, 768, stride=4), :] for r in range(4)]
    flat[pl.ds(first, 768, stride=5), :] = t0[0]
    for q in (1, 2, 3):
        shift = 32 * (q - 1)
        tail = t1[0]
        if q > 1:
            tail = jnp.where(lane < shift, pltpu.roll(t0[q - 1], shift, 1), pltpu.roll(t1[q - 1], shift, 1))
        flat[pl.ds(first + q, 768, stride=5), :] = jnp.where(lane < 32 * q, tail, pltpu.roll(t0[q], 32 * q, 1))
    flat[pl.ds(first + 4, 768, stride=5), :] = jnp.where(
        lane < 96, pltpu.roll(t0[3], 96, 1), pltpu.roll(t1[3], 96, 1)
    )


def gelu_parts(act):
    square = act * act
    t = jnp.tanh(GELU_C * act * (1.0 + 0.044715 * square))
    cdf = 0.5 + 0.5 * t
    slope = cdf + (0.5 * act) * (1.0 - t * t) * (GELU_C + (3 * 0.044715 * GELU_C) * square)
    return act * cdf, slope


def put_sums(st, first, v):
    for s, (a, b) in enumerate(SEGS):
        st[first + s : first + s + 1, :] = jnp.sum(v[a:b], axis=0, keepdims=True)


def norm_rows(tot, s, cols):
    count = tot[6:7, s : s + 1]
    mean = tot[s : s + 1, cols] / count
    var = tot[3 + s : 4 + s, cols] / count - mean * mean
    return mean, lax.rsqrt(var + norm_eps)


def put_stats(st, cols, hidden, mask):
    masked = hidden * mask
    square = masked * hidden
    for s, (a, b) in enumerate(SEGS):
        st[s : s + 1, cols] = jnp.sum(masked[a:b], axis=0, keepdims=True)
        st[3 + s : 4 + s, cols] = jnp.sum(square[a:b], axis=0, keepdims=True)


def put_counts(st, mask):
    lane = lax.broadcasted_iota(jnp.int32, (2, HID), 1)
    counts = [jnp.sum(mask[a:b], axis=0, keepdims=True) for a, b in SEGS]
    st[6:8, :] = jnp.where(lane == 0, counts[0], jnp.where(lane == 1, counts[1], counts[2]))


def put_grads(st, cols, s, grad, normed):
    st[s : s + 1, cols] = jnp.sum(grad, axis=0, keepdims=True)
    st[3 + s : 4 + s, cols] = jnp.sum(grad * normed, axis=0, keepdims=True)


def in_kernel(spl, w, b, rowm, h, gp, st):
    mask = rowm[:, 0:1]

    @pl.loop(0, NB)
    def _(j):
        cols = at(j, BIG)
        hidden, slope = gelu_parts(dot(spl[...], w[:, cols]) + b[:, cols])
        h[:, cols] = hidden
        gp[:, cols] = slope.astype(BF)
        put_stats(st, cols, hidden, mask)

    put_counts(st, mask)


def layer_in(spliced, w_in, b_in, rowm):
    return kernel_call(
        in_kernel,
        [here((ROWS, HID)), here((ROWS, HID), BF), shape((8, HID))],
        "vnvv",
        name="layer_in",
        us=4.1,
    )(spliced, w_in, b_in, rowm)


def mid_kernel(h, tot, w1a, w1b, w2a, w2b, b2, rowm, rounded, fac, fnext, h2, gp2, st):
    valid = rowm[:, 2:3]
    mask = rowm[:, 0:1]

    @pl.loop(0, NT)
    def _(j):
        cols = at(j, TILE)
        for s, (a, b) in enumerate(SEGS):
            mean, scale = norm_rows(tot, s, cols)
            rounded[a:b, cols] = ((h[a:b, cols] - mean) * scale).astype(BF)

    ua = dot(rounded[...], w1a[...])
    ub = dot(rounded[...], w1b[...])
    f = ((ub + pltpu.roll(ua * valid, 1, 0)) * valid).astype(BF)
    fac[...] = f
    fnext[...] = (pltpu.roll(f.astype(F32), ROWS - 1, 0) * valid).astype(BF)

    @pl.loop(0, NB)
    def _(j):
        cols = at(j, BIG)
        act = dot(fac[...], w2a[:, cols]) + dot(fnext[...], w2b[:, cols]) + b2[:, cols]
        hidden, slope = gelu_parts(act)
        h2[:, cols] = hidden
        gp2[:, cols] = slope.astype(BF)
        put_stats(st, cols, hidden, mask)

    put_counts(st, mask)


def layer_mid(h, tot, w1a, w1b, w2a, w2b, b2, rowm):
    return kernel_call(
        mid_kernel,
        [
            here((ROWS, HID), BF),
            here((ROWS, 256), BF),
            here((ROWS, 256), BF),
            here((ROWS, HID)),
            here((ROWS, HID), BF),
            shape((8, HID)),
        ],
        "nvnnnnvv",
        name="layer_mid",
        us=7.4,
    )(h, tot, w1a, w1b, w2a, w2b, b2, rowm)


def head_kernel(
    h1, tot1, h2, tot2, wp, bp, wo, bo, rowm, summed, n2b, dpre, dsum, go, gb, st, loss, acc, run, run2, run3
):
    @pl.loop(0, NT)
    def _(j):
        cols = at(j, TILE)
        for s, (a, b) in enumerate(SEGS):
            mean1, scale1 = norm_rows(tot1, s, cols)
            mean2, scale2 = norm_rows(tot2, s, cols)
            n1 = (h1[a:b, cols] - mean1) * scale1
            n2 = (h2[a:b, cols] - mean2) * scale2
            summed[a:b, cols] = (n2 + bypass_scale * n1).astype(BF)
            n2b[a:b, cols] = n2.astype(BF)

    pre = (dot(summed[...], wp[...]) + bp[...]).astype(BF)
    lane = lax.broadcasted_iota(jnp.int32, (ROWS, 128), 1)
    where = rowm[:, 3:4].astype(jnp.int32) - lane
    weight = rowm[:, 1:2]
    run[...] = jnp.full_like(run, -1e30)
    run2[...] = jnp.zeros_like(run2)
    run3[...] = jnp.zeros_like(run3)

    @pl.loop(0, NW)
    def _(j):
        v = dot(pre, wo[:, at(j, WIDE)]) + bo[:, at(j, WIDE)]
        parts = [v[:, 128 * q : 128 * q + 128] for q in range(WIDE // 128)]
        old = run[...]
        m = old
        picked = run3[...]
        for q, p in enumerate(parts):
            m = jnp.maximum(m, p)
            picked = picked + jnp.where(where == j * WIDE + 128 * q, p, 0.0)
        total = run2[...] * jnp.exp(old - m)
        for p in parts:
            total = total + jnp.exp(p - m)
        run[...] = m
        run2[...] = total
        run3[...] = picked

    top = jnp.max(run[...], axis=1, keepdims=True)
    total = jnp.sum(run2[...] * jnp.exp(run[...] - top), axis=1, keepdims=True)
    picked = jnp.sum(run3[...], axis=1, keepdims=True)
    lse = jnp.log(total) + top
    loss[...] = jnp.zeros((8, 128), F32) + jnp.sum(weight * (lse - picked), axis=0, keepdims=True)
    acc[...] = jnp.zeros_like(acc)
    pre_t = pre.astype(F32).T.astype(BF)
    ones = jnp.ones((16, ROWS), BF)

    @pl.loop(0, NW)
    def _(j):
        v = dot(pre, wo[:, at(j, WIDE)]) + bo[:, at(j, WIDE)]
        parts = []
        for q in range(WIDE // 128):
            e = jnp.exp(v[:, 128 * q : 128 * q + 128] - lse)
            hit = where == j * WIDE + 128 * q
            parts.append((e * weight - jnp.where(hit, weight, 0.0)).astype(BF))
        d = jnp.concatenate(parts, axis=1)
        acc[...] += dot_nt(d, wo[:, at(j, WIDE)])
        go[:, at(j, WIDE)] = dot(pre_t, d).astype(BF)
        gb[:, at(j, WIDE)] = dot(ones, d)[0:8]

    dp = acc[...].astype(BF)
    dpre[...] = dp

    @pl.loop(0, NT)
    def _(j):
        cols = at(j, TILE)
        ds = dot_nt(dp, wp[cols, :])
        dsum[:, cols] = ds
        for s, (a, b) in enumerate(SEGS):
            put_grads(st, cols, s, ds[a:b], n2b[a:b, cols].astype(F32))

    st[6:8, :] = jnp.zeros((2, HID), F32)


def head(h1, tot1, h2, tot2, wp, bp, wo, bo, rowm):
    return kernel_call(
        head_kernel,
        [
            here((ROWS, HID), BF),
            here((ROWS, HID), BF),
            here((ROWS, PRE), BF),
            here((ROWS, HID)),
            here((PRE, SENP), BF),
            shape((8, SENP)),
            shape((8, HID)),
            shape((8, 128)),
        ],
        "nvnvnvnvv",
        [
            vmem((ROWS, PRE)),
            vmem((ROWS, 128)),
            vmem((ROWS, 128)),
            vmem((ROWS, 128)),
        ],
        name="head",
        us=26.0,
    )(h1, tot1, h2, tot2, wp, bp, wo, bo, rowm)


def back_mid_kernel(
    n1b, tot1, n2b, gp2, tot2, dsum, tot3, w1a, w1b, w2a, w2b, rowm, dact, dfac, dfnext, dn, st
):
    valid = rowm[:, 2:3]

    @pl.loop(0, NT)
    def _(j):
        cols = at(j, TILE)
        for s, (a, b) in enumerate(SEGS):
            mean, scale = norm_rows(tot2, s, cols)
            along = tot3[s : s + 1, cols]
            cross = tot3[3 + s : 4 + s, cols]
            part = rowm[a:b, 0:1] / tot1[6:7, s : s + 1]
            n2 = n2b[a:b, cols].astype(F32)
            back = scale * (dsum[a:b, cols] - part * (along + cross * n2))
            dact[a:b, cols] = (gp2[a:b, cols] * back).astype(BF)

    ua = dot_nt(dact[...], w2a[...])
    ub = dot_nt(dact[...], w2b[...])
    f = ((ua + pltpu.roll(ub, 1, 0)) * valid).astype(BF)
    dfac[...] = f
    dfnext[...] = (pltpu.roll(f.astype(F32), ROWS - 1, 0) * valid).astype(BF)

    @pl.loop(0, NT)
    def _(j):
        cols = at(j, TILE)
        grad = bypass_scale * dsum[:, cols] + dot_nt(dfac[...], w1b[cols, :]) + dot_nt(dfnext[...], w1a[cols, :])
        dn[:, cols] = grad
        for s, (a, b) in enumerate(SEGS):
            put_grads(st, cols, s, grad[a:b], n1b[a:b, cols].astype(F32))

    st[6:8, :] = jnp.zeros((2, HID), F32)


def back_mid(n1b, tot1, n2b, gp2, tot2, dsum, tot3, w1a, w1b, w2a, w2b, rowm):
    return kernel_call(
        back_mid_kernel,
        [
            here((ROWS, HID), BF),
            here((ROWS, 256), BF),
            here((ROWS, 256), BF),
            here((ROWS, HID)),
            shape((8, HID)),
        ],
        "nvnnvnvnnnnv",
        name="back_mid",
        us=5.9,
    )(n1b, tot1, n2b, gp2, tot2, dsum, tot3, w1a, w1b, w2a, w2b, rowm)


def side_out_kernel(me, summed, dpre, go, keep, send, edge, gbp, flat):
    ones = jnp.ones((16, ROWS), BF)
    gbp[...] = dot(ones, dpre[...])[0:8]
    for j in range(NT):
        t = summed[:, TILE * j : TILE * j + TILE].astype(F32).T.astype(BF)
        g = dot(t, dpre[...])
        put_columns(flat, 2 * TILE * j, lambda c: g[:, c : c + 128], TILE, PRE)
    put_columns(flat, OFF[4] - OFF[3], lambda c: go[:, c : c + 128].astype(F32), PRE, SEN)
    flat[ROWS_ALL - OFF[3] :, :] = jnp.zeros((FLAT - ROWS_ALL, 128), F32)
    edge[...] = flat[0:16, :]
    for dc, out in ((0, keep), (1, send)):
        for k in range(4):
            for j in range(4):
                d = me[0] ^ (8 * k + 2 * j + dc)

                @pl.when(d > 12)
                def _():
                    out[k, j] = flat[pl.ds(block_row(d) - OFF[3], BLK), :].astype(BF)


def side_out(me, summed, dpre, go):
    return kernel_call(
        side_out_kernel,
        [here((4, 4, BLK, 128), BF), here((4, 4, BLK, 128), BF), shape((16, 128)), shape((8, PRE))],
        "snvn",
        [vmem((FLAT - OFF[3], 128))],
        mb=14,
        name="side_out",
        us=4.0,
    )(me, summed, dpre, go)


def side_mid_kernel(
    me, edge, fac, fnext, dact, rounded, dfac, dfnext, keep_in, send_in, keep, send, gbs, flat, tall, tall2
):
    fac_t = fac[...].astype(F32).T.astype(BF)
    next_t = fnext[...].astype(F32).T.astype(BF)
    ones = jnp.ones((16, ROWS), BF)
    flat[0 : OFF[1] - FROM, :] = jnp.zeros((OFF[1] - FROM, 128), F32)
    for j in range(NT):
        cols = slice(TILE * j, TILE * j + TILE)
        t = rounded[:, cols].astype(F32).T.astype(BF)
        for k, d in enumerate((dfnext, dfac)):
            g = dot(t, d[...])
            tall[HID * k + TILE * j : HID * k + TILE * j + TILE, :] = g[:, 0:128]
            tall2[HID * k + TILE * j : HID * k + TILE * j + TILE, :] = g[:, 128:256]
        for k, f in enumerate((fac_t, next_t)):
            g = dot(f, dact[:, cols])
            for q in range(TILE // 128):
                row = OFF[2] - FROM + 1920 * k + TILE // 128 * j + q
                flat[pl.ds(row, BOT, stride=12), :] = g[0:BOT, 128 * q : 128 * q + 128]
        gbs[:, cols] = dot(ones, dact[:, cols])[0:8]
    put_first(flat, OFF[1] - FROM, tall, tall2)
    flat[OFF[3] - FROM : OFF[3] - FROM + 16, :] = edge[...]
    flat[OFF[3] - FROM + 16 :, :] = jnp.zeros((7968 - (OFF[3] - FROM + 16), 128), F32)
    for dc, src, out in ((0, keep_in, keep), (1, send_in, send)):
        for k in range(4):
            for j in range(4):
                d = me[0] ^ (8 * k + 2 * j + dc)

                @pl.when(d > 12)
                def _():
                    out[k, j] = src[k, j]

                @pl.when((d > 2) & (d < 13))
                def _():
                    out[k, j] = flat[pl.ds(block_row(d) - FROM, BLK), :].astype(BF)

                @pl.when(d < 3)
                def _():
                    out[k, j] = jnp.zeros((BLK, 128), BF)


def side_mid(me, keep, send, *args):
    return kernel_call(
        side_mid_kernel,
        [here((4, 4, BLK, 128), BF), here((4, 4, BLK, 128), BF), shape((8, HID))],
        "svnnnnnnnn",
        [vmem((7968, 128)), vmem((3072, 128)), vmem((3072, 128))],
        mb=26,
        name="side_mid",
        us=6.4,
    )(me, *args, keep, send)


def back_in_kernel(me, n1b, gp, tot1, dn, tot4, spl_t, rowm, keep, send, gb, d, flat):
    @pl.loop(0, NT)
    def _(j):
        cols = at(j, TILE)
        for s, (a, b) in enumerate(SEGS):
            mean, scale = norm_rows(tot1, s, cols)
            along = tot4[s : s + 1, cols]
            cross = tot4[3 + s : 4 + s, cols]
            part = rowm[a:b, 0:1] / tot1[6:7, s : s + 1]
            n1 = n1b[a:b, cols].astype(F32)
            back = scale * (dn[a:b, cols] - part * (along + cross * n1))
            d[a:b, cols] = (gp[a:b, cols] * back).astype(BF)

    for j in range(NT):
        g = dot(spl_t[...], d[:, TILE * j : TILE * j + TILE])
        gb[:, TILE * j : TILE * j + TILE] = g[216:224]
        for q in range(TILE // 128):
            flat[pl.ds(TILE // 128 * j + q, 220, stride=12), :] = g[0:220, 128 * q : 128 * q + 128]
    flat[OFF[1] :, :] = jnp.zeros((2 * CHIP + 14 - OFF[1], 128), F32)
    for dc, out in ((0, keep), (1, send)):
        for dx in (0, 1):
            t = (me[0] & 3) ^ (2 * dx + dc)
            out[dx] = flat[pl.ds(block_row(t), BLK), :].astype(BF)


def back_in(me, n1b, gp, tot1, dn, tot4, spl_t, rowm):
    return kernel_call(
        back_in_kernel,
        [shape((2, BLK, 128), BF), shape((2, BLK, 128), BF), shape((8, HID))],
        "snnvnvvv",
        [vmem((ROWS, HID), BF), vmem((2 * CHIP + 14, 128))],
        name="back_in",
        us=2.8,
    )(me, n1b, gp, tot1, dn, tot4, spl_t, rowm)


def move(x, n, mask, to=None):
    return lax.ppermute(x, "dp", [(i, i ^ mask) for i in range(n) if to is None or to(i ^ mask)])


def exchange(x, n, masks):
    a, b, c = (move(x, n, k) for k in masks)
    return (x + a) + (b + c)


def sum_core(x, n):
    return x + move(x, n, 1)


def sum_layers(x, n):
    return exchange(x, n, (8, 16, 24))


def sum_plane(x, n):
    return exchange(x, n, (2, 4, 6))


def total(x, n):
    if n == 32:
        return sum_plane(sum_layers(sum_core(x, n), n), n)
    bit = 1
    while bit < n:
        x = x + move(x, n, bit)
        bit = 2 * bit
    return x


def fits(n, shard):
    return n == 32 and 2 * shard == CHIP * 128


def spread_plane(v, n):
    return v, move(v, n, 2), move(v, n, 4), move(v, n, 6)


def with_sibling(parts, n):
    stack = jnp.stack(parts)
    return stack, move(stack, n, 1)


def once(v, *earlier):
    return lax.optimization_barrier((v,) + earlier)[0]


def to_layers(v, n, me, layer):
    out = v
    for k in (1, 2, 3):
        out = jnp.where((me >> 3) == (layer ^ k), move(v, n, 8 * k, lambda t: (t >> 3) == (layer ^ k)), out)
    return out


def gather_low(own, n, me):
    moved = move(own[HALF:], n, 4)
    mine = own[:HALF]
    row = (me >> 2) & 1
    first = jnp.where(row == 0, mine, moved)
    second = jnp.where(row == 1, mine, moved)
    parts = spread_plane(to_layers(first, n, me, 0), n)
    moved = {k: move(own, n, 8 * k, lambda t: ((t >> 3) ^ k) >= 2) for k in (1, 2, 3)}
    pair, moved[1], moved[3], _ = lax.optimization_barrier((jnp.stack([first, second]), moved[1], moved[3], parts[1]))
    return with_sibling(parts, n), pair, moved


def gather_mid(pair, n, me):
    one = to_layers(pair[1], n, me, 0)
    two = to_layers(pair, n, me, 1)
    return jnp.concatenate([one[None], two])


def pick_high(own, moved, me):
    out = []
    z = me >> 3
    for layer in (2, 3):
        v = own
        for k in (1, 2, 3):
            v = jnp.where(z == (layer ^ k), moved[k], v)
        out.append(v)
    return jnp.stack(out)


def gather_all(shard, n):
    flat = lax.all_gather(shard, "dp", axis=0, tiled=True).reshape(32, -1)
    blocks = jnp.pad(flat, ((0, 0), (0, BLK * 128 - flat.shape[1]))).reshape(8, 2, 2, BLK, 128)

    def split(rows):
        parts = [v.reshape(2, 2, 2, HALF, 128).transpose(1, 2, 0, 3, 4) for v in blocks[rows]]
        parts = [v[:, ::-1] if r % 2 else v for r, v in zip(range(8)[rows], parts)]
        return jnp.stack(parts, axis=3).reshape(2, 4, -1, HALF, 128)

    low, mid = split(slice(0, 1)), split(slice(1, 4))
    high = blocks[4:].reshape(2, 4, 2, BLK, 128).transpose(2, 1, 0, 3, 4)
    return (low[0][:, 0], low[1][:, 0]), (mid[0], mid[1]), (high[0], high[1])


def plane_one(v, n):
    a, b = v[:, :, :HALF], v[:, :, HALF:]
    a = a[:, 0::2] + move(a[:, 1::2], n, 2)
    b = b[:, :2] + move(b[:, 2:], n, 4)
    return a, b


def first_one(v, n, me):
    a = v[0, :HALF] + move(v[1, :HALF], n, 2)
    b = v[:, HALF:] + move(v[:, HALF:], n, 4, lambda t: (t & 4) == 0)
    here = (jnp.arange(4) == (me >> 3))[:, None, None, None]
    a = jnp.where(here & (jnp.arange(2) == ((me >> 2) & 1))[None, :, None, None], a[None, None], 0)
    b = jnp.where(here & ((me & 4) == 0), b[None], 0)
    return a, b


def plane_two(a, b, n):
    a = a[:, 0] + move(a[:, 1], n, 4)
    b = b[:, 0] + move(b[:, 1], n, 2)
    return jnp.concatenate([a, b], axis=1)


def layers(v, n):
    out = v[0].astype(F32)
    for k in (1, 2, 3):
        out = out + move(v[k], n, 8 * k).astype(F32)
    return out


def to_rows(even, odd):
    return jnp.concatenate([even[:, :794], odd[:, :795]], axis=1).reshape(-1, 128)


def adam(value, grad, first, second, decay):
    first = beta_one * first + (1.0 - beta_one) * grad
    second = beta_two * second + (1.0 - beta_two) * grad * grad
    first_hat = first / (1.0 - beta_one**STEP)
    second_hat = second / (1.0 - beta_two**STEP)
    value = value - learn_rate * (first_hat / (jnp.sqrt(second_hat) + adam_eps) + decay * value)
    return (value, first, second)


def pad_rows(v):
    parts = []
    at_row = 0
    for k, length in enumerate(SPAN):
        parts.append(v[at_row : at_row + length])
        end = START[k + 1] if k + 1 < len(START) else ROWS
        parts.append(jnp.zeros((end - START[k] - length,) + v.shape[1:], v.dtype))
        at_row = at_row + length
    return jnp.concatenate(parts, axis=0)


def on_device(
    features,
    ivectors,
    frame_mask,
    labels,
    confidence,
    weights,
    first_moment,
    second_moment,
    biases,
    bias_first,
    bias_second,
):
    n = lax.axis_size("dp")
    size = weights.shape[1]
    index = lax.axis_index("dp")
    fast = fits(n, size)
    me = index if fast else jnp.int32(0)
    place = me.reshape(1)
    shard = weights.astype(BF).reshape(-1)
    if fast:
        own = jnp.pad(shard, (0, BLK * 128 - size)).reshape(BLK, 128)
        low, pair, moved = gather_low(own, n, me)
        mid = gather_mid(pair, n, me)
    else:
        low, mid, high = gather_all(shard, n)
    b_in = biases[None, :HID]
    b_second = biases[None, HID : 2 * HID]
    b_pre = biases[None, 2 * HID : 2 * HID + PRE]
    b_out = jnp.pad(biases[None, 2 * HID + PRE :], ((0, 0), (0, SENP - SEN)), constant_values=-1e30)

    mask = frame_mask.astype(F32)
    weight = confidence * mask
    meta = jnp.stack([mask, weight, jnp.ones_like(mask), labels.astype(F32)] + [jnp.zeros_like(mask)] * 4, axis=1)
    rowm = pad_rows(meta)
    valid = rowm[:, 2:3].astype(BF)
    feats = pad_rows(features)
    gap = jnp.zeros((1, FEAT), BF)
    before = jnp.concatenate([gap, feats[:-1]], axis=0)
    after = jnp.concatenate([feats[1:], gap], axis=0)
    wide = pad_rows(jnp.concatenate([jnp.broadcast_to(ivectors[k : k + 1], (SPAN[k], IVEC)) for k in range(4)], axis=0))
    spliced = jnp.concatenate(
        [before, feats, after, wide, valid, jnp.zeros((ROWS, 256 - 3 * FEAT - IVEC - 1), BF)], axis=1
    )
    spl_t = spliced.T

    w_in, last = unpack_in(place, *low)
    h1, gp1, st = layer_in(spliced, w_in, b_in, rowm)
    if fast:
        mid, moved[2], _ = lax.optimization_barrier((mid, moved[2], st))
        mid = spread_plane(mid, n)
        high = pick_high(own, moved, me)
        tot1 = sum_layers(sum_core(st, n), n)
        mid, tot1 = lax.optimization_barrier((mid, tot1))
        mid = with_sibling(mid, n)
        tot1 = sum_plane(tot1, n)
        high, tot1 = lax.optimization_barrier((high, tot1))
        high = spread_plane(high, n)
    else:
        tot1 = total(st, n)
    w1a, w1b, w2a, w2b, rest = unpack_mid(place, last, *mid)
    rounded, fac, fnext, h2, gp2, st = layer_mid(h1, tot1, w1a, w1b, w2a, w2b, b_second, rowm)
    if fast:
        st = sum_core(st, n)
        high, st = lax.optimization_barrier((high, st))
        high = with_sibling(high, n)
        tot2 = sum_plane(sum_layers(st, n), n)
    else:
        tot2 = total(st, n)
    w_pre, w_out = unpack_out(place, rest, *high)
    summed, n2b, dpre, dsum, go, gbo, st, loss = head(h1, tot1, h2, tot2, w_pre, b_pre, w_out, b_out, rowm)
    tot3 = sum_layers(sum_core(st, n), n) if fast else total(st, n)
    keep, send, edge, gbp = side_out(place, *once((summed, dpre, go), tot3))
    if fast:
        tot3 = sum_plane(tot3, n)
        tot3, keep = lax.optimization_barrier((tot3, keep))
    dact, dfac, dfnext, dn, st = back_mid(rounded, tot1, n2b, gp2, tot2, dsum, tot3, w1a, w1b, w2a, w2b, rowm)
    parts = (edge, fac, fnext, dact, rounded, dfac, dfnext)
    if fast:
        tot4 = sum_core(st, n)
        keep, send, gbs = side_mid(place, keep, send, *once(parts, tot4))
        tot4 = sum_plane(tot4, n)
        keep, send, tot4 = lax.optimization_barrier((keep, send, tot4))
        blocks = keep + move(send, n, 1)
        tot4 = sum_layers(tot4, n)
        a, b = plane_one(blocks, n)
    else:
        tot4 = total(st, n)
        keep, send, gbs = side_mid(place, keep, send, *parts)
    keep_in, send_in, gbi = back_in(place, rounded, gp1, tot1, dn, tot4, spl_t, rowm)
    if fast:
        first = keep_in + move(send_in, n, 1)
        a, b, first = lax.optimization_barrier((a, b, first))
        first_a, first_b = first_one(first, n, me)
        grad = layers(plane_two(a + first_a, b + first_b, n), n)
        grad = lax.dynamic_slice(grad.reshape(-1), (64 * (me & 1),), (size,))
    else:
        rows = to_rows(keep.reshape(16, BLK, 128), send.reshape(16, BLK, 128))
        head_rows = to_rows(keep_in, send_in)
        rows = jnp.concatenate([rows[: 2 * CHIP] + head_rows, rows[2 * CHIP :]], axis=0)
        grad = lax.psum_scatter(rows.astype(F32).reshape(n, size), "dp", scatter_dimension=0, tiled=True).reshape(-1)
    square = jnp.sum(grad * grad)
    bias_grad = jnp.concatenate([gbi[4], gbs[0], gbp[0], gbo[0, :SEN]])
    extra = jnp.stack([square, loss[0, 0], jnp.sum(weight)])
    last = total(jnp.concatenate([bias_grad, jnp.pad(extra, (0, 7 * 128 - 3))]).reshape(80, 128), n).reshape(-1)
    bias_sum = last[:NBIAS]
    squares, loss_sum, loss_weight = last[NBIAS], last[NBIAS + 1], last[NBIAS + 2]
    grad_norm = jnp.sqrt(squares + jnp.sum(bias_sum * bias_sum))
    scale = jnp.minimum(jnp.float32(1.0), clip_norm / grad_norm)
    new_w, new_m, new_v = adam(weights, (grad * scale)[None], first_moment, second_moment, decay_rate)
    new_b, new_bm, new_bv = adam(biases, bias_sum * scale, bias_first, bias_second, 0.0)
    return (new_w, new_m, new_v, new_b, new_bm, new_bv, loss_sum, loss_weight, grad_norm)


def solution(mesh):
    return jax.shard_map(
        on_device,
        mesh=mesh,
        in_specs=(
            P("dp", None),
            P("dp", None),
            P("dp"),
            P("dp"),
            P("dp"),
            P("dp", None),
            P("dp", None),
            P("dp", None),
            P(),
            P(),
            P(),
        ),
        out_specs=(P("dp", None), P("dp", None), P("dp", None), P(), P(), P(), P(), P(), P()),
        check_vma=False,
    )
```

```python
import math

import jax
import jax.numpy as jnp
from jax import lax
from jax.experimental import pallas as pl
from jax.experimental.pallas import tpu as pltpu
from jax.sharding import PartitionSpec as P

FEAT = 40
IVEC = 100
HID = 1536
BOT = 160
PRE = 256
SEN = 6016
SPAN = (140, 140, 150, 300)
START = (0, 144, 288, 448)
ROWS = 768
SEGS = ((0, 288), (288, 448), (448, 768))
SENP = 6144
STEP = 10
NBIAS = 9344

bypass_scale = 0.66
norm_eps = 0.001
learn_rate = 0.05
beta_one = 0.9
beta_two = 0.999
adam_eps = 1e-08
decay_rate = 0.01
clip_norm = 1.0

F32 = jnp.float32
BF = jnp.bfloat16
VM = pl.BlockSpec(memory_space=pltpu.VMEM)
SM = pl.BlockSpec(memory_space=pltpu.SMEM)
HB = pl.BlockSpec(memory_space=pltpu.HBM)

CHIP = 1589
BLK = 800
GROUPS = ((0, (0, 2)), (1, (0, 2)), (0, (1, 3)), (1, (1, 3)))
OFF = (0, 2640, 6480, 10320, 13392)
ROWS_ALL = 16 * CHIP
TILE = 256
NT = HID // TILE
WIDE = 1024
NW = SENP // WIDE
FLAT = ROWS_ALL + 64
FROM = 2376
HALF = BLK // 2
BIG = 512
NB = HID // BIG
GELU_C = math.sqrt(2.0 / math.pi)


def shape(dims, kind=F32):
    return jax.ShapeDtypeStruct(dims, kind)


def params(mb):
    return pltpu.CompilerParams(vmem_limit_bytes=mb * 2**20)


def here(dims, kind=F32):
    return pltpu.VMEM(dims, kind)


def kernel_call(body, outs, ins, scratch=(), mb=12, name=None, us=1.0):
    spec = {"s": SM, "v": VM, "n": VM, "h": HB}
    call = pl.pallas_call(
        body,
        out_shape=tuple(outs),
        in_specs=[spec[k] for k in ins],
        out_specs=tuple(VM for _ in outs),
        scratch_shapes=list(scratch),
        compiler_params=params(mb),
        cost_estimate=pl.CostEstimate(flops=int(us * 1e9), bytes_accessed=int(us * 3e6), transcendentals=0),
        name=name,
    )
    return lambda *args: call(
        *(pltpu.with_memory_space_constraint(v, pltpu.VMEM) if k == "n" else v for k, v in zip(ins, args))
    )


def sems(n):
    return pltpu.SemaphoreType.DMA((n,))


def vmem(dims, kind=F32):
    return pltpu.VMEM(dims, kind)


def dot(a, b):
    return jnp.dot(a, b, preferred_element_type=F32)


def dot_nt(a, b):
    return lax.dot_general(a, b, (((1,), (1,)), ((), ())), preferred_element_type=F32)


def at(j, size):
    return pl.ds(pl.multiple_of(j * size, size), size)


def block_row(d):
    return (d >> 1) * CHIP + (d & 1) * 794


def put_block(flat, d, v, start=0):
    first = block_row(d) - start
    v = v.astype(F32)
    if d % 2:
        v = pltpu.roll(v, 64, 1)
        low = lax.broadcasted_iota(jnp.int32, v.shape, 1) < 64
        flat[first : first + 1, :] = jnp.where(low[0:1], flat[first : first + 1, :], v[0:1])
        flat[first + 1 : first + 795, :] = jnp.where(low[:794], v[0:794], v[1:795])
    else:
        flat[first : first + 795, :] = v[:795]


def fetch_blocks(me, groups, first, last, stage, sem):
    for src, (core, layers) in zip(groups, GROUPS):
        for i in range(8):
            low, high = i & 1, (i >> 1) & 1
            x, y = (low, high) if i < 4 else (high, low)
            d = me[0] ^ (8 * layers[i // 4] + 4 * y + 2 * x + core)

            @pl.when((d >= first) & (d <= last))
            def _():
                pltpu.make_async_copy(src.at[i], stage.at[d - first], sem.at[d - first]).start()


def block_ready(src, d, stage, sem):
    pltpu.make_async_copy(src.at[0], stage.at[d], sem.at[d]).wait()


def unpack_in_kernel(me, g0, g1, g2, g3, win, stage, flat, sem):
    fetch_blocks(me, (g0, g1, g2, g3), 0, 3, stage, sem)
    for d in range(4):
        block_ready(g0, d, stage, sem)
        put_block(flat, d, stage[d])
    for j in range(12):
        v = flat[pl.ds(j, 224, stride=12), :]
        v = jnp.where(lax.broadcasted_iota(jnp.int32, (224, 128), 0) < 220, v, 0.0)
        win[0:224, 128 * j : 128 * j + 128] = v.astype(BF)
    win[224:256, :] = jnp.zeros((32, HID), BF)


def unpack_in(me, groups):
    return kernel_call(
        unpack_in_kernel,
        [here((256, HID), BF)],
        "shhhh",
        [vmem((4, BLK, 128), BF), vmem((2 * CHIP + 14, 128)), sems(4)],
        name="unpack_in",
        us=1.5,
    )(me, *groups)[0]


def unpack_mid_kernel(me, g0, g1, g2, g3, w1a, w1b, w2a, w2b, stage, flat, tall, tall2, sem):
    fetch_blocks(me, (g0, g1, g2, g3), 2, 12, stage, sem)
    start = block_row(2)
    first, second = OFF[1] - start, OFF[2] - start
    for d in range(2, 13):
        block_ready(g0, d - 2, stage, sem)
        put_block(flat, d, stage[d - 2], start)
    lane = lax.broadcasted_iota(jnp.int32, (768, 128), 1)
    a = [flat[pl.ds(first + q, 768, stride=5), :] for q in range(5)]

    def put(r, t0, t1):
        tall[pl.ds(r, 768, stride=4), :] = t0
        tall2[pl.ds(r, 768, stride=4), :] = jnp.where(lane < 32, t1, 0.0)

    put(0, a[0], a[1])
    for r in (1, 2, 3):
        turn = 128 - 32 * r
        low = pltpu.roll(a[r], turn, 1)
        high = pltpu.roll(a[r + 1], turn, 1)
        put(r, jnp.where(lane < turn, low, high), high)
    for out, row in ((w1a, 0), (w1b, 1536)):
        out[:, 0:128] = tall[row : row + 1536, :].astype(BF)
        out[:, 128:256] = tall2[row : row + 1536, :].astype(BF)
    for j in range(12):
        v = flat[pl.ds(second + j, 320, stride=12), :].astype(BF)
        w2a[0:160, 128 * j : 128 * j + 128] = v[:160]
        w2b[0:160, 128 * j : 128 * j + 128] = v[160:]
    w2a[160:256, :] = jnp.zeros((96, HID), BF)
    w2b[160:256, :] = jnp.zeros((96, HID), BF)


def unpack_mid(me, groups):
    return kernel_call(
        unpack_mid_kernel,
        [here((HID, 256), BF)] * 2 + [here((256, HID), BF)] * 2,
        "shhhh",
        [
            vmem((11, BLK, 128), BF),
            vmem((6 * CHIP, 128)),
            vmem((3072, 128)),
            vmem((3072, 128)),
            sems(11),
        ],
        mb=15,
        name="unpack_mid",
        us=5.2,
    )(me, *groups)


def flatten_out_kernel(me, g0, g1, g2, g3, flat, stage, sem):
    fetch_blocks(me, (g0, g1, g2, g3), 12, 31, stage, sem)
    for d in range(12, 32):
        block_ready(g0, d - 12, stage, sem)
        put_block(flat, d, stage[d - 12], block_row(12))


def flatten_out(me, groups):
    return kernel_call(
        flatten_out_kernel,
        [here((10 * CHIP, 128))],
        "shhhh",
        [vmem((20, BLK, 128), BF), sems(20)],
        name="flatten_out",
        us=3.0,
    )(me, *groups)[0]


def unpack_out_kernel(flat, _, wp, wo):
    pre, out = OFF[3] - block_row(12), OFF[4] - block_row(12)
    for j in range(2):
        wp[:, 128 * j : 128 * j + 128] = flat[pl.ds(pre + j, 1536, stride=2), :].astype(BF)
    for j in range(47):
        wo[:, 128 * j : 128 * j + 128] = flat[pl.ds(out + j, 256, stride=47), :].astype(BF)
    wo[:, 6016:] = jnp.zeros((256, 128), BF)


def unpack_out(flat, h2):
    return kernel_call(
        unpack_out_kernel,
        [here((HID, PRE), BF), here((PRE, SENP), BF)],
        "nn",
        name="unpack_out",
        us=3.0,
    )(flat, h2)


def put_columns(flat, first, grad, rows, width):
    for j in range(width // 128):
        flat[pl.ds(first + j, rows, stride=width // 128), :] = grad(128 * j)


def put_first(flat, first, tall, tall2):
    lane = lax.broadcasted_iota(jnp.int32, (768, 128), 1)
    t0 = [tall[pl.ds(r, 768, stride=4), :] for r in range(4)]
    t1 = [tall2[pl.ds(r, 768, stride=4), :] for r in range(4)]
    flat[pl.ds(first, 768, stride=5), :] = t0[0]
    for q in (1, 2, 3):
        shift = 32 * (q - 1)
        tail = t1[0]
        if q > 1:
            tail = jnp.where(lane < shift, pltpu.roll(t0[q - 1], shift, 1), pltpu.roll(t1[q - 1], shift, 1))
        flat[pl.ds(first + q, 768, stride=5), :] = jnp.where(lane < 32 * q, tail, pltpu.roll(t0[q], 32 * q, 1))
    flat[pl.ds(first + 4, 768, stride=5), :] = jnp.where(
        lane < 96, pltpu.roll(t0[3], 96, 1), pltpu.roll(t1[3], 96, 1)
    )


def gelu_parts(act):
    square = act * act
    t = jnp.tanh(GELU_C * act * (1.0 + 0.044715 * square))
    cdf = 0.5 + 0.5 * t
    slope = cdf + (0.5 * act) * (1.0 - t * t) * (GELU_C + (3 * 0.044715 * GELU_C) * square)
    return act * cdf, slope


def put_sums(st, first, v):
    for s, (a, b) in enumerate(SEGS):
        st[first + s : first + s + 1, :] = jnp.sum(v[a:b], axis=0, keepdims=True)


def norm_rows(tot, s, cols):
    count = tot[6:7, s : s + 1]
    mean = tot[s : s + 1, cols] / count
    var = tot[3 + s : 4 + s, cols] / count - mean * mean
    return mean, lax.rsqrt(var + norm_eps)


def put_stats(st, cols, hidden, mask):
    masked = hidden * mask
    square = masked * hidden
    for s, (a, b) in enumerate(SEGS):
        st[s : s + 1, cols] = jnp.sum(masked[a:b], axis=0, keepdims=True)
        st[3 + s : 4 + s, cols] = jnp.sum(square[a:b], axis=0, keepdims=True)


def put_counts(st, mask):
    lane = lax.broadcasted_iota(jnp.int32, (2, HID), 1)
    counts = [jnp.sum(mask[a:b], axis=0, keepdims=True) for a, b in SEGS]
    st[6:8, :] = jnp.where(lane == 0, counts[0], jnp.where(lane == 1, counts[1], counts[2]))


def put_grads(st, cols, s, grad, normed):
    st[s : s + 1, cols] = jnp.sum(grad, axis=0, keepdims=True)
    st[3 + s : 4 + s, cols] = jnp.sum(grad * normed, axis=0, keepdims=True)


def in_kernel(spl, w, b, rowm, h, gp, st):
    mask = rowm[:, 0:1]

    @pl.loop(0, NB)
    def _(j):
        cols = at(j, BIG)
        hidden, slope = gelu_parts(dot(spl[...], w[:, cols]) + b[:, cols])
        h[:, cols] = hidden
        gp[:, cols] = slope.astype(BF)
        put_stats(st, cols, hidden, mask)

    put_counts(st, mask)


def layer_in(spliced, w_in, b_in, rowm):
    return kernel_call(
        in_kernel,
        [here((ROWS, HID)), here((ROWS, HID), BF), shape((8, HID))],
        "vnvv",
        name="layer_in",
        us=4.1,
    )(spliced, w_in, b_in, rowm)


def mid_kernel(h, tot, w1a, w1b, w2a, w2b, bias, rowm, rounded, fac, fnext, h2, gp2, st):
    valid = rowm[:, 2:3]
    mask = rowm[:, 0:1]

    @pl.loop(0, NT)
    def _(j):
        cols = at(j, TILE)
        for s, (a, b) in enumerate(SEGS):
            mean, scale = norm_rows(tot, s, cols)
            rounded[a:b, cols] = ((h[a:b, cols] - mean) * scale).astype(BF)

    ua = dot(rounded[...], w1a[...])
    ub = dot(rounded[...], w1b[...])
    f = ((ub + pltpu.roll(ua * valid, 1, 0)) * valid).astype(BF)
    fac[...] = f
    fnext[...] = (pltpu.roll(f.astype(F32), ROWS - 1, 0) * valid).astype(BF)

    @pl.loop(0, NB)
    def _(j):
        cols = at(j, BIG)
        act = dot(fac[...], w2a[:, cols]) + dot(fnext[...], w2b[:, cols]) + bias[:, at(j + HID // BIG, BIG)]
        hidden, slope = gelu_parts(act)
        h2[:, cols] = hidden
        gp2[:, cols] = slope.astype(BF)
        put_stats(st, cols, hidden, mask)

    put_counts(st, mask)


def layer_mid(h, tot, w1a, w1b, w2a, w2b, bias, rowm):
    return kernel_call(
        mid_kernel,
        [
            here((ROWS, HID), BF),
            here((ROWS, 256), BF),
            here((ROWS, 256), BF),
            here((ROWS, HID)),
            here((ROWS, HID), BF),
            shape((8, HID)),
        ],
        "nvnnnnvv",
        name="layer_mid",
        us=7.4,
    )(h, tot, w1a, w1b, w2a, w2b, bias, rowm)


def head_kernel(
    h1, tot1, h2, tot2, wp, wo, bias, rowm, summed, n2b, dpre, dsum, go, gb, st, loss, acc
):
    @pl.loop(0, NT)
    def _(j):
        cols = at(j, TILE)
        for s, (a, b) in enumerate(SEGS):
            mean1, scale1 = norm_rows(tot1, s, cols)
            mean2, scale2 = norm_rows(tot2, s, cols)
            n1 = (h1[a:b, cols] - mean1) * scale1
            n2 = (h2[a:b, cols] - mean2) * scale2
            summed[a:b, cols] = (n2 + bypass_scale * n1).astype(BF)
            n2b[a:b, cols] = n2.astype(BF)

    pre = (dot(summed[...], wp[...]) + bias[:, 2 * HID : 2 * HID + PRE]).astype(BF)
    lane = lax.broadcasted_iota(jnp.int32, (ROWS, 128), 1)
    where = rowm[:, 3:4].astype(jnp.int32) - lane
    weight = rowm[:, 1:2]

    bo = jnp.concatenate([bias[:, 2 * HID + PRE :], jnp.full((1, SENP - SEN), -1e30, F32)], axis=1)

    m = jnp.full((ROWS, 128), -1e30, F32)
    total = jnp.zeros((ROWS, 128), F32)
    for j in range(NW):
        cols = slice(WIDE * j, WIDE * j + WIDE)
        v = dot(pre, wo[:, cols]) + bo[:, cols]
        parts = [v[:, 128 * q : 128 * q + 128] for q in range(WIDE // 128)]
        old = m
        for p in parts:
            m = jnp.maximum(m, p)
        total = total * jnp.exp(old - m)
        for p in parts:
            total = total + jnp.exp(p - m)

    top = jnp.max(m, axis=1, keepdims=True)
    total = jnp.sum(total * jnp.exp(m - top), axis=1, keepdims=True)
    lse = jnp.log(total) + top
    less = lse - jnp.log(weight)
    acc[...] = jnp.zeros_like(acc)
    pre_t = jnp.concatenate([pre.astype(F32).T.astype(BF), jnp.ones((16, ROWS), BF)], axis=0)
    picked = jnp.zeros((ROWS, 128), F32)
    for j in range(NW):
        cols = slice(WIDE * j, WIDE * j + WIDE)
        v = dot(pre, wo[:, cols]) + bo[:, cols]
        parts = []
        for q in range(WIDE // 128):
            p = v[:, 128 * q : 128 * q + 128]
            hit = jnp.where(where == j * WIDE + 128 * q, weight, 0.0)
            picked = picked + hit * p
            parts.append((jnp.exp(p - less) - hit).astype(BF))
        d = jnp.concatenate(parts, axis=1)
        acc[...] += dot_nt(d, wo[:, cols])
        g = dot(pre_t, d)
        go[:, cols] = g[0:PRE].astype(BF)
        gb[:, cols] = g[PRE : PRE + 8]

    entropy = jnp.sum(weight * lse, axis=0, keepdims=True)
    picked = jnp.sum(jnp.sum(picked, axis=1, keepdims=True), axis=0, keepdims=True)
    loss[...] = jnp.zeros((8, 128), F32) + (entropy - picked)
    dp = acc[...].astype(BF)
    dpre[...] = dp

    @pl.loop(0, NT)
    def _(j):
        cols = at(j, TILE)
        ds = dot_nt(dp, wp[cols, :])
        dsum[:, cols] = ds
        for s, (a, b) in enumerate(SEGS):
            put_grads(st, cols, s, ds[a:b], n2b[a:b, cols].astype(F32))

    st[6:8, :] = jnp.zeros((2, HID), F32)


def head(h1, tot1, h2, tot2, wp, wo, bias, rowm):
    return kernel_call(
        head_kernel,
        [
            here((ROWS, HID), BF),
            here((ROWS, HID), BF),
            here((ROWS, PRE), BF),
            here((ROWS, HID)),
            here((PRE, SENP), BF),
            shape((8, SENP)),
            shape((8, HID)),
            shape((8, 128)),
        ],
        "nvnvnnvv",
        [
            vmem((ROWS, PRE)),
        ],
        mb=14,
        name="head",
        us=20.0,
    )(h1, tot1, h2, tot2, wp, wo, bias, rowm)


def back_mid_kernel(
    n1b, tot1, n2b, gp2, tot2, dsum, tot3, w1a, w1b, w2a, w2b, rowm, dact, dfac, dfnext, dn, st
):
    valid = rowm[:, 2:3]

    @pl.loop(0, NT)
    def _(j):
        cols = at(j, TILE)
        for s, (a, b) in enumerate(SEGS):
            mean, scale = norm_rows(tot2, s, cols)
            along = tot3[s : s + 1, cols]
            cross = tot3[3 + s : 4 + s, cols]
            part = rowm[a:b, 0:1] / tot1[6:7, s : s + 1]
            n2 = n2b[a:b, cols].astype(F32)
            back = scale * (dsum[a:b, cols] - part * (along + cross * n2))
            dact[a:b, cols] = (gp2[a:b, cols] * back).astype(BF)

    ua = dot_nt(dact[...], w2a[...])
    ub = dot_nt(dact[...], w2b[...])
    f = ((ua + pltpu.roll(ub, 1, 0)) * valid).astype(BF)
    dfac[...] = f
    dfnext[...] = (pltpu.roll(f.astype(F32), ROWS - 1, 0) * valid).astype(BF)

    @pl.loop(0, NT)
    def _(j):
        cols = at(j, TILE)
        grad = bypass_scale * dsum[:, cols] + dot_nt(dfac[...], w1b[cols, :]) + dot_nt(dfnext[...], w1a[cols, :])
        dn[:, cols] = grad
        for s, (a, b) in enumerate(SEGS):
            put_grads(st, cols, s, grad[a:b], n1b[a:b, cols].astype(F32))

    st[6:8, :] = jnp.zeros((2, HID), F32)


def back_mid(n1b, tot1, n2b, gp2, tot2, dsum, tot3, w1a, w1b, w2a, w2b, rowm):
    return kernel_call(
        back_mid_kernel,
        [
            here((ROWS, HID), BF),
            here((ROWS, 256), BF),
            here((ROWS, 256), BF),
            here((ROWS, HID)),
            shape((8, HID)),
        ],
        "nvnnvnvnnnnv",
        name="back_mid",
        us=5.9,
    )(n1b, tot1, n2b, gp2, tot2, dsum, tot3, w1a, w1b, w2a, w2b, rowm)


def side_out_kernel(me, summed, dpre, go, keep, send, edge, gbp, flat):
    ones = jnp.ones((16, ROWS), BF)
    gbp[...] = dot(ones, dpre[...])[0:8]
    for j in range(NT):
        t = summed[:, TILE * j : TILE * j + TILE].astype(F32).T.astype(BF)
        g = dot(t, dpre[...])
        put_columns(flat, 2 * TILE * j, lambda c: g[:, c : c + 128], TILE, PRE)
    put_columns(flat, OFF[4] - OFF[3], lambda c: go[:, c : c + 128].astype(F32), PRE, SEN)
    flat[ROWS_ALL - OFF[3] :, :] = jnp.zeros((FLAT - ROWS_ALL, 128), F32)
    edge[...] = flat[0:16, :]
    for dc, out in ((0, keep), (1, send)):
        for k in range(4):
            for j in range(4):
                d = me[0] ^ (8 * k + 2 * j + dc)

                @pl.when(d > 12)
                def _():
                    out[j, k] = flat[pl.ds(block_row(d) - OFF[3], BLK), :].astype(BF)


def side_out(me, summed, dpre, go):
    return kernel_call(
        side_out_kernel,
        [here((4, 4, BLK, 128), BF), here((4, 4, BLK, 128), BF), shape((16, 128)), shape((8, PRE))],
        "snvn",
        [vmem((FLAT - OFF[3], 128))],
        mb=14,
        name="side_out",
        us=4.0,
    )(me, summed, dpre, go)


def side_mid_kernel(
    me, edge, fac, fnext, dact, rounded, dfac, dfnext, _, keep_in, send_in, keep, send, gbs, flat, tall, tall2
):
    fac_t = fac[...].astype(F32).T.astype(BF)
    next_t = fnext[...].astype(F32).T.astype(BF)
    ones = jnp.ones((16, ROWS), BF)
    flat[0 : OFF[1] - FROM, :] = jnp.zeros((OFF[1] - FROM, 128), F32)
    for j in range(NT):
        cols = slice(TILE * j, TILE * j + TILE)
        t = rounded[:, cols].astype(F32).T.astype(BF)
        for k, d in enumerate((dfnext, dfac)):
            g = dot(t, d[...])
            tall[HID * k + TILE * j : HID * k + TILE * j + TILE, :] = g[:, 0:128]
            tall2[HID * k + TILE * j : HID * k + TILE * j + TILE, :] = g[:, 128:256]
        for k, f in enumerate((fac_t, next_t)):
            g = dot(f, dact[:, cols])
            for q in range(TILE // 128):
                row = OFF[2] - FROM + 1920 * k + TILE // 128 * j + q
                flat[pl.ds(row, BOT, stride=12), :] = g[0:BOT, 128 * q : 128 * q + 128]
        gbs[:, cols] = dot(ones, dact[:, cols])[0:8]
    put_first(flat, OFF[1] - FROM, tall, tall2)
    flat[OFF[3] - FROM : OFF[3] - FROM + 16, :] = edge[...]
    flat[OFF[3] - FROM + 16 :, :] = jnp.zeros((7968 - (OFF[3] - FROM + 16), 128), F32)
    for dc, src, out in ((0, keep_in, keep), (1, send_in, send)):
        for k in range(4):
            for j in range(4):
                d = me[0] ^ (8 * k + 2 * j + dc)

                @pl.when(d > 12)
                def _():
                    out[j, k] = src[j, k]

                @pl.when((d > 2) & (d < 13))
                def _():
                    out[j, k] = flat[pl.ds(block_row(d) - FROM, BLK), :].astype(BF)

                @pl.when(d < 3)
                def _():
                    out[j, k] = jnp.zeros((BLK, 128), BF)


def side_mid(me, keep, send, *args):
    return kernel_call(
        side_mid_kernel,
        [here((4, 4, BLK, 128), BF), here((4, 4, BLK, 128), BF), shape((8, HID))],
        "svnnnnnnnnn",
        [vmem((7968, 128)), vmem((3072, 128)), vmem((3072, 128))],
        mb=14,
        name="side_mid",
        us=6.4,
    )(me, *args, keep, send)


def back_in_kernel(me, n1b, gp, tot1, dn, tot4, spl_t, rowm, keep, send, gb, d, flat):
    @pl.loop(0, NT)
    def _(j):
        cols = at(j, TILE)
        for s, (a, b) in enumerate(SEGS):
            mean, scale = norm_rows(tot1, s, cols)
            along = tot4[s : s + 1, cols]
            cross = tot4[3 + s : 4 + s, cols]
            part = rowm[a:b, 0:1] / tot1[6:7, s : s + 1]
            n1 = n1b[a:b, cols].astype(F32)
            back = scale * (dn[a:b, cols] - part * (along + cross * n1))
            d[a:b, cols] = (gp[a:b, cols] * back).astype(BF)

    for j in range(NT):
        g = dot(spl_t[...], d[:, TILE * j : TILE * j + TILE])
        gb[:, TILE * j : TILE * j + TILE] = g[216:224]
        for q in range(TILE // 128):
            flat[pl.ds(TILE // 128 * j + q, 220, stride=12), :] = g[0:220, 128 * q : 128 * q + 128]
    flat[OFF[1] :, :] = jnp.zeros((2 * CHIP + 14 - OFF[1], 128), F32)
    for dc, out in ((0, keep), (1, send)):
        for dx in (0, 1):
            t = (me[0] & 3) ^ (2 * dx + dc)
            out[dx] = flat[pl.ds(block_row(t), BLK), :].astype(BF)


def back_in(me, n1b, gp, tot1, dn, tot4, spl_t, rowm):
    return kernel_call(
        back_in_kernel,
        [shape((2, BLK, 128), BF), shape((2, BLK, 128), BF), shape((8, HID))],
        "snnvnvvv",
        [vmem((ROWS, HID), BF), vmem((2 * CHIP + 14, 128))],
        name="back_in",
        us=2.8,
    )(me, n1b, gp, tot1, dn, tot4, spl_t, rowm)


def move(x, n, mask, to=None):
    return lax.ppermute(x, "dp", [(i, i ^ mask) for i in range(n) if to is None or to(i ^ mask)])


def exchange(x, n, masks):
    a, b, c = (move(x, n, k) for k in masks)
    return (x + a) + (b + c)


def sum_core(x, n):
    return x + move(x, n, 1)


def sum_layers(x, n):
    return exchange(x, n, (8, 16, 24))


def sum_plane(x, n):
    return exchange(x, n, (2, 4, 6))


def total(x, n):
    if n == 32:
        return sum_plane(sum_layers(sum_core(x, n), n), n)
    bit = 1
    while bit < n:
        x = x + move(x, n, bit)
        bit = 2 * bit
    return x


def fits(n, shard):
    return n == 32 and 2 * shard == CHIP * 128


def once(v, *earlier):
    return lax.optimization_barrier((v,) + earlier)[0]


def gather_blocks(shard, n, make, inputs):
    size = shard.shape[0]
    if fits(n, size):
        own = jnp.pad(shard, (0, BLK * 128 - size)).reshape(BLK, 128)
        own_x = move(own, n, 2)
        second, first, third = (move(own, n, 8 * k) for k in (2, 1, 3))
        meanwhile = make(*once(inputs, own_x))
        one = jnp.stack([own, own_x])
        one = jnp.concatenate([one, move(one, n, 4)])
        one, first, meanwhile = lax.optimization_barrier((one, first, meanwhile))
        three = jnp.stack([first, move(first, n, 2)])
        two = jnp.stack([second, move(second, n, 4)])
        four = jnp.stack([third, move(third, n, 4)])
        two, three = lax.optimization_barrier((two, three))
        left = jnp.concatenate([one, two, move(two, n, 2)])
        right = jnp.concatenate([three, move(three, n, 4), four, move(four, n, 2)])
        return [left, move(left, n, 1), right, move(right, n, 1)], meanwhile
    flat = lax.all_gather(shard, "dp", axis=0, tiled=True).reshape(32, -1)
    blocks = jnp.pad(flat, ((0, 0), (0, BLK * 128 - flat.shape[1]))).reshape(4, 2, 2, 2, BLK, 128)
    groups = []
    for core, layers in GROUPS:
        v = blocks[:, :, :, core]
        both = [v[layers[0]], v[layers[1]].transpose(1, 0, 2, 3)]
        groups.append(jnp.stack(both).reshape(8, BLK, 128))
    return groups, make(*inputs)


def add(a, b):
    return (a.astype(F32) + b.astype(F32)).astype(BF)


def fold_core_kernel(keep, come, ak, asend, bk, bsend):
    for j in range(4):
        for k in range(4):
            v = add(keep[j, k], come[j, k])
            (ak, asend)[j & 1][j >> 1, k] = v[:HALF]
            (bk, bsend)[j >> 1][j & 1, k] = v[HALF:]


def fold_core(keep, come):
    part = here((2, 4, HALF, 128), BF)
    return kernel_call(fold_core_kernel, [part] * 4, "vv", mb=16, name="fold_core", us=2.0)(keep, come)


def fold_first_kernel(keep, come, ak, asend, b):
    v = [add(keep[x], come[x]) for x in (0, 1)]
    ak[...] = v[0][:HALF]
    asend[...] = v[1][:HALF]
    for x in (0, 1):
        b[x] = v[x][HALF:]


def fold_first(keep, come):
    outs = [shape((HALF, 128), BF), shape((HALF, 128), BF), shape((2, HALF, 128), BF)]
    return kernel_call(fold_first_kernel, outs, "vv", name="fold_first", us=0.6)(keep, come)


def fold_plane_kernel(me, ak, acome, bk, bcome, fak, facome, fb, fbcome, ak2, asend2, bk2, bsend2):
    z, y = me[0] >> 3, (me[0] >> 2) & 1
    for i, (a, b) in enumerate(((ak2, bk2), (asend2, bsend2))):
        for k in range(4):
            a[k] = add(ak[i, k], acome[i, k])
            b[k] = add(bk[i, k], bcome[i, k])

        @pl.when(y == i)
        def _():
            a[z] = add(a[z], add(fak[...], facome[...]))

        @pl.when(y == 0)
        def _():
            b[z] = add(b[z], add(fb[i], fbcome[i]))


def fold_plane(me, *args):
    part = here((4, HALF, 128), BF)
    return kernel_call(fold_plane_kernel, [part] * 4, "s" + "v" * 8, name="fold_plane", us=1.0)(me, *args)


def fold_layers_kernel(ak, acome, bk, bcome, *outs):
    for k, out in enumerate(outs):
        out[0:HALF] = add(ak[k], acome[k])
        out[HALF:] = add(bk[k], bcome[k])


def fold_layers(*args):
    return kernel_call(fold_layers_kernel, [shape((BLK, 128), BF)] * 4, "vvvv", name="fold_layers", us=0.6)(*args)


def to_rows(even, odd):
    return jnp.concatenate([even[:, :794], odd[:, :795]], axis=1).reshape(-1, 128)


def own_kernel(me, v0, v1, v2, v3, gbi, gbs, gbp, gbo, loss, rowm, grad, last):
    g = (v0[...].astype(F32) + v1[...].astype(F32)) + (v2[...].astype(F32) + v3[...].astype(F32))
    grad[0:BLK, :] = g
    grad[BLK:, :] = jnp.zeros((8, 128), F32)
    row = lax.broadcasted_iota(jnp.int32, (BLK, 128), 0)
    lane = lax.broadcasted_iota(jnp.int32, (BLK, 128), 1)
    place = 128 * row + lane - 64 * (me[0] & 1)
    mine = jnp.where((place >= 0) & (place < 64 * CHIP), g, 0.0)
    square = jnp.sum(jnp.sum(mine * mine, axis=0, keepdims=True), axis=1, keepdims=True)
    weight = jnp.sum(rowm[:, 1:2], axis=0, keepdims=True)
    at_row = 0
    for src, line, count in ((gbi, 4, 12), (gbs, 0, 12), (gbp, 0, 2), (gbo, 0, 47)):
        for j in range(count):
            last[at_row : at_row + 1, :] = src[line : line + 1, 128 * j : 128 * j + 128]
            at_row = at_row + 1
    lane = lax.broadcasted_iota(jnp.int32, (1, 128), 1)
    extra = jnp.where(lane == 0, square, jnp.where(lane == 1, loss[0:1, :], jnp.where(lane == 2, weight, 0.0)))
    last[at_row : at_row + 1, :] = extra
    last[at_row + 1 :, :] = jnp.zeros((80 - at_row - 1, 128), F32)


def own_sums(me, *args):
    return kernel_call(
        own_kernel,
        [here((BLK + 8, 128)), shape((80, 128))],
        "s" + "v" * 10,
        name="own_sums",
        us=1.0,
    )(me, *args)


def adam(value, grad, first, second, decay):
    first = beta_one * first + (1.0 - beta_one) * grad
    second = beta_two * second + (1.0 - beta_two) * grad * grad
    first_hat = first * (1.0 / (1.0 - beta_one**STEP))
    second_hat = second * (1.0 / (1.0 - beta_two**STEP))
    value = value - learn_rate * (first_hat / (jnp.sqrt(second_hat) + adam_eps) + decay * value)
    return (value, first, second)


def update_kernel(me, last, grad, w, m, v, b, bm, bv, nw, nm, nv, nb, nbm, nbv, loss, weight, norm):
    rows = NBIAS // 128
    total = last[0:rows, :]
    squares = jnp.sum(jnp.sum(total * total, axis=0, keepdims=True), axis=1, keepdims=True)
    size = jnp.sqrt(squares + last[rows : rows + 1, 0:1])
    scale = jnp.minimum(1.0, clip_norm / size)
    norm[0, 0] = jnp.sum(size)
    loss[0, 0] = jnp.sum(last[rows : rows + 1, 1:2])
    weight[0, 0] = jnp.sum(last[rows : rows + 1, 2:3])
    odd = (me[0] & 1) == 1

    def weights(start, count):
        cols = pl.ds(start, 128 * count)
        row = start // 128
        low = grad[pl.ds(row, count), :]
        high = grad[pl.ds(row + 1, count), :]
        lane = lax.broadcasted_iota(jnp.int32, (count, 128), 1)
        turned = jnp.where(lane < 64, pltpu.roll(low, 64, 1), pltpu.roll(high, 64, 1))
        g = jnp.where(odd, turned, low) * scale
        load = lambda ref: ref[0:1, cols].reshape(count, 128)
        for ref, out in zip((nw, nm, nv), adam(load(w), g, load(m), load(v), decay_rate)):
            ref[0:1, cols] = out.reshape(1, 128 * count)

    wide = 72
    whole = w.shape[1] // 128
    for row in range(0, whole // 8 * 8, wide):
        weights(128 * row, min(wide, whole // 8 * 8 - row))
    for row in range(whole // 8 * 8, whole):
        weights(128 * row, 1)
    cols = slice(128 * whole, 128 * whole + 64)
    low, high = grad[whole : whole + 1, :], grad[whole + 1 : whole + 2, :]
    g = jnp.where(odd, pltpu.roll(low, 64, 1), low)[:, 0:64] * scale
    for ref, out in zip((nw, nm, nv), adam(w[0:1, cols], g, m[0:1, cols], v[0:1, cols], decay_rate)):
        ref[0:1, cols] = out
    for row in range(0, rows, 8):
        count = min(8, rows - row)
        cols = slice(128 * row, 128 * (row + count))
        load = lambda ref: ref[cols].reshape(count, 128)
        for ref, out in zip((nb, nbm, nbv), adam(load(b), total[row : row + count] * scale, load(bm), load(bv), 0.0)):
            ref[cols] = out.reshape(128 * count)


def update(me, last, grad, w, m, v, b, bm, bv):
    one = jax.ShapeDtypeStruct((1, 1), F32)
    return pl.pallas_call(
        update_kernel,
        out_shape=(shape(w.shape),) * 3 + (shape(b.shape),) * 3 + (one,) * 3,
        in_specs=[SM] + [VM] * 8,
        out_specs=(VM,) * 6 + (SM,) * 3,
        compiler_params=params(12),
        name="update",
    )(me, last, grad, w, m, v, b, bm, bv)


def adam_all(last, grad, w, m, v, b, bm, bv):
    total = last[: NBIAS // 128].reshape(-1)
    squares, loss_sum, loss_weight = (last[NBIAS // 128, k] for k in range(3))
    norm = jnp.sqrt(squares + jnp.sum(total * total))
    scale = jnp.minimum(jnp.float32(1.0), clip_norm / norm)
    new = adam(w, (grad * scale)[None], m, v, decay_rate) + adam(b, total * scale, bm, bv, 0.0)
    return (*new, loss_sum, loss_weight, norm)


def prepare_kernel(feats, ivecs, meta, spl, spl_t, rowm, rows, ivs):
    rows[...] = jnp.zeros_like(rows)
    frames = feats[...].astype(F32)
    columns = meta[...].T
    rowm[...] = jnp.zeros_like(rowm)
    first = 0
    for start, length in zip(START, SPAN):
        rows[8 + start : 8 + start + length, 0:FEAT] = frames[first : first + length]
        rowm[start : start + length, :] = columns[first : first + length]
        first = first + length
    ivs[...] = jnp.zeros_like(ivs)
    ivs[0:4, 0:IVEC] = ivecs[...].astype(F32)
    row = lax.broadcasted_iota(jnp.int32, (ROWS, 128), 0)
    lane = lax.broadcasted_iota(jnp.int32, (ROWS, 128), 1)
    iv = ivs[3:4, :]
    for k in (2, 1, 0):
        iv = jnp.where(row < START[k + 1], ivs[k : k + 1, :], iv)
    left = rows[7 : 7 + ROWS, :]
    left = jnp.where(lane < FEAT, left, pltpu.roll(rows[8 : 8 + ROWS, :], FEAT, 1))
    left = jnp.where(lane < 2 * FEAT, left, pltpu.roll(rows[9 : 9 + ROWS, :], 2 * FEAT, 1))
    left = jnp.where(lane < 3 * FEAT, left, pltpu.roll(iv, 3 * FEAT, 1))
    ones = 3 * FEAT + IVEC - 128
    right = jnp.where(lane < ones, pltpu.roll(iv, 3 * FEAT, 1), jnp.where(lane == ones, 1.0, 0.0))
    spl[:, 0:128] = left.astype(BF)
    spl[:, 128:256] = right.astype(BF)
    spl_t[0:128, :] = left.T.astype(BF)
    spl_t[128:256, :] = right.T.astype(BF)


def prepare(features, ivectors, frame_mask, labels, confidence):
    mask = frame_mask.astype(F32)
    meta = jnp.stack([mask, confidence * mask, jnp.ones_like(mask), labels.astype(F32)])
    meta = jnp.pad(meta, ((0, 4), (0, ROWS - mask.shape[0])))
    return kernel_call(
        prepare_kernel,
        [shape((ROWS, 256), BF), shape((256, ROWS), BF), shape((ROWS, 8))],
        "vvv",
        [vmem((ROWS + 16, 128)), vmem((8, 128))],
        name="prepare",
        us=2.0,
    )(features, ivectors, meta)


def on_device(
    features,
    ivectors,
    frame_mask,
    labels,
    confidence,
    weights,
    first_moment,
    second_moment,
    biases,
    bias_first,
    bias_second,
):
    n = lax.axis_size("dp")
    size = weights.shape[1]
    index = lax.axis_index("dp")
    fast = fits(n, size)
    me = index if fast else jnp.int32(0)
    place = me.reshape(1)
    blocks, (spliced, spl_t, rowm) = gather_blocks(
        weights.astype(BF).reshape(-1), n, prepare, (features, ivectors, frame_mask, labels, confidence)
    )
    bias = biases[None]
    w_in = unpack_in(place, blocks)
    h1, gp1, st = layer_in(spliced, w_in, bias, rowm)
    if fast:
        tot1 = sum_core(st, n)
        w1a, w1b, w2a, w2b = unpack_mid(place, once(blocks, tot1))
        tot1 = sum_layers(tot1, n)
        tot1, w1a = lax.optimization_barrier((tot1, w1a))
        flat_out = flatten_out(place, once(blocks, tot1))
        tot1 = sum_plane(tot1, n)
        tot1, flat_out = lax.optimization_barrier((tot1, flat_out))
    else:
        tot1 = total(st, n)
        w1a, w1b, w2a, w2b = unpack_mid(place, blocks)
        flat_out = flatten_out(place, blocks)
    rounded, fac, fnext, h2, gp2, st = layer_mid(h1, tot1, w1a, w1b, w2a, w2b, bias, rowm)
    if fast:
        tot2 = sum_core(st, n)
        w_pre, w_out = unpack_out(once(flat_out, tot2), h2)
        tot2 = sum_layers(tot2, n)
        tot2, w_pre = lax.optimization_barrier((tot2, w_pre))
        tot2 = sum_plane(tot2, n)
    else:
        tot2 = total(st, n)
        w_pre, w_out = unpack_out(flat_out, h2)
    summed, n2b, dpre, dsum, go, gbo, st, loss = head(h1, tot1, h2, tot2, w_pre, w_out, bias, rowm)
    tot3 = sum_layers(sum_core(st, n), n) if fast else total(st, n)
    keep, send, edge, gbp = side_out(place, *once((summed, dpre, go), tot3))
    if fast:
        tot3 = sum_plane(tot3, n)
        tot3, keep = lax.optimization_barrier((tot3, keep))
    dact, dfac, dfnext, dn, st = back_mid(rounded, tot1, n2b, gp2, tot2, dsum, tot3, w1a, w1b, w2a, w2b, rowm)
    parts = (edge, fac, fnext, dact, rounded, dfac, dfnext, dn)
    if fast:
        tot4 = sum_core(st, n)
        keep, send, gbs = side_mid(place, keep, send, *once(parts, tot4))
        keep, send, tot4 = lax.optimization_barrier((keep, send, tot4))
        blocks = fold_core(keep, move(send, n, 1))
        tot4, blocks = lax.optimization_barrier((sum_plane(tot4, n), blocks))
        tot4 = sum_layers(tot4, n)
        a_keep, a_send, b_keep, b_send = blocks
        a_come, b_come = move(a_send, n, 2), move(b_send, n, 4)
    else:
        tot4 = total(st, n)
        keep, send, gbs = side_mid(place, keep, send, *parts)
    keep_in, send_in, gbi = back_in(place, rounded, gp1, tot1, dn, tot4, spl_t, rowm)
    if fast:
        first = fold_first(keep_in, move(send_in, n, 1))
        a_come, b_come, first = lax.optimization_barrier((a_come, b_come, first))
        first_keep, first_send, first_b = first
        first_a = (first_keep, move(first_send, n, 2))
        first_b = (first_b, move(first_b, n, 4, lambda t: (t & 4) == 0))
        a_keep, a_send, b_keep, b_send = fold_plane(place, a_keep, a_come, b_keep, b_come, *first_a, *first_b)
        parts = fold_layers(a_keep, move(a_send, n, 4), b_keep, move(b_send, n, 2))
        parts = [parts[0]] + [move(parts[k], n, 8 * k) for k in (1, 2, 3)]
        grad, last = own_sums(place, *parts, gbi, gbs, gbp, gbo, loss, rowm)
        *new, loss_sum, loss_weight, norm = update(
            place, total(last, n), grad, weights, first_moment, second_moment, biases, bias_first, bias_second
        )
        return (*new, loss_sum.reshape(()), loss_weight.reshape(()), norm.reshape(()))
    in_order = lambda v: v.transpose(1, 0, 2, 3).reshape(16, BLK, 128)
    rows = to_rows(in_order(keep), in_order(send))
    rows = jnp.concatenate([rows[: 2 * CHIP] + to_rows(keep_in, send_in), rows[2 * CHIP :]], axis=0)
    grad = lax.psum_scatter(rows.astype(F32).reshape(n, size), "dp", scatter_dimension=0, tiled=True).reshape(-1)
    bias_grad = jnp.concatenate([gbi[4], gbs[0], gbp[0], gbo[0, :SEN]])
    extra = jnp.stack([jnp.sum(grad * grad), loss[0, 0], jnp.sum(rowm[:, 1])])
    last = total(jnp.concatenate([bias_grad, jnp.pad(extra, (0, 7 * 128 - 3))]).reshape(80, 128), n)
    return adam_all(last, grad, weights, first_moment, second_moment, biases, bias_first, bias_second)


def solution(mesh):
    return jax.shard_map(
        on_device,
        mesh=mesh,
        in_specs=(
            P("dp", None),
            P("dp", None),
            P("dp"),
            P("dp"),
            P("dp"),
            P("dp", None),
            P("dp", None),
            P("dp", None),
            P(),
            P(),
            P(),
        ),
        out_specs=(P("dp", None), P("dp", None), P("dp", None), P(), P(), P(), P(), P(), P()),
        check_vma=False,
    )
```

```python
import functools
import math

import jax
import jax.numpy as jnp
from jax import lax
from jax.experimental import pallas as pl
from jax.experimental.pallas import tpu as pltpu
from jax.sharding import PartitionSpec as P

FEAT = 40
IVEC = 100
HID = 1536
BOT = 160
PRE = 256
SEN = 6016
SPAN = (140, 140, 150, 300)
START = (0, 144, 288, 448)
ROWS = 768
SEGS = ((0, 288), (288, 448), (448, 768))
SENP = 6144
STEP = 10
NBIAS = 9344

bypass_scale = 0.66
norm_eps = 0.001
learn_rate = 0.05
beta_one = 0.9
beta_two = 0.999
adam_eps = 1e-08
decay_rate = 0.01
clip_norm = 1.0

F32 = jnp.float32
BF = jnp.bfloat16
VM = pl.BlockSpec(memory_space=pltpu.VMEM)
SM = pl.BlockSpec(memory_space=pltpu.SMEM)
HB = pl.BlockSpec(memory_space=pltpu.HBM)

CHIP = 1589
BLK = 800
GROUPS = ((0, (0, 2)), (1, (0, 2)), (0, (1, 3)), (1, (1, 3)))
OFF = (0, 2640, 6480, 10320, 13392)
ROWS_ALL = 16 * CHIP
TILE = 256
NT = HID // TILE
WIDE = 1024
NW = SENP // WIDE
FLAT = ROWS_ALL + 64
FROM = 2376
HALF = BLK // 2
BIG = 512
NB = HID // BIG
GELU_C = math.sqrt(2.0 / math.pi)


def shape(dims, kind=F32):
    return jax.ShapeDtypeStruct(dims, kind)


def params(mb):
    return pltpu.CompilerParams(vmem_limit_bytes=mb * 2**20)


def here(dims, kind=F32):
    return pltpu.VMEM(dims, kind)


def kernel_call(body, outs, ins, scratch=(), mb=12, name=None, us=1.0):
    spec = {"s": SM, "v": VM, "n": VM, "h": HB}
    call = pl.pallas_call(
        body,
        out_shape=tuple(outs),
        in_specs=[spec[k] for k in ins],
        out_specs=tuple(VM for _ in outs),
        scratch_shapes=list(scratch),
        compiler_params=params(mb),
        cost_estimate=pl.CostEstimate(flops=int(us * 1e9), bytes_accessed=int(us * 3e6), transcendentals=0),
        name=name,
    )
    return lambda *args: call(
        *(pltpu.with_memory_space_constraint(v, pltpu.VMEM) if k == "n" else v for k, v in zip(ins, args))
    )


def sems(n):
    return pltpu.SemaphoreType.DMA((n,))


def vmem(dims, kind=F32):
    return pltpu.VMEM(dims, kind)


def dot(a, b):
    return jnp.dot(a, b, preferred_element_type=F32)


def dot_nt(a, b):
    return lax.dot_general(a, b, (((1,), (1,)), ((), ())), preferred_element_type=F32)


def at(j, size):
    return pl.ds(pl.multiple_of(j * size, size), size)


def block_row(d):
    return (d >> 1) * CHIP + (d & 1) * 794


def put_block(flat, d, v, start=0):
    first = block_row(d) - start
    v = v.astype(F32)
    if d % 2:
        v = pltpu.roll(v, 64, 1)
        low = lax.broadcasted_iota(jnp.int32, v.shape, 1) < 64
        flat[first : first + 1, :] = jnp.where(low[0:1], flat[first : first + 1, :], v[0:1])
        flat[first + 1 : first + 795, :] = jnp.where(low[:794], v[0:794], v[1:795])
    else:
        flat[first : first + 795, :] = v[:795]


def fetch_blocks(me, groups, first, last, stage, sem):
    for src, (core, layers) in zip(groups, GROUPS):
        for i in range(8):
            low, high = i & 1, (i >> 1) & 1
            x, y = (low, high) if i < 4 else (high, low)
            d = me[0] ^ (8 * layers[i // 4] + 4 * y + 2 * x + core)

            @pl.when((d >= first) & (d <= last))
            def _():
                pltpu.make_async_copy(src.at[i], stage.at[d - first], sem.at[d - first]).start()


def block_ready(src, d, stage, sem):
    pltpu.make_async_copy(src.at[0], stage.at[d], sem.at[d]).wait()


def unpack_in_kernel(me, g0, g1, g2, g3, win, stage, flat, sem):
    fetch_blocks(me, (g0, g1, g2, g3), 0, 3, stage, sem)
    for d in range(4):
        block_ready(g0, d, stage, sem)
        put_block(flat, d, stage[d])
    for j in range(12):
        v = flat[pl.ds(j, 224, stride=12), :]
        v = jnp.where(lax.broadcasted_iota(jnp.int32, (224, 128), 0) < 220, v, 0.0)
        win[0:224, 128 * j : 128 * j + 128] = v.astype(BF)
    win[224:256, :] = jnp.zeros((32, HID), BF)


def unpack_in(me, groups):
    return kernel_call(
        unpack_in_kernel,
        [here((256, HID), BF)],
        "shhhh",
        [vmem((4, BLK, 128), BF), vmem((2 * CHIP + 14, 128)), sems(4)],
        name="unpack_in",
        us=1.5,
    )(me, *groups)[0]


def unpack_mid_kernel(me, g0, g1, g2, g3, w1a, w1b, w2a, w2b, stage, flat, tall, tall2, sem):
    fetch_blocks(me, (g0, g1, g2, g3), 2, 12, stage, sem)
    start = block_row(2)
    first, second = OFF[1] - start, OFF[2] - start
    for d in range(2, 13):
        block_ready(g0, d - 2, stage, sem)
        put_block(flat, d, stage[d - 2], start)
    lane = lax.broadcasted_iota(jnp.int32, (768, 128), 1)
    a = [flat[pl.ds(first + q, 768, stride=5), :] for q in range(5)]

    def put(r, t0, t1):
        tall[pl.ds(r, 768, stride=4), :] = t0
        tall2[pl.ds(r, 768, stride=4), :] = jnp.where(lane < 32, t1, 0.0)

    put(0, a[0], a[1])
    for r in (1, 2, 3):
        turn = 128 - 32 * r
        low = pltpu.roll(a[r], turn, 1)
        high = pltpu.roll(a[r + 1], turn, 1)
        put(r, jnp.where(lane < turn, low, high), high)
    for out, row in ((w1a, 0), (w1b, 1536)):
        out[:, 0:128] = tall[row : row + 1536, :].astype(BF)
        out[:, 128:256] = tall2[row : row + 1536, :].astype(BF)
    for j in range(12):
        v = flat[pl.ds(second + j, 320, stride=12), :].astype(BF)
        w2a[0:160, 128 * j : 128 * j + 128] = v[:160]
        w2b[0:160, 128 * j : 128 * j + 128] = v[160:]
    w2a[160:256, :] = jnp.zeros((96, HID), BF)
    w2b[160:256, :] = jnp.zeros((96, HID), BF)


def unpack_mid(me, groups):
    return kernel_call(
        unpack_mid_kernel,
        [here((HID, 256), BF)] * 2 + [here((256, HID), BF)] * 2,
        "shhhh",
        [
            vmem((11, BLK, 128), BF),
            vmem((6 * CHIP, 128)),
            vmem((3072, 128)),
            vmem((3072, 128)),
            sems(11),
        ],
        mb=15,
        name="unpack_mid",
        us=5.2,
    )(me, *groups)


SPLIT = 22


def flatten_out_kernel(first, last, me, g0, g1, g2, g3, flat, stage, sem):
    fetch_blocks(me, (g0, g1, g2, g3), first, last, stage, sem)
    for d in range(first, last + 1):
        block_ready(g0, d - first, stage, sem)
        put_block(flat, d, stage[d - first], block_row(first))


def flatten_out(me, groups, first, last):
    count = last + 1 - first
    return kernel_call(
        functools.partial(flatten_out_kernel, first, last),
        [here((CHIP * count // 2, 128))],
        "shhhh",
        [vmem((count, BLK, 128), BF), sems(count)],
        name="flatten_out",
        us=3.0,
    )(me, *groups)[0]


def unpack_out_kernel(one, two, _, wp, wo, flat):
    pre, out = OFF[3] - block_row(12), OFF[4] - block_row(12)
    flat[0 : one.shape[0], :] = one[...]
    flat[one.shape[0] :, :] = two[...]
    for j in range(2):
        wp[:, 128 * j : 128 * j + 128] = flat[pl.ds(pre + j, 1536, stride=2), :].astype(BF)
    for j in range(47):
        wo[:, 128 * j : 128 * j + 128] = flat[pl.ds(out + j, 256, stride=47), :].astype(BF)
    wo[:, 6016:] = jnp.zeros((256, 128), BF)


def unpack_out(one, two, h2):
    return kernel_call(
        unpack_out_kernel,
        [here((HID, PRE), BF), here((PRE, SENP), BF)],
        "nnn",
        [vmem((10 * CHIP, 128))],
        mb=14,
        name="unpack_out",
        us=3.0,
    )(one, two, h2)


def put_columns(flat, first, grad, rows, width):
    for j in range(width // 128):
        flat[pl.ds(first + j, rows, stride=width // 128), :] = grad(128 * j)


def put_first(flat, first, tall, tall2):
    lane = lax.broadcasted_iota(jnp.int32, (768, 128), 1)
    t0 = [tall[pl.ds(r, 768, stride=4), :] for r in range(4)]
    t1 = [tall2[pl.ds(r, 768, stride=4), :] for r in range(4)]
    flat[pl.ds(first, 768, stride=5), :] = t0[0]
    for q in (1, 2, 3):
        shift = 32 * (q - 1)
        tail = t1[0]
        if q > 1:
            tail = jnp.where(lane < shift, pltpu.roll(t0[q - 1], shift, 1), pltpu.roll(t1[q - 1], shift, 1))
        flat[pl.ds(first + q, 768, stride=5), :] = jnp.where(lane < 32 * q, tail, pltpu.roll(t0[q], 32 * q, 1))
    flat[pl.ds(first + 4, 768, stride=5), :] = jnp.where(
        lane < 96, pltpu.roll(t0[3], 96, 1), pltpu.roll(t1[3], 96, 1)
    )


def gelu_parts(act):
    square = act * act
    t = jnp.tanh(GELU_C * act * (1.0 + 0.044715 * square))
    cdf = 0.5 + 0.5 * t
    slope = cdf + (0.5 * act) * (1.0 - t * t) * (GELU_C + (3 * 0.044715 * GELU_C) * square)
    return act * cdf, slope


def put_sums(st, first, v):
    for s, (a, b) in enumerate(SEGS):
        st[first + s : first + s + 1, :] = jnp.sum(v[a:b], axis=0, keepdims=True)


def norm_rows(tot, s, cols):
    count = tot[6:7, s : s + 1]
    mean = tot[s : s + 1, cols] / count
    var = tot[3 + s : 4 + s, cols] / count - mean * mean
    return mean, lax.rsqrt(var + norm_eps)


def put_stats(st, cols, hidden, mask):
    masked = hidden * mask
    square = masked * hidden
    for s, (a, b) in enumerate(SEGS):
        st[s : s + 1, cols] = jnp.sum(masked[a:b], axis=0, keepdims=True)
        st[3 + s : 4 + s, cols] = jnp.sum(square[a:b], axis=0, keepdims=True)


def put_counts(st, mask):
    lane = lax.broadcasted_iota(jnp.int32, (2, HID), 1)
    counts = [jnp.sum(mask[a:b], axis=0, keepdims=True) for a, b in SEGS]
    st[6:8, :] = jnp.where(lane == 0, counts[0], jnp.where(lane == 1, counts[1], counts[2]))


def put_grads(st, cols, s, grad, normed):
    st[s : s + 1, cols] = jnp.sum(grad, axis=0, keepdims=True)
    st[3 + s : 4 + s, cols] = jnp.sum(grad * normed, axis=0, keepdims=True)


def in_kernel(spl, w, b, rowm, h, gp, st):
    mask = rowm[:, 0:1]

    @pl.loop(0, NB)
    def _(j):
        cols = at(j, BIG)
        hidden, slope = gelu_parts(dot(spl[...], w[:, cols]) + b[:, cols])
        h[:, cols] = hidden
        gp[:, cols] = slope.astype(BF)
        put_stats(st, cols, hidden, mask)

    put_counts(st, mask)


def layer_in(spliced, w_in, b_in, rowm):
    return kernel_call(
        in_kernel,
        [here((ROWS, HID)), here((ROWS, HID), BF), shape((8, HID))],
        "vnvv",
        name="layer_in",
        us=4.1,
    )(spliced, w_in, b_in, rowm)


def mid_kernel(h, tot, w1a, w1b, w2a, w2b, bias, rowm, rounded, fac, fnext, h2, gp2, st):
    valid = rowm[:, 2:3]
    mask = rowm[:, 0:1]

    @pl.loop(0, NT)
    def _(j):
        cols = at(j, TILE)
        for s, (a, b) in enumerate(SEGS):
            mean, scale = norm_rows(tot, s, cols)
            rounded[a:b, cols] = ((h[a:b, cols] - mean) * scale).astype(BF)

    ua = dot(rounded[...], w1a[...])
    ub = dot(rounded[...], w1b[...])
    f = ((ub + pltpu.roll(ua * valid, 1, 0)) * valid).astype(BF)
    fac[...] = f
    fnext[...] = (pltpu.roll(f.astype(F32), ROWS - 1, 0) * valid).astype(BF)

    @pl.loop(0, NB)
    def _(j):
        cols = at(j, BIG)
        act = dot(fac[...], w2a[:, cols]) + dot(fnext[...], w2b[:, cols]) + bias[:, at(j + HID // BIG, BIG)]
        hidden, slope = gelu_parts(act)
        h2[:, cols] = hidden
        gp2[:, cols] = slope.astype(BF)
        put_stats(st, cols, hidden, mask)

    put_counts(st, mask)


def layer_mid(h, tot, w1a, w1b, w2a, w2b, bias, rowm):
    return kernel_call(
        mid_kernel,
        [
            here((ROWS, HID), BF),
            here((ROWS, 256), BF),
            here((ROWS, 256), BF),
            here((ROWS, HID)),
            here((ROWS, HID), BF),
            shape((8, HID)),
        ],
        "nvnnnnvv",
        name="layer_mid",
        us=7.4,
    )(h, tot, w1a, w1b, w2a, w2b, bias, rowm)


def head_kernel(
    h1, tot1, h2, tot2, wp, wo, bias, rowm, summed, n2b, dpre, dsum, go, gb, st, loss, acc
):
    @pl.loop(0, NT)
    def _(j):
        cols = at(j, TILE)
        for s, (a, b) in enumerate(SEGS):
            mean1, scale1 = norm_rows(tot1, s, cols)
            mean2, scale2 = norm_rows(tot2, s, cols)
            n1 = (h1[a:b, cols] - mean1) * scale1
            n2 = (h2[a:b, cols] - mean2) * scale2
            summed[a:b, cols] = (n2 + bypass_scale * n1).astype(BF)
            n2b[a:b, cols] = n2.astype(BF)

    pre = (dot(summed[...], wp[...]) + bias[:, 2 * HID : 2 * HID + PRE]).astype(BF)
    lane = lax.broadcasted_iota(jnp.int32, (ROWS, 128), 1)
    where = rowm[:, 3:4].astype(jnp.int32) - lane
    weight = rowm[:, 1:2]

    bo = jnp.concatenate([bias[:, 2 * HID + PRE :], jnp.full((1, SENP - SEN), -1e30, F32)], axis=1)

    m = jnp.full((ROWS, 128), -1e30, F32)
    total = jnp.zeros((ROWS, 128), F32)
    for j in range(NW):
        cols = slice(WIDE * j, WIDE * j + WIDE)
        v = dot(pre, wo[:, cols]) + bo[:, cols]
        parts = [v[:, 128 * q : 128 * q + 128] for q in range(WIDE // 128)]
        old = m
        for p in parts:
            m = jnp.maximum(m, p)
        total = total * jnp.exp(old - m)
        for p in parts:
            total = total + jnp.exp(p - m)

    top = jnp.max(m, axis=1, keepdims=True)
    total = jnp.sum(total * jnp.exp(m - top), axis=1, keepdims=True)
    lse = jnp.log(total) + top
    less = lse - jnp.log(weight)
    acc[...] = jnp.zeros_like(acc)
    pre_t = jnp.concatenate([pre.astype(F32).T.astype(BF), jnp.ones((16, ROWS), BF)], axis=0)
    picked = jnp.zeros((ROWS, 128), F32)
    for j in range(NW):
        cols = slice(WIDE * j, WIDE * j + WIDE)
        v = dot(pre, wo[:, cols]) + bo[:, cols]
        parts = []
        for q in range(WIDE // 128):
            p = v[:, 128 * q : 128 * q + 128]
            hit = jnp.where(where == j * WIDE + 128 * q, weight, 0.0)
            picked = picked + hit * p
            parts.append((jnp.exp(p - less) - hit).astype(BF))
        d = jnp.concatenate(parts, axis=1)
        acc[...] += dot_nt(d, wo[:, cols])
        g = dot(pre_t, d)
        go[:, cols] = g[0:PRE].astype(BF)
        gb[:, cols] = g[PRE : PRE + 8]

    entropy = jnp.sum(weight * lse, axis=0, keepdims=True)
    picked = jnp.sum(jnp.sum(picked, axis=1, keepdims=True), axis=0, keepdims=True)
    loss[...] = jnp.zeros((8, 128), F32) + (entropy - picked)
    dp = acc[...].astype(BF)
    dpre[...] = dp

    @pl.loop(0, NT)
    def _(j):
        cols = at(j, TILE)
        ds = dot_nt(dp, wp[cols, :])
        dsum[:, cols] = ds
        for s, (a, b) in enumerate(SEGS):
            put_grads(st, cols, s, ds[a:b], n2b[a:b, cols].astype(F32))

    st[6:8, :] = jnp.zeros((2, HID), F32)


def head(h1, tot1, h2, tot2, wp, wo, bias, rowm):
    return kernel_call(
        head_kernel,
        [
            here((ROWS, HID), BF),
            here((ROWS, HID), BF),
            here((ROWS, PRE), BF),
            here((ROWS, HID)),
            here((PRE, SENP), BF),
            shape((8, SENP)),
            shape((8, HID)),
            shape((8, 128)),
        ],
        "nvnvnnvv",
        [
            vmem((ROWS, PRE)),
        ],
        mb=14,
        name="head",
        us=20.0,
    )(h1, tot1, h2, tot2, wp, wo, bias, rowm)


def back_mid_kernel(
    n1b, tot1, n2b, gp2, tot2, dsum, tot3, w1a, w1b, w2a, w2b, rowm, dact, dfac, dfnext, dn, st
):
    valid = rowm[:, 2:3]

    @pl.loop(0, NT)
    def _(j):
        cols = at(j, TILE)
        for s, (a, b) in enumerate(SEGS):
            mean, scale = norm_rows(tot2, s, cols)
            along = tot3[s : s + 1, cols]
            cross = tot3[3 + s : 4 + s, cols]
            part = rowm[a:b, 0:1] / tot1[6:7, s : s + 1]
            n2 = n2b[a:b, cols].astype(F32)
            back = scale * (dsum[a:b, cols] - part * (along + cross * n2))
            dact[a:b, cols] = (gp2[a:b, cols] * back).astype(BF)

    ua = dot_nt(dact[...], w2a[...])
    ub = dot_nt(dact[...], w2b[...])
    f = ((ua + pltpu.roll(ub, 1, 0)) * valid).astype(BF)
    dfac[...] = f
    dfnext[...] = (pltpu.roll(f.astype(F32), ROWS - 1, 0) * valid).astype(BF)

    @pl.loop(0, NT)
    def _(j):
        cols = at(j, TILE)
        grad = bypass_scale * dsum[:, cols] + dot_nt(dfac[...], w1b[cols, :]) + dot_nt(dfnext[...], w1a[cols, :])
        dn[:, cols] = grad
        for s, (a, b) in enumerate(SEGS):
            put_grads(st, cols, s, grad[a:b], n1b[a:b, cols].astype(F32))

    st[6:8, :] = jnp.zeros((2, HID), F32)


def back_mid(n1b, tot1, n2b, gp2, tot2, dsum, tot3, w1a, w1b, w2a, w2b, rowm):
    return kernel_call(
        back_mid_kernel,
        [
            here((ROWS, HID), BF),
            here((ROWS, 256), BF),
            here((ROWS, 256), BF),
            here((ROWS, HID)),
            shape((8, HID)),
        ],
        "nvnnvnvnnnnv",
        name="back_mid",
        us=5.9,
    )(n1b, tot1, n2b, gp2, tot2, dsum, tot3, w1a, w1b, w2a, w2b, rowm)


def side_out_kernel(me, summed, dpre, go, keep, send, edge, gbp, flat):
    ones = jnp.ones((16, ROWS), BF)
    gbp[...] = dot(ones, dpre[...])[0:8]
    for j in range(NT):
        t = summed[:, TILE * j : TILE * j + TILE].astype(F32).T.astype(BF)
        g = dot(t, dpre[...])
        put_columns(flat, 2 * TILE * j, lambda c: g[:, c : c + 128], TILE, PRE)
    put_columns(flat, OFF[4] - OFF[3], lambda c: go[:, c : c + 128].astype(F32), PRE, SEN)
    flat[ROWS_ALL - OFF[3] :, :] = jnp.zeros((FLAT - ROWS_ALL, 128), F32)
    edge[...] = flat[0:16, :]
    for dc, out in ((0, keep), (1, send)):
        for k in range(4):
            for j in range(4):
                d = me[0] ^ (8 * k + 2 * j + dc)

                @pl.when(d > 12)
                def _():
                    out[j, k] = flat[pl.ds(block_row(d) - OFF[3], BLK), :].astype(BF)


def side_out(me, summed, dpre, go):
    return kernel_call(
        side_out_kernel,
        [here((4, 4, BLK, 128), BF), here((4, 4, BLK, 128), BF), shape((16, 128)), shape((8, PRE))],
        "snvn",
        [vmem((FLAT - OFF[3], 128))],
        mb=14,
        name="side_out",
        us=4.0,
    )(me, summed, dpre, go)


def side_mid_kernel(
    me, edge, fac, fnext, dact, rounded, dfac, dfnext, _, keep_in, send_in, keep, send, gbs, flat, tall, tall2
):
    fac_t = fac[...].astype(F32).T.astype(BF)
    next_t = fnext[...].astype(F32).T.astype(BF)
    ones = jnp.ones((16, ROWS), BF)
    flat[0 : OFF[1] - FROM, :] = jnp.zeros((OFF[1] - FROM, 128), F32)
    for j in range(NT):
        cols = slice(TILE * j, TILE * j + TILE)
        t = rounded[:, cols].astype(F32).T.astype(BF)
        for k, d in enumerate((dfnext, dfac)):
            g = dot(t, d[...])
            tall[HID * k + TILE * j : HID * k + TILE * j + TILE, :] = g[:, 0:128]
            tall2[HID * k + TILE * j : HID * k + TILE * j + TILE, :] = g[:, 128:256]
        for k, f in enumerate((fac_t, next_t)):
            g = dot(f, dact[:, cols])
            for q in range(TILE // 128):
                row = OFF[2] - FROM + 1920 * k + TILE // 128 * j + q
                flat[pl.ds(row, BOT, stride=12), :] = g[0:BOT, 128 * q : 128 * q + 128]
        gbs[:, cols] = dot(ones, dact[:, cols])[0:8]
    put_first(flat, OFF[1] - FROM, tall, tall2)
    flat[OFF[3] - FROM : OFF[3] - FROM + 16, :] = edge[...]
    flat[OFF[3] - FROM + 16 :, :] = jnp.zeros((7968 - (OFF[3] - FROM + 16), 128), F32)
    for dc, src, out in ((0, keep_in, keep), (1, send_in, send)):
        for k in range(4):
            for j in range(4):
                d = me[0] ^ (8 * k + 2 * j + dc)

                @pl.when(d > 12)
                def _():
                    out[j, k] = src[j, k]

                @pl.when((d > 2) & (d < 13))
                def _():
                    out[j, k] = flat[pl.ds(block_row(d) - FROM, BLK), :].astype(BF)

                @pl.when(d < 3)
                def _():
                    out[j, k] = jnp.zeros((BLK, 128), BF)


def side_mid(me, keep, send, *args):
    return kernel_call(
        side_mid_kernel,
        [here((4, 4, BLK, 128), BF), here((4, 4, BLK, 128), BF), shape((8, HID))],
        "svnnnnnnnnn",
        [vmem((7968, 128)), vmem((3072, 128)), vmem((3072, 128))],
        mb=14,
        name="side_mid",
        us=6.4,
    )(me, *args, keep, send)


def back_in_kernel(me, n1b, gp, tot1, dn, tot4, spl_t, rowm, keep, send, gb, d, flat):
    @pl.loop(0, NT)
    def _(j):
        cols = at(j, TILE)
        for s, (a, b) in enumerate(SEGS):
            mean, scale = norm_rows(tot1, s, cols)
            along = tot4[s : s + 1, cols]
            cross = tot4[3 + s : 4 + s, cols]
            part = rowm[a:b, 0:1] / tot1[6:7, s : s + 1]
            n1 = n1b[a:b, cols].astype(F32)
            back = scale * (dn[a:b, cols] - part * (along + cross * n1))
            d[a:b, cols] = (gp[a:b, cols] * back).astype(BF)

    for j in range(NT):
        g = dot(spl_t[...], d[:, TILE * j : TILE * j + TILE])
        gb[:, TILE * j : TILE * j + TILE] = g[216:224]
        for q in range(TILE // 128):
            flat[pl.ds(TILE // 128 * j + q, 220, stride=12), :] = g[0:220, 128 * q : 128 * q + 128]
    flat[OFF[1] :, :] = jnp.zeros((2 * CHIP + 14 - OFF[1], 128), F32)
    for dc, out in ((0, keep), (1, send)):
        for dx in (0, 1):
            t = (me[0] & 3) ^ (2 * dx + dc)
            out[dx] = flat[pl.ds(block_row(t), BLK), :].astype(BF)


def back_in(me, n1b, gp, tot1, dn, tot4, spl_t, rowm):
    return kernel_call(
        back_in_kernel,
        [shape((2, BLK, 128), BF), shape((2, BLK, 128), BF), shape((8, HID))],
        "snnvnvvv",
        [vmem((ROWS, HID), BF), vmem((2 * CHIP + 14, 128))],
        name="back_in",
        us=2.8,
    )(me, n1b, gp, tot1, dn, tot4, spl_t, rowm)


def move(x, n, mask, to=None):
    return lax.ppermute(x, "dp", [(i, i ^ mask) for i in range(n) if to is None or to(i ^ mask)])


def exchange(x, n, masks):
    a, b, c = (move(x, n, k) for k in masks)
    return (x + a) + (b + c)


def sum_core(x, n):
    return x + move(x, n, 1)


def sum_layers(x, n):
    return exchange(x, n, (8, 16, 24))


def sum_plane(x, n):
    return exchange(x, n, (2, 4, 6))


def total(x, n):
    if n == 32:
        return sum_plane(sum_layers(sum_core(x, n), n), n)
    bit = 1
    while bit < n:
        x = x + move(x, n, bit)
        bit = 2 * bit
    return x


def fits(n, shard):
    return n == 32 and 2 * shard == CHIP * 128


def once(v, *earlier):
    return lax.optimization_barrier((v,) + earlier)[0]


def gather_blocks(shard, n, make, inputs):
    size = shard.shape[0]
    if fits(n, size):
        own = jnp.pad(shard, (0, BLK * 128 - size)).reshape(BLK, 128)
        own_x = move(own, n, 2)
        first, third, second = (move(own, n, 8 * k) for k in (1, 3, 2))
        meanwhile = make(*once(inputs, own_x))
        one = jnp.stack([own, own_x])
        one = jnp.concatenate([one, move(one, n, 4)])
        one, first, meanwhile = lax.optimization_barrier((one, first, meanwhile))
        three = jnp.stack([first, move(first, n, 2)])
        two = jnp.stack([second, move(second, n, 4)])
        four = jnp.stack([third, move(third, n, 4)])
        two, three = lax.optimization_barrier((two, three))
        left = jnp.concatenate([one, two, move(two, n, 2)])
        right = jnp.concatenate([three, move(three, n, 4), four, move(four, n, 2)])
        return [left, move(left, n, 1), right, move(right, n, 1)], meanwhile
    flat = lax.all_gather(shard, "dp", axis=0, tiled=True).reshape(32, -1)
    blocks = jnp.pad(flat, ((0, 0), (0, BLK * 128 - flat.shape[1]))).reshape(4, 2, 2, 2, BLK, 128)
    groups = []
    for core, layers in GROUPS:
        v = blocks[:, :, :, core]
        both = [v[layers[0]], v[layers[1]].transpose(1, 0, 2, 3)]
        groups.append(jnp.stack(both).reshape(8, BLK, 128))
    return groups, make(*inputs)


def add(a, b):
    return (a.astype(F32) + b.astype(F32)).astype(BF)


def fold_core_kernel(keep, come, ak, asend, bk, bsend):
    for j in range(4):
        for k in range(4):
            v = add(keep[j, k], come[j, k])
            (ak, asend)[j & 1][j >> 1, k] = v[:HALF]
            (bk, bsend)[j >> 1][j & 1, k] = v[HALF:]


def fold_core(keep, come):
    part = here((2, 4, HALF, 128), BF)
    return kernel_call(fold_core_kernel, [part] * 4, "vv", mb=16, name="fold_core", us=2.0)(keep, come)


def fold_first_kernel(keep, come, ak, asend, b):
    v = [add(keep[x], come[x]) for x in (0, 1)]
    ak[...] = v[0][:HALF]
    asend[...] = v[1][:HALF]
    for x in (0, 1):
        b[x] = v[x][HALF:]


def fold_first(keep, come):
    outs = [shape((HALF, 128), BF), shape((HALF, 128), BF), shape((2, HALF, 128), BF)]
    return kernel_call(fold_first_kernel, outs, "vv", name="fold_first", us=0.6)(keep, come)


def fold_plane_kernel(me, ak, acome, bk, bcome, fak, facome, fb, fbcome, ak2, asend2, bk2, bsend2):
    z, y = me[0] >> 3, (me[0] >> 2) & 1
    for i, (a, b) in enumerate(((ak2, bk2), (asend2, bsend2))):
        for k in range(4):
            a[k] = add(ak[i, k], acome[i, k])
            b[k] = add(bk[i, k], bcome[i, k])

        @pl.when(y == i)
        def _():
            a[z] = add(a[z], add(fak[...], facome[...]))

        @pl.when(y == 0)
        def _():
            b[z] = add(b[z], add(fb[i], fbcome[i]))


def fold_plane(me, *args):
    part = here((4, HALF, 128), BF)
    return kernel_call(fold_plane_kernel, [part] * 4, "s" + "v" * 8, name="fold_plane", us=1.0)(me, *args)


def fold_layers_kernel(ak, acome, bk, bcome, *outs):
    for k, out in enumerate(outs):
        out[0:HALF] = add(ak[k], acome[k])
        out[HALF:] = add(bk[k], bcome[k])


def fold_layers(*args):
    return kernel_call(fold_layers_kernel, [shape((BLK, 128), BF)] * 4, "vvvv", name="fold_layers", us=0.6)(*args)


def to_rows(even, odd):
    return jnp.concatenate([even[:, :794], odd[:, :795]], axis=1).reshape(-1, 128)


def own_kernel(me, v0, v1, v2, v3, gbi, gbs, gbp, gbo, loss, rowm, grad, last):
    g = (v0[...].astype(F32) + v1[...].astype(F32)) + (v2[...].astype(F32) + v3[...].astype(F32))
    grad[0:BLK, :] = g
    grad[BLK:, :] = jnp.zeros((8, 128), F32)
    row = lax.broadcasted_iota(jnp.int32, (BLK, 128), 0)
    lane = lax.broadcasted_iota(jnp.int32, (BLK, 128), 1)
    place = 128 * row + lane - 64 * (me[0] & 1)
    mine = jnp.where((place >= 0) & (place < 64 * CHIP), g, 0.0)
    square = jnp.sum(jnp.sum(mine * mine, axis=0, keepdims=True), axis=1, keepdims=True)
    weight = jnp.sum(rowm[:, 1:2], axis=0, keepdims=True)
    at_row = 0
    for src, line, count in ((gbi, 4, 12), (gbs, 0, 12), (gbp, 0, 2), (gbo, 0, 47)):
        for j in range(count):
            last[at_row : at_row + 1, :] = src[line : line + 1, 128 * j : 128 * j + 128]
            at_row = at_row + 1
    lane = lax.broadcasted_iota(jnp.int32, (1, 128), 1)
    extra = jnp.where(lane == 0, square, jnp.where(lane == 1, loss[0:1, :], jnp.where(lane == 2, weight, 0.0)))
    last[at_row : at_row + 1, :] = extra
    last[at_row + 1 :, :] = jnp.zeros((80 - at_row - 1, 128), F32)


def own_sums(me, *args):
    return kernel_call(
        own_kernel,
        [here((BLK + 8, 128)), shape((80, 128))],
        "s" + "v" * 10,
        name="own_sums",
        us=1.0,
    )(me, *args)


def adam(value, grad, first, second, decay):
    first = beta_one * first + (1.0 - beta_one) * grad
    second = beta_two * second + (1.0 - beta_two) * grad * grad
    first_hat = first * (1.0 / (1.0 - beta_one**STEP))
    second_hat = second * (1.0 / (1.0 - beta_two**STEP))
    value = value - learn_rate * (first_hat / (jnp.sqrt(second_hat) + adam_eps) + decay * value)
    return (value, first, second)


def update_kernel(me, last, grad, w, m, v, b, bm, bv, nw, nm, nv, nb, nbm, nbv, loss, weight, norm):
    rows = NBIAS // 128
    total = last[0:rows, :]
    squares = jnp.sum(jnp.sum(total * total, axis=0, keepdims=True), axis=1, keepdims=True)
    size = jnp.sqrt(squares + last[rows : rows + 1, 0:1])
    scale = jnp.minimum(1.0, clip_norm / size)
    norm[0, 0] = jnp.sum(size)
    loss[0, 0] = jnp.sum(last[rows : rows + 1, 1:2])
    weight[0, 0] = jnp.sum(last[rows : rows + 1, 2:3])
    odd = (me[0] & 1) == 1

    def weights(start, count):
        cols = pl.ds(start, 128 * count)
        row = start // 128
        low = grad[pl.ds(row, count), :]
        high = grad[pl.ds(row + 1, count), :]
        lane = lax.broadcasted_iota(jnp.int32, (count, 128), 1)
        turned = jnp.where(lane < 64, pltpu.roll(low, 64, 1), pltpu.roll(high, 64, 1))
        g = jnp.where(odd, turned, low) * scale
        load = lambda ref: ref[0:1, cols].reshape(count, 128)
        for ref, out in zip((nw, nm, nv), adam(load(w), g, load(m), load(v), decay_rate)):
            ref[0:1, cols] = out.reshape(1, 128 * count)

    wide = 72
    whole = w.shape[1] // 128
    for row in range(0, whole // 8 * 8, wide):
        weights(128 * row, min(wide, whole // 8 * 8 - row))
    for row in range(whole // 8 * 8, whole):
        weights(128 * row, 1)
    cols = slice(128 * whole, 128 * whole + 64)
    low, high = grad[whole : whole + 1, :], grad[whole + 1 : whole + 2, :]
    g = jnp.where(odd, pltpu.roll(low, 64, 1), low)[:, 0:64] * scale
    for ref, out in zip((nw, nm, nv), adam(w[0:1, cols], g, m[0:1, cols], v[0:1, cols], decay_rate)):
        ref[0:1, cols] = out
    for row in range(0, rows, 8):
        count = min(8, rows - row)
        cols = slice(128 * row, 128 * (row + count))
        load = lambda ref: ref[cols].reshape(count, 128)
        for ref, out in zip((nb, nbm, nbv), adam(load(b), total[row : row + count] * scale, load(bm), load(bv), 0.0)):
            ref[cols] = out.reshape(128 * count)


def update(me, last, grad, w, m, v, b, bm, bv):
    one = jax.ShapeDtypeStruct((1, 1), F32)
    return pl.pallas_call(
        update_kernel,
        out_shape=(shape(w.shape),) * 3 + (shape(b.shape),) * 3 + (one,) * 3,
        in_specs=[SM] + [VM] * 8,
        out_specs=(VM,) * 6 + (SM,) * 3,
        compiler_params=params(12),
        name="update",
    )(me, last, grad, w, m, v, b, bm, bv)


def adam_all(last, grad, w, m, v, b, bm, bv):
    total = last[: NBIAS // 128].reshape(-1)
    squares, loss_sum, loss_weight = (last[NBIAS // 128, k] for k in range(3))
    norm = jnp.sqrt(squares + jnp.sum(total * total))
    scale = jnp.minimum(jnp.float32(1.0), clip_norm / norm)
    new = adam(w, (grad * scale)[None], m, v, decay_rate) + adam(b, total * scale, bm, bv, 0.0)
    return (*new, loss_sum, loss_weight, norm)


def prepare_kernel(feats, ivecs, meta, spl, spl_t, rowm, rows, ivs):
    rows[...] = jnp.zeros_like(rows)
    frames = feats[...].astype(F32)
    columns = meta[...].T
    rowm[...] = jnp.zeros_like(rowm)
    first = 0
    for start, length in zip(START, SPAN):
        rows[8 + start : 8 + start + length, 0:FEAT] = frames[first : first + length]
        rowm[start : start + length, :] = columns[first : first + length]
        first = first + length
    ivs[...] = jnp.zeros_like(ivs)
    ivs[0:4, 0:IVEC] = ivecs[...].astype(F32)
    row = lax.broadcasted_iota(jnp.int32, (ROWS, 128), 0)
    lane = lax.broadcasted_iota(jnp.int32, (ROWS, 128), 1)
    iv = ivs[3:4, :]
    for k in (2, 1, 0):
        iv = jnp.where(row < START[k + 1], ivs[k : k + 1, :], iv)
    left = rows[7 : 7 + ROWS, :]
    left = jnp.where(lane < FEAT, left, pltpu.roll(rows[8 : 8 + ROWS, :], FEAT, 1))
    left = jnp.where(lane < 2 * FEAT, left, pltpu.roll(rows[9 : 9 + ROWS, :], 2 * FEAT, 1))
    left = jnp.where(lane < 3 * FEAT, left, pltpu.roll(iv, 3 * FEAT, 1))
    ones = 3 * FEAT + IVEC - 128
    right = jnp.where(lane < ones, pltpu.roll(iv, 3 * FEAT, 1), jnp.where(lane == ones, 1.0, 0.0))
    spl[:, 0:128] = left.astype(BF)
    spl[:, 128:256] = right.astype(BF)
    spl_t[0:128, :] = left.T.astype(BF)
    spl_t[128:256, :] = right.T.astype(BF)


def prepare(features, ivectors, frame_mask, labels, confidence):
    mask = frame_mask.astype(F32)
    meta = jnp.stack([mask, confidence * mask, jnp.ones_like(mask), labels.astype(F32)])
    meta = jnp.pad(meta, ((0, 4), (0, ROWS - mask.shape[0])))
    return kernel_call(
        prepare_kernel,
        [shape((ROWS, 256), BF), shape((256, ROWS), BF), shape((ROWS, 8))],
        "vvv",
        [vmem((ROWS + 16, 128)), vmem((8, 128))],
        name="prepare",
        us=2.0,
    )(features, ivectors, meta)


def on_device(
    features,
    ivectors,
    frame_mask,
    labels,
    confidence,
    weights,
    first_moment,
    second_moment,
    biases,
    bias_first,
    bias_second,
):
    n = lax.axis_size("dp")
    size = weights.shape[1]
    index = lax.axis_index("dp")
    fast = fits(n, size)
    me = index if fast else jnp.int32(0)
    place = me.reshape(1)
    blocks, (spliced, spl_t, rowm) = gather_blocks(
        weights.astype(BF).reshape(-1), n, prepare, (features, ivectors, frame_mask, labels, confidence)
    )
    bias = biases[None]
    w_in = unpack_in(place, blocks)
    h1, gp1, st = layer_in(spliced, w_in, bias, rowm)
    if fast:
        tot1 = sum_core(st, n)
        w1a, w1b, w2a, w2b = unpack_mid(place, once(blocks, tot1))
        tot1 = sum_layers(tot1, n)
        tot1, w1a = lax.optimization_barrier((tot1, w1a))
        flat_out = flatten_out(place, once(blocks, tot1), 12, SPLIT - 1)
        tot1 = sum_plane(tot1, n)
        tot1, flat_out = lax.optimization_barrier((tot1, flat_out))
    else:
        tot1 = total(st, n)
        w1a, w1b, w2a, w2b = unpack_mid(place, blocks)
        flat_out = flatten_out(place, blocks, 12, SPLIT - 1)
        flat_two = flatten_out(place, blocks, SPLIT, 31)
    rounded, fac, fnext, h2, gp2, st = layer_mid(h1, tot1, w1a, w1b, w2a, w2b, bias, rowm)
    if fast:
        tot2 = sum_core(st, n)
        flat_two = flatten_out(place, once(blocks, tot2), SPLIT, 31)
        tot2 = sum_layers(tot2, n)
        tot2, flat_two = lax.optimization_barrier((tot2, flat_two))
        w_pre, w_out = unpack_out(flat_out, once(flat_two, tot2), h2)
        tot2 = sum_plane(tot2, n)
        tot2, w_pre = lax.optimization_barrier((tot2, w_pre))
    else:
        tot2 = total(st, n)
        w_pre, w_out = unpack_out(flat_out, flat_two, h2)
    summed, n2b, dpre, dsum, go, gbo, st, loss = head(h1, tot1, h2, tot2, w_pre, w_out, bias, rowm)
    tot3 = sum_layers(sum_core(st, n), n) if fast else total(st, n)
    keep, send, edge, gbp = side_out(place, *once((summed, dpre, go), tot3))
    if fast:
        tot3 = sum_plane(tot3, n)
        tot3, keep = lax.optimization_barrier((tot3, keep))
    dact, dfac, dfnext, dn, st = back_mid(rounded, tot1, n2b, gp2, tot2, dsum, tot3, w1a, w1b, w2a, w2b, rowm)
    parts = (edge, fac, fnext, dact, rounded, dfac, dfnext, dn)
    if fast:
        tot4 = sum_core(st, n)
        keep, send, gbs = side_mid(place, keep, send, *once(parts, tot4))
        keep, send, tot4 = lax.optimization_barrier((keep, send, tot4))
        blocks = fold_core(keep, move(send, n, 1))
        tot4, blocks = lax.optimization_barrier((sum_plane(tot4, n), blocks))
        tot4 = sum_layers(tot4, n)
        a_keep, a_send, b_keep, b_send = blocks
        a_come, b_come = move(a_send, n, 2), move(b_send, n, 4)
    else:
        tot4 = total(st, n)
        keep, send, gbs = side_mid(place, keep, send, *parts)
    keep_in, send_in, gbi = back_in(place, rounded, gp1, tot1, dn, tot4, spl_t, rowm)
    if fast:
        first = fold_first(keep_in, move(send_in, n, 1))
        first = list(first)
        a_come, first[1] = lax.optimization_barrier((a_come, first[1]))
        first_keep, first_send, first_b = first
        first_a = (first_keep, move(first_send, n, 2))
        first_b = (first_b, move(first_b, n, 4, lambda t: (t & 4) == 0))
        a_keep, a_send, b_keep, b_send = fold_plane(place, a_keep, a_come, b_keep, b_come, *first_a, *first_b)
        parts = fold_layers(a_keep, move(a_send, n, 4), b_keep, move(b_send, n, 2))
        parts = [parts[0]] + [move(parts[k], n, 8 * k) for k in (1, 2, 3)]
        grad, last = own_sums(place, *parts, gbi, gbs, gbp, gbo, loss, rowm)
        *new, loss_sum, loss_weight, norm = update(
            place, total(last, n), grad, weights, first_moment, second_moment, biases, bias_first, bias_second
        )
        return (*new, loss_sum.reshape(()), loss_weight.reshape(()), norm.reshape(()))
    in_order = lambda v: v.transpose(1, 0, 2, 3).reshape(16, BLK, 128)
    rows = to_rows(in_order(keep), in_order(send))
    rows = jnp.concatenate([rows[: 2 * CHIP] + to_rows(keep_in, send_in), rows[2 * CHIP :]], axis=0)
    grad = lax.psum_scatter(rows.astype(F32).reshape(n, size), "dp", scatter_dimension=0, tiled=True).reshape(-1)
    bias_grad = jnp.concatenate([gbi[4], gbs[0], gbp[0], gbo[0, :SEN]])
    extra = jnp.stack([jnp.sum(grad * grad), loss[0, 0], jnp.sum(rowm[:, 1])])
    last = total(jnp.concatenate([bias_grad, jnp.pad(extra, (0, 7 * 128 - 3))]).reshape(80, 128), n)
    return adam_all(last, grad, weights, first_moment, second_moment, biases, bias_first, bias_second)


def solution(mesh):
    return jax.shard_map(
        on_device,
        mesh=mesh,
        in_specs=(
            P("dp", None),
            P("dp", None),
            P("dp"),
            P("dp"),
            P("dp"),
            P("dp", None),
            P("dp", None),
            P("dp", None),
            P(),
            P(),
            P(),
        ),
        out_specs=(P("dp", None), P("dp", None), P("dp", None), P(), P(), P(), P(), P(), P()),
        check_vma=False,
    )
```

```python
import functools
import math

import jax
import jax.numpy as jnp
from jax import lax
from jax.experimental import pallas as pl
from jax.experimental.pallas import tpu as pltpu
from jax.sharding import PartitionSpec as P

FEAT = 40
IVEC = 100
HID = 1536
BOT = 160
PRE = 256
SEN = 6016
SPAN = (140, 140, 150, 300)
START = (0, 144, 288, 448)
ROWS = 768
SEGS = ((0, 288), (288, 448), (448, 768))
SENP = 6144
STEP = 10
NBIAS = 9344

bypass_scale = 0.66
norm_eps = 0.001
learn_rate = 0.05
beta_one = 0.9
beta_two = 0.999
adam_eps = 1e-08
decay_rate = 0.01
clip_norm = 1.0

F32 = jnp.float32
BF = jnp.bfloat16
VM = pl.BlockSpec(memory_space=pltpu.VMEM)
SM = pl.BlockSpec(memory_space=pltpu.SMEM)
HB = pl.BlockSpec(memory_space=pltpu.HBM)

CHIP = 1589
BLK = 800
GROUPS = ((0, (0, 2)), (1, (0, 2)), (0, (1, 3)), (1, (1, 3)))
OFF = (0, 2640, 6480, 10320, 13392)
ROWS_ALL = 16 * CHIP
TILE = 256
NT = HID // TILE
WIDE = 1024
NW = SENP // WIDE
FLAT = ROWS_ALL + 64
FROM = 2376
HALF = BLK // 2
BIG = 512
NB = HID // BIG
GELU_C = math.sqrt(2.0 / math.pi)


def shape(dims, kind=F32):
    return jax.ShapeDtypeStruct(dims, kind)


def params(mb):
    return pltpu.CompilerParams(vmem_limit_bytes=mb * 2**20)


def here(dims, kind=F32):
    return pltpu.VMEM(dims, kind)


def kernel_call(body, outs, ins, scratch=(), mb=12, name=None, us=1.0):
    spec = {"s": SM, "v": VM, "n": VM, "h": HB}
    call = pl.pallas_call(
        body,
        out_shape=tuple(outs),
        in_specs=[spec[k] for k in ins],
        out_specs=tuple(VM for _ in outs),
        scratch_shapes=list(scratch),
        compiler_params=params(mb),
        cost_estimate=pl.CostEstimate(flops=int(us * 1e9), bytes_accessed=int(us * 3e6), transcendentals=0),
        name=name,
    )
    return lambda *args: call(
        *(pltpu.with_memory_space_constraint(v, pltpu.VMEM) if k == "n" else v for k, v in zip(ins, args))
    )


def sems(n):
    return pltpu.SemaphoreType.DMA((n,))


def vmem(dims, kind=F32):
    return pltpu.VMEM(dims, kind)


def dot(a, b):
    return jnp.dot(a, b, preferred_element_type=F32)


def dot_nt(a, b):
    return lax.dot_general(a, b, (((1,), (1,)), ((), ())), preferred_element_type=F32)


def at(j, size):
    return pl.ds(pl.multiple_of(j * size, size), size)


def block_row(d):
    return (d >> 1) * CHIP + (d & 1) * 794


def own_rows_kernel(w, out, lines):
    whole = w.shape[1] // 128
    lines[whole:, :] = jnp.zeros((BLK - whole, 128), F32)
    for row in range(0, whole // 8 * 8, 72):
        count = min(72, whole // 8 * 8 - row)
        lines[row : row + count, :] = w[0:1, 128 * row : 128 * (row + count)].reshape(count, 128)
    for row in range(whole // 8 * 8, whole):
        lines[row : row + 1, :] = w[0:1, 128 * row : 128 * row + 128]
    lines[whole : whole + 1, 0:64] = w[0:1, 128 * whole :]
    out[...] = lines[...].astype(BF)


def own_rows(weights):
    return kernel_call(own_rows_kernel, [shape((BLK, 128), BF)], "v", [vmem((BLK, 128))], name="own_rows", us=1.0)(weights)[0]


def put_block(flat, d, v, start=0):
    first = block_row(d) - start
    v = v.astype(F32)
    if d % 2:
        v = pltpu.roll(v, 64, 1)
        low = lax.broadcasted_iota(jnp.int32, v.shape, 1) < 64
        flat[first : first + 1, :] = jnp.where(low[0:1], flat[first : first + 1, :], v[0:1])
        flat[first + 1 : first + 795, :] = jnp.where(low[:794], v[0:794], v[1:795])
    else:
        flat[first : first + 795, :] = v[:795]


def fetch_blocks(me, groups, first, last, stage, sem):
    for src, (core, layers) in zip(groups, GROUPS):
        for i in range(8):
            low, high = i & 1, (i >> 1) & 1
            x, y = (low, high) if i < 4 else (high, low)
            d = me[0] ^ (8 * layers[i // 4] + 4 * y + 2 * x + core)

            @pl.when((d >= first) & (d <= last))
            def _():
                pltpu.make_async_copy(src.at[i], stage.at[d - first], sem.at[d - first]).start()


def block_ready(src, d, stage, sem):
    pltpu.make_async_copy(src.at[0], stage.at[d], sem.at[d]).wait()


def unpack_in_kernel(me, g0, g1, g2, g3, win, stage, flat, sem):
    fetch_blocks(me, (g0, g1, g2, g3), 0, 3, stage, sem)
    for d in range(4):
        block_ready(g0, d, stage, sem)
        put_block(flat, d, stage[d])
    for j in range(12):
        v = flat[pl.ds(j, 224, stride=12), :]
        v = jnp.where(lax.broadcasted_iota(jnp.int32, (224, 128), 0) < 220, v, 0.0)
        win[0:224, 128 * j : 128 * j + 128] = v.astype(BF)
    win[224:256, :] = jnp.zeros((32, HID), BF)


def unpack_in(me, groups):
    return kernel_call(
        unpack_in_kernel,
        [here((256, HID), BF)],
        "shhhh",
        [vmem((4, BLK, 128), BF), vmem((2 * CHIP + 14, 128)), sems(4)],
        name="unpack_in",
        us=1.5,
    )(me, *groups)[0]


def unpack_mid_kernel(me, g0, g1, g2, g3, w1a, w1b, w2a, w2b, stage, flat, tall, tall2, sem):
    fetch_blocks(me, (g0, g1, g2, g3), 2, 12, stage, sem)
    start = block_row(2)
    first, second = OFF[1] - start, OFF[2] - start
    for d in range(2, 13):
        block_ready(g0, d - 2, stage, sem)
        put_block(flat, d, stage[d - 2], start)
    lane = lax.broadcasted_iota(jnp.int32, (768, 128), 1)
    a = [flat[pl.ds(first + q, 768, stride=5), :] for q in range(5)]

    def put(r, t0, t1):
        tall[pl.ds(r, 768, stride=4), :] = t0
        tall2[pl.ds(r, 768, stride=4), :] = jnp.where(lane < 32, t1, 0.0)

    put(0, a[0], a[1])
    for r in (1, 2, 3):
        turn = 128 - 32 * r
        low = pltpu.roll(a[r], turn, 1)
        high = pltpu.roll(a[r + 1], turn, 1)
        put(r, jnp.where(lane < turn, low, high), high)
    for out, row in ((w1a, 0), (w1b, 1536)):
        out[:, 0:128] = tall[row : row + 1536, :].astype(BF)
        out[:, 128:256] = tall2[row : row + 1536, :].astype(BF)
    for j in range(12):
        v = flat[pl.ds(second + j, 320, stride=12), :].astype(BF)
        w2a[0:160, 128 * j : 128 * j + 128] = v[:160]
        w2b[0:160, 128 * j : 128 * j + 128] = v[160:]
    w2a[160:256, :] = jnp.zeros((96, HID), BF)
    w2b[160:256, :] = jnp.zeros((96, HID), BF)


def unpack_mid(me, groups):
    return kernel_call(
        unpack_mid_kernel,
        [here((HID, 256), BF)] * 2 + [here((256, HID), BF)] * 2,
        "shhhh",
        [
            vmem((11, BLK, 128), BF),
            vmem((6 * CHIP, 128)),
            vmem((3072, 128)),
            vmem((3072, 128)),
            sems(11),
        ],
        mb=15,
        name="unpack_mid",
        us=5.2,
    )(me, *groups)


SPLIT = 22


def flatten_out_kernel(first, last, me, g0, g1, g2, g3, flat, stage, sem):
    fetch_blocks(me, (g0, g1, g2, g3), first, last, stage, sem)
    for d in range(first, last + 1):
        block_ready(g0, d - first, stage, sem)
        put_block(flat, d, stage[d - first], block_row(first))


def flatten_out(me, groups, first, last):
    count = last + 1 - first
    return kernel_call(
        functools.partial(flatten_out_kernel, first, last),
        [here((CHIP * count // 2, 128))],
        "shhhh",
        [vmem((count, BLK, 128), BF), sems(count)],
        name="flatten_out",
        us=3.0,
    )(me, *groups)[0]


def unpack_out_kernel(one, two, _, wp, wo, flat):
    pre, out = OFF[3] - block_row(12), OFF[4] - block_row(12)
    flat[0 : one.shape[0], :] = one[...]
    flat[one.shape[0] :, :] = two[...]
    for j in range(2):
        wp[:, 128 * j : 128 * j + 128] = flat[pl.ds(pre + j, 1536, stride=2), :].astype(BF)
    for j in range(47):
        wo[:, 128 * j : 128 * j + 128] = flat[pl.ds(out + j, 256, stride=47), :].astype(BF)
    wo[:, 6016:] = jnp.zeros((256, 128), BF)


def unpack_out(one, two, h2):
    return kernel_call(
        unpack_out_kernel,
        [here((HID, PRE), BF), here((PRE, SENP), BF)],
        "nnn",
        [vmem((10 * CHIP, 128))],
        mb=14,
        name="unpack_out",
        us=3.0,
    )(one, two, h2)


def put_columns(flat, first, grad, rows, width):
    for j in range(width // 128):
        flat[pl.ds(first + j, rows, stride=width // 128), :] = grad(128 * j)


def put_first(flat, first, tall, tall2):
    lane = lax.broadcasted_iota(jnp.int32, (768, 128), 1)
    t0 = [tall[pl.ds(r, 768, stride=4), :] for r in range(4)]
    t1 = [tall2[pl.ds(r, 768, stride=4), :] for r in range(4)]
    flat[pl.ds(first, 768, stride=5), :] = t0[0]
    for q in (1, 2, 3):
        shift = 32 * (q - 1)
        tail = t1[0]
        if q > 1:
            tail = jnp.where(lane < shift, pltpu.roll(t0[q - 1], shift, 1), pltpu.roll(t1[q - 1], shift, 1))
        flat[pl.ds(first + q, 768, stride=5), :] = jnp.where(lane < 32 * q, tail, pltpu.roll(t0[q], 32 * q, 1))
    flat[pl.ds(first + 4, 768, stride=5), :] = jnp.where(
        lane < 96, pltpu.roll(t0[3], 96, 1), pltpu.roll(t1[3], 96, 1)
    )


def gelu_parts(act):
    square = act * act
    t = jnp.tanh(GELU_C * act * (1.0 + 0.044715 * square))
    cdf = 0.5 + 0.5 * t
    slope = cdf + (0.5 * act) * (1.0 - t * t) * (GELU_C + (3 * 0.044715 * GELU_C) * square)
    return act * cdf, slope


def put_sums(st, first, v):
    for s, (a, b) in enumerate(SEGS):
        st[first + s : first + s + 1, :] = jnp.sum(v[a:b], axis=0, keepdims=True)


def norm_rows(tot, s, cols):
    count = tot[6:7, s : s + 1]
    mean = tot[s : s + 1, cols] / count
    var = tot[3 + s : 4 + s, cols] / count - mean * mean
    return mean, lax.rsqrt(var + norm_eps)


def put_stats(st, cols, hidden, mask):
    masked = hidden * mask
    square = masked * hidden
    for s, (a, b) in enumerate(SEGS):
        st[s : s + 1, cols] = jnp.sum(masked[a:b], axis=0, keepdims=True)
        st[3 + s : 4 + s, cols] = jnp.sum(square[a:b], axis=0, keepdims=True)


def put_counts(st, mask):
    lane = lax.broadcasted_iota(jnp.int32, (2, HID), 1)
    counts = [jnp.sum(mask[a:b], axis=0, keepdims=True) for a, b in SEGS]
    st[6:8, :] = jnp.where(lane == 0, counts[0], jnp.where(lane == 1, counts[1], counts[2]))


def put_grads(st, cols, s, grad, normed):
    st[s : s + 1, cols] = jnp.sum(grad, axis=0, keepdims=True)
    st[3 + s : 4 + s, cols] = jnp.sum(grad * normed, axis=0, keepdims=True)


def in_kernel(spl, w, b, rowm, h, gp, st):
    mask = rowm[:, 0:1]

    @pl.loop(0, NB)
    def _(j):
        cols = at(j, BIG)
        hidden, slope = gelu_parts(dot(spl[...], w[:, cols]) + b[:, cols])
        h[:, cols] = hidden
        gp[:, cols] = slope.astype(BF)
        put_stats(st, cols, hidden, mask)

    put_counts(st, mask)


def layer_in(spliced, w_in, b_in, rowm):
    return kernel_call(
        in_kernel,
        [here((ROWS, HID)), here((ROWS, HID), BF), shape((8, HID))],
        "vnvv",
        name="layer_in",
        us=4.1,
    )(spliced, w_in, b_in, rowm)


def mid_kernel(h, tot, w1a, w1b, w2a, w2b, bias, rowm, rounded, fac, fnext, h2, gp2, st):
    valid = rowm[:, 2:3]
    mask = rowm[:, 0:1]

    @pl.loop(0, NT)
    def _(j):
        cols = at(j, TILE)
        for s, (a, b) in enumerate(SEGS):
            mean, scale = norm_rows(tot, s, cols)
            rounded[a:b, cols] = ((h[a:b, cols] - mean) * scale).astype(BF)

    ua = dot(rounded[...], w1a[...])
    ub = dot(rounded[...], w1b[...])
    f = ((ub + pltpu.roll(ua * valid, 1, 0)) * valid).astype(BF)
    fac[...] = f
    fnext[...] = (pltpu.roll(f.astype(F32), ROWS - 1, 0) * valid).astype(BF)

    @pl.loop(0, NB)
    def _(j):
        cols = at(j, BIG)
        act = dot(fac[...], w2a[:, cols]) + dot(fnext[...], w2b[:, cols]) + bias[:, at(j + HID // BIG, BIG)]
        hidden, slope = gelu_parts(act)
        h2[:, cols] = hidden
        gp2[:, cols] = slope.astype(BF)
        put_stats(st, cols, hidden, mask)

    put_counts(st, mask)


def layer_mid(h, tot, w1a, w1b, w2a, w2b, bias, rowm):
    return kernel_call(
        mid_kernel,
        [
            here((ROWS, HID), BF),
            here((ROWS, 256), BF),
            here((ROWS, 256), BF),
            here((ROWS, HID)),
            here((ROWS, HID), BF),
            shape((8, HID)),
        ],
        "nvnnnnvv",
        name="layer_mid",
        us=7.4,
    )(h, tot, w1a, w1b, w2a, w2b, bias, rowm)


def head_kernel(
    h1, tot1, h2, tot2, wp, wo, bias, rowm, summed, n2b, dpre, dsum, go, gb, st, loss, pre_out, acc
):
    @pl.loop(0, NT)
    def _(j):
        cols = at(j, TILE)
        for s, (a, b) in enumerate(SEGS):
            mean1, scale1 = norm_rows(tot1, s, cols)
            mean2, scale2 = norm_rows(tot2, s, cols)
            n1 = (h1[a:b, cols] - mean1) * scale1
            n2 = (h2[a:b, cols] - mean2) * scale2
            summed[a:b, cols] = (n2 + bypass_scale * n1).astype(BF)
            n2b[a:b, cols] = n2.astype(BF)

    pre = (dot(summed[...], wp[...]) + bias[:, 2 * HID : 2 * HID + PRE]).astype(BF)
    lane = lax.broadcasted_iota(jnp.int32, (ROWS, 128), 1)
    where = rowm[:, 3:4].astype(jnp.int32) - lane
    weight = rowm[:, 1:2]

    bo = jnp.concatenate([bias[:, 2 * HID + PRE :], jnp.full((1, SENP - SEN), -1e30, F32)], axis=1)

    m = jnp.full((ROWS, 128), -1e30, F32)
    total = jnp.zeros((ROWS, 128), F32)
    for j in range(NW):
        cols = slice(WIDE * j, WIDE * j + WIDE)
        v = dot(pre, wo[:, cols]) + bo[:, cols]
        parts = [v[:, 128 * q : 128 * q + 128] for q in range(WIDE // 128)]
        old = m
        for p in parts:
            m = jnp.maximum(m, p)
        total = total * jnp.exp(old - m)
        for p in parts:
            total = total + jnp.exp(p - m)

    top = jnp.max(m, axis=1, keepdims=True)
    total = jnp.sum(total * jnp.exp(m - top), axis=1, keepdims=True)
    lse = jnp.log(total) + top
    less = lse - jnp.log(weight)
    acc[...] = jnp.zeros_like(acc)
    pre_t = jnp.concatenate([pre.astype(F32).T.astype(BF), jnp.ones((16, ROWS), BF)], axis=0)
    for j in range(NW):
        cols = slice(WIDE * j, WIDE * j + WIDE)
        v = dot(pre, wo[:, cols]) + bo[:, cols]
        parts = []
        for q in range(WIDE // 128):
            p = v[:, 128 * q : 128 * q + 128]
            hit = jnp.where(where == j * WIDE + 128 * q, weight, 0.0)
            parts.append((jnp.exp(p - less) - hit).astype(BF))
        d = jnp.concatenate(parts, axis=1)
        acc[...] += dot_nt(d, wo[:, cols])
        g = dot(pre_t, d)
        go[:, cols] = g[0:PRE].astype(BF)
        gb[:, cols] = g[PRE : PRE + 8]

    entropy = jnp.sum(weight * lse, axis=0, keepdims=True)
    loss[...] = jnp.zeros((8, 128), F32) + entropy
    pre_out[...] = pre
    dp = acc[...].astype(BF)
    dpre[...] = dp

    @pl.loop(0, NT)
    def _(j):
        cols = at(j, TILE)
        ds = dot_nt(dp, wp[cols, :])
        dsum[:, cols] = ds
        for s, (a, b) in enumerate(SEGS):
            put_grads(st, cols, s, ds[a:b], n2b[a:b, cols].astype(F32))

    st[6:8, :] = jnp.zeros((2, HID), F32)


def head(h1, tot1, h2, tot2, wp, wo, bias, rowm):
    return kernel_call(
        head_kernel,
        [
            here((ROWS, HID), BF),
            here((ROWS, HID), BF),
            here((ROWS, PRE), BF),
            here((ROWS, HID)),
            here((PRE, SENP), BF),
            shape((8, SENP)),
            shape((8, HID)),
            shape((8, 128)),
            shape((ROWS, PRE), BF),
        ],
        "nvnvnnvv",
        [
            vmem((ROWS, PRE)),
        ],
        mb=14,
        name="head",
        us=20.0,
    )(h1, tot1, h2, tot2, wp, wo, bias, rowm)


def picked_kernel(pre, wo, bias, rowm, out):
    lane = lax.broadcasted_iota(jnp.int32, (ROWS, 128), 1)
    where = rowm[:, 3:4].astype(jnp.int32) - lane
    weight = rowm[:, 1:2]
    bo = jnp.concatenate([bias[:, 2 * HID + PRE :], jnp.zeros((1, SENP - SEN), F32)], axis=1)
    total = jnp.zeros((ROWS, 128), F32)
    for j in range(NW):
        cols = slice(WIDE * j, WIDE * j + WIDE)
        v = dot(pre[...], wo[:, cols]) + bo[:, cols]
        for q in range(WIDE // 128):
            total = total + jnp.where(where == j * WIDE + 128 * q, v[:, 128 * q : 128 * q + 128], 0.0)
    total = jnp.sum(total, axis=1, keepdims=True) * weight
    out[...] = jnp.zeros((8, 128), F32) + jnp.sum(total, axis=0, keepdims=True)


def picked_sum(pre, wo, bias, rowm):
    return kernel_call(picked_kernel, [shape((8, 128))], "vvvv", mb=14, name="picked_sum", us=5.0)(pre, wo, bias, rowm)[0]


def back_mid_kernel(
    n1b, tot1, n2b, gp2, tot2, dsum, tot3, w1a, w1b, w2a, w2b, rowm, dact, dfac, dfnext, dn, st
):
    valid = rowm[:, 2:3]

    @pl.loop(0, NT)
    def _(j):
        cols = at(j, TILE)
        for s, (a, b) in enumerate(SEGS):
            mean, scale = norm_rows(tot2, s, cols)
            along = tot3[s : s + 1, cols]
            cross = tot3[3 + s : 4 + s, cols]
            part = rowm[a:b, 0:1] / tot1[6:7, s : s + 1]
            n2 = n2b[a:b, cols].astype(F32)
            back = scale * (dsum[a:b, cols] - part * (along + cross * n2))
            dact[a:b, cols] = (gp2[a:b, cols] * back).astype(BF)

    ua = dot_nt(dact[...], w2a[...])
    ub = dot_nt(dact[...], w2b[...])
    f = ((ua + pltpu.roll(ub, 1, 0)) * valid).astype(BF)
    dfac[...] = f
    dfnext[...] = (pltpu.roll(f.astype(F32), ROWS - 1, 0) * valid).astype(BF)

    @pl.loop(0, NT)
    def _(j):
        cols = at(j, TILE)
        grad = bypass_scale * dsum[:, cols] + dot_nt(dfac[...], w1b[cols, :]) + dot_nt(dfnext[...], w1a[cols, :])
        dn[:, cols] = grad
        for s, (a, b) in enumerate(SEGS):
            put_grads(st, cols, s, grad[a:b], n1b[a:b, cols].astype(F32))

    st[6:8, :] = jnp.zeros((2, HID), F32)


def back_mid(n1b, tot1, n2b, gp2, tot2, dsum, tot3, w1a, w1b, w2a, w2b, rowm):
    return kernel_call(
        back_mid_kernel,
        [
            here((ROWS, HID), BF),
            here((ROWS, 256), BF),
            here((ROWS, 256), BF),
            here((ROWS, HID)),
            shape((8, HID)),
        ],
        "nvnnvnvnnnnv",
        name="back_mid",
        us=5.9,
    )(n1b, tot1, n2b, gp2, tot2, dsum, tot3, w1a, w1b, w2a, w2b, rowm)


def side_out_kernel(me, summed, dpre, go, keep, send, edge, gbp, flat):
    ones = jnp.ones((16, ROWS), BF)
    gbp[...] = dot(ones, dpre[...])[0:8]
    for j in range(NT):
        t = summed[:, TILE * j : TILE * j + TILE].astype(F32).T.astype(BF)
        g = dot(t, dpre[...])
        put_columns(flat, 2 * TILE * j, lambda c: g[:, c : c + 128], TILE, PRE)
    put_columns(flat, OFF[4] - OFF[3], lambda c: go[:, c : c + 128].astype(F32), PRE, SEN)
    flat[ROWS_ALL - OFF[3] :, :] = jnp.zeros((FLAT - ROWS_ALL, 128), F32)
    edge[...] = flat[0:16, :]
    for dc, out in ((0, keep), (1, send)):
        for k in range(4):
            for j in range(4):
                d = me[0] ^ (8 * k + 2 * j + dc)

                @pl.when(d > 12)
                def _():
                    out[j, k] = flat[pl.ds(block_row(d) - OFF[3], BLK), :].astype(BF)


def side_out(me, summed, dpre, go):
    return kernel_call(
        side_out_kernel,
        [here((4, 4, BLK, 128), BF), here((4, 4, BLK, 128), BF), shape((16, 128)), shape((8, PRE))],
        "snvn",
        [vmem((FLAT - OFF[3], 128))],
        mb=14,
        name="side_out",
        us=4.0,
    )(me, summed, dpre, go)


def side_mid_kernel(
    me, edge, fac, fnext, dact, rounded, dfac, dfnext, _, keep_in, send_in, keep, send, gbs, flat, tall, tall2
):
    fac_t = fac[...].astype(F32).T.astype(BF)
    next_t = fnext[...].astype(F32).T.astype(BF)
    ones = jnp.ones((16, ROWS), BF)
    flat[0 : OFF[1] - FROM, :] = jnp.zeros((OFF[1] - FROM, 128), F32)
    for j in range(NT):
        cols = slice(TILE * j, TILE * j + TILE)
        t = rounded[:, cols].astype(F32).T.astype(BF)
        for k, d in enumerate((dfnext, dfac)):
            g = dot(t, d[...])
            tall[HID * k + TILE * j : HID * k + TILE * j + TILE, :] = g[:, 0:128]
            tall2[HID * k + TILE * j : HID * k + TILE * j + TILE, :] = g[:, 128:256]
        for k, f in enumerate((fac_t, next_t)):
            g = dot(f, dact[:, cols])
            for q in range(TILE // 128):
                row = OFF[2] - FROM + 1920 * k + TILE // 128 * j + q
                flat[pl.ds(row, BOT, stride=12), :] = g[0:BOT, 128 * q : 128 * q + 128]
        gbs[:, cols] = dot(ones, dact[:, cols])[0:8]
    put_first(flat, OFF[1] - FROM, tall, tall2)
    flat[OFF[3] - FROM : OFF[3] - FROM + 16, :] = edge[...]
    flat[OFF[3] - FROM + 16 :, :] = jnp.zeros((7968 - (OFF[3] - FROM + 16), 128), F32)
    for dc, src, out in ((0, keep_in, keep), (1, send_in, send)):
        for k in range(4):
            for j in range(4):
                d = me[0] ^ (8 * k + 2 * j + dc)

                @pl.when(d > 12)
                def _():
                    out[j, k] = src[j, k]

                @pl.when((d > 2) & (d < 13))
                def _():
                    out[j, k] = flat[pl.ds(block_row(d) - FROM, BLK), :].astype(BF)

                @pl.when(d < 3)
                def _():
                    out[j, k] = jnp.zeros((BLK, 128), BF)


def side_mid(me, keep, send, *args):
    return kernel_call(
        side_mid_kernel,
        [here((4, 4, BLK, 128), BF), here((4, 4, BLK, 128), BF), shape((8, HID))],
        "svnnnnnnnnn",
        [vmem((7968, 128)), vmem((3072, 128)), vmem((3072, 128))],
        mb=14,
        name="side_mid",
        us=6.4,
    )(me, *args, keep, send)


def back_in_kernel(me, n1b, gp, tot1, dn, tot4, spl_t, rowm, keep, send, gb, d, flat):
    @pl.loop(0, NT)
    def _(j):
        cols = at(j, TILE)
        for s, (a, b) in enumerate(SEGS):
            mean, scale = norm_rows(tot1, s, cols)
            along = tot4[s : s + 1, cols]
            cross = tot4[3 + s : 4 + s, cols]
            part = rowm[a:b, 0:1] / tot1[6:7, s : s + 1]
            n1 = n1b[a:b, cols].astype(F32)
            back = scale * (dn[a:b, cols] - part * (along + cross * n1))
            d[a:b, cols] = (gp[a:b, cols] * back).astype(BF)

    for j in range(NT):
        g = dot(spl_t[...], d[:, TILE * j : TILE * j + TILE])
        gb[:, TILE * j : TILE * j + TILE] = g[216:224]
        for q in range(TILE // 128):
            flat[pl.ds(TILE // 128 * j + q, 220, stride=12), :] = g[0:220, 128 * q : 128 * q + 128]
    flat[OFF[1] :, :] = jnp.zeros((2 * CHIP + 14 - OFF[1], 128), F32)
    for dc, out in ((0, keep), (1, send)):
        for dx in (0, 1):
            t = (me[0] & 3) ^ (2 * dx + dc)
            out[dx] = flat[pl.ds(block_row(t), BLK), :].astype(BF)


def back_in(me, n1b, gp, tot1, dn, tot4, spl_t, rowm):
    return kernel_call(
        back_in_kernel,
        [shape((2, BLK, 128), BF), shape((2, BLK, 128), BF), shape((8, HID))],
        "snnvnvvv",
        [vmem((ROWS, HID), BF), vmem((2 * CHIP + 14, 128))],
        name="back_in",
        us=2.8,
    )(me, n1b, gp, tot1, dn, tot4, spl_t, rowm)


def move(x, n, mask, to=None):
    return lax.ppermute(x, "dp", [(i, i ^ mask) for i in range(n) if to is None or to(i ^ mask)])


def exchange(x, n, masks):
    a, b, c = (move(x, n, k) for k in masks)
    return (x + a) + (b + c)


def sum_core(x, n):
    return x + move(x, n, 1)


def sum_layers(x, n):
    return exchange(x, n, (8, 16, 24))


def sum_plane(x, n):
    return exchange(x, n, (2, 4, 6))


def total(x, n):
    if n == 32:
        return sum_plane(sum_layers(sum_core(x, n), n), n)
    bit = 1
    while bit < n:
        x = x + move(x, n, bit)
        bit = 2 * bit
    return x


def fits(n, shard):
    return n == 32 and 2 * shard == CHIP * 128


def once(v, *earlier):
    return lax.optimization_barrier((v,) + earlier)[0]


def gather_blocks(weights, n, make, inputs):
    if fits(n, weights.shape[1]):
        own = own_rows(weights)
        own_x = move(own, n, 2)
        first, third, second = (move(own, n, 8 * k) for k in (1, 3, 2))
        meanwhile = make(*once(inputs, own_x))
        one = jnp.stack([own, own_x])
        one = jnp.concatenate([one, move(one, n, 4)])
        one, first, meanwhile = lax.optimization_barrier((one, first, meanwhile))
        three = jnp.stack([first, move(first, n, 2)])
        two = jnp.stack([second, move(second, n, 4)])
        four = jnp.stack([third, move(third, n, 4)])
        two, three = lax.optimization_barrier((two, three))
        left = jnp.concatenate([one, two, move(two, n, 2)])
        right = jnp.concatenate([three, move(three, n, 4), four, move(four, n, 2)])
        return [left, move(left, n, 1), right, move(right, n, 1)], meanwhile
    flat = lax.all_gather(weights.astype(BF), "dp", axis=0, tiled=True).reshape(32, -1)
    blocks = jnp.pad(flat, ((0, 0), (0, BLK * 128 - flat.shape[1]))).reshape(4, 2, 2, 2, BLK, 128)
    groups = []
    for core, layers in GROUPS:
        v = blocks[:, :, :, core]
        both = [v[layers[0]], v[layers[1]].transpose(1, 0, 2, 3)]
        groups.append(jnp.stack(both).reshape(8, BLK, 128))
    return groups, make(*inputs)


def add(a, b):
    return (a.astype(F32) + b.astype(F32)).astype(BF)


def fold_core_kernel(keep, come, ak, asend, bk, bsend):
    for j in range(4):
        for k in range(4):
            v = add(keep[j, k], come[j, k])
            (ak, asend)[j & 1][j >> 1, k] = v[:HALF]
            (bk, bsend)[j >> 1][j & 1, k] = v[HALF:]


def fold_core(keep, come):
    part = here((2, 4, HALF, 128), BF)
    return kernel_call(fold_core_kernel, [part] * 4, "vv", mb=16, name="fold_core", us=2.0)(keep, come)


def fold_first_kernel(keep, come, ak, asend, b):
    v = [add(keep[x], come[x]) for x in (0, 1)]
    ak[...] = v[0][:HALF]
    asend[...] = v[1][:HALF]
    for x in (0, 1):
        b[x] = v[x][HALF:]


def fold_first(keep, come):
    outs = [shape((HALF, 128), BF), shape((HALF, 128), BF), shape((2, HALF, 128), BF)]
    return kernel_call(fold_first_kernel, outs, "vv", name="fold_first", us=0.6)(keep, come)


def fold_plane_kernel(me, ak, acome, bk, bcome, fak, facome, fb, fbcome, ak2, asend2, bk2, bsend2):
    z, y = me[0] >> 3, (me[0] >> 2) & 1
    for i, (a, b) in enumerate(((ak2, bk2), (asend2, bsend2))):
        for k in range(4):
            a[k] = add(ak[i, k], acome[i, k])
            b[k] = add(bk[i, k], bcome[i, k])

        @pl.when(y == i)
        def _():
            a[z] = add(a[z], add(fak[...], facome[...]))

        @pl.when(y == 0)
        def _():
            b[z] = add(b[z], add(fb[i], fbcome[i]))


def fold_plane(me, *args):
    part = here((4, HALF, 128), BF)
    return kernel_call(fold_plane_kernel, [part] * 4, "s" + "v" * 8, name="fold_plane", us=1.0)(me, *args)


def fold_layers_kernel(ak, acome, bk, bcome, *outs):
    for k, out in enumerate(outs):
        out[0:HALF] = add(ak[k], acome[k])
        out[HALF:] = add(bk[k], bcome[k])


def fold_layers(*args):
    return kernel_call(fold_layers_kernel, [shape((BLK, 128), BF)] * 4, "vvvv", name="fold_layers", us=0.6)(*args)


def to_rows(even, odd):
    return jnp.concatenate([even[:, :794], odd[:, :795]], axis=1).reshape(-1, 128)


def own_kernel(me, v0, v1, v2, v3, gbi, gbs, gbp, gbo, loss, rowm, grad, last):
    g = (v0[...].astype(F32) + v1[...].astype(F32)) + (v2[...].astype(F32) + v3[...].astype(F32))
    grad[0:BLK, :] = g
    grad[BLK:, :] = jnp.zeros((8, 128), F32)
    row = lax.broadcasted_iota(jnp.int32, (BLK, 128), 0)
    lane = lax.broadcasted_iota(jnp.int32, (BLK, 128), 1)
    place = 128 * row + lane - 64 * (me[0] & 1)
    mine = jnp.where((place >= 0) & (place < 64 * CHIP), g, 0.0)
    square = jnp.sum(jnp.sum(mine * mine, axis=0, keepdims=True), axis=1, keepdims=True)
    weight = jnp.sum(rowm[:, 1:2], axis=0, keepdims=True)
    at_row = 0
    for src, line, count in ((gbi, 4, 12), (gbs, 0, 12), (gbp, 0, 2), (gbo, 0, 47)):
        for j in range(count):
            last[at_row : at_row + 1, :] = src[line : line + 1, 128 * j : 128 * j + 128]
            at_row = at_row + 1
    lane = lax.broadcasted_iota(jnp.int32, (1, 128), 1)
    extra = jnp.where(lane == 0, square, jnp.where(lane == 1, loss[0:1, :], jnp.where(lane == 2, weight, 0.0)))
    last[at_row : at_row + 1, :] = extra
    last[at_row + 1 :, :] = jnp.zeros((80 - at_row - 1, 128), F32)


def own_sums(me, *args):
    return kernel_call(
        own_kernel,
        [here((BLK + 8, 128)), shape((80, 128))],
        "s" + "v" * 10,
        name="own_sums",
        us=1.0,
    )(me, *args)


def adam(value, grad, first, second, decay):
    first = beta_one * first + (1.0 - beta_one) * grad
    second = beta_two * second + (1.0 - beta_two) * grad * grad
    first_hat = first * (1.0 / (1.0 - beta_one**STEP))
    second_hat = second * (1.0 / (1.0 - beta_two**STEP))
    value = value - learn_rate * (first_hat / (jnp.sqrt(second_hat) + adam_eps) + decay * value)
    return (value, first, second)


def update_kernel(me, last, grad, w, m, v, b, bm, bv, nw, nm, nv, nb, nbm, nbv, loss, weight, norm):
    rows = NBIAS // 128
    total = last[0:rows, :]
    squares = jnp.sum(jnp.sum(total * total, axis=0, keepdims=True), axis=1, keepdims=True)
    size = jnp.sqrt(squares + last[rows : rows + 1, 0:1])
    scale = jnp.minimum(1.0, clip_norm / size)
    norm[0, 0] = jnp.sum(size)
    loss[0, 0] = jnp.sum(last[rows : rows + 1, 1:2])
    weight[0, 0] = jnp.sum(last[rows : rows + 1, 2:3])
    odd = (me[0] & 1) == 1

    def weights(start, count):
        cols = pl.ds(start, 128 * count)
        row = start // 128
        low = grad[pl.ds(row, count), :]
        high = grad[pl.ds(row + 1, count), :]
        lane = lax.broadcasted_iota(jnp.int32, (count, 128), 1)
        turned = jnp.where(lane < 64, pltpu.roll(low, 64, 1), pltpu.roll(high, 64, 1))
        g = jnp.where(odd, turned, low) * scale
        load = lambda ref: ref[0:1, cols].reshape(count, 128)
        for ref, out in zip((nw, nm, nv), adam(load(w), g, load(m), load(v), decay_rate)):
            ref[0:1, cols] = out.reshape(1, 128 * count)

    wide = 72
    whole = w.shape[1] // 128
    for row in range(0, whole // 8 * 8, wide):
        weights(128 * row, min(wide, whole // 8 * 8 - row))
    for row in range(whole // 8 * 8, whole):
        weights(128 * row, 1)
    cols = slice(128 * whole, 128 * whole + 64)
    low, high = grad[whole : whole + 1, :], grad[whole + 1 : whole + 2, :]
    g = jnp.where(odd, pltpu.roll(low, 64, 1), low)[:, 0:64] * scale
    for ref, out in zip((nw, nm, nv), adam(w[0:1, cols], g, m[0:1, cols], v[0:1, cols], decay_rate)):
        ref[0:1, cols] = out
    for row in range(0, rows, 8):
        count = min(8, rows - row)
        cols = slice(128 * row, 128 * (row + count))
        load = lambda ref: ref[cols].reshape(count, 128)
        for ref, out in zip((nb, nbm, nbv), adam(load(b), total[row : row + count] * scale, load(bm), load(bv), 0.0)):
            ref[cols] = out.reshape(128 * count)


def update(me, last, grad, w, m, v, b, bm, bv):
    one = jax.ShapeDtypeStruct((1, 1), F32)
    return pl.pallas_call(
        update_kernel,
        out_shape=(shape(w.shape),) * 3 + (shape(b.shape),) * 3 + (one,) * 3,
        in_specs=[SM] + [VM] * 8,
        out_specs=(VM,) * 6 + (SM,) * 3,
        compiler_params=params(12),
        name="update",
    )(me, last, grad, w, m, v, b, bm, bv)


def adam_all(last, grad, w, m, v, b, bm, bv):
    total = last[: NBIAS // 128].reshape(-1)
    squares, loss_sum, loss_weight = (last[NBIAS // 128, k] for k in range(3))
    norm = jnp.sqrt(squares + jnp.sum(total * total))
    scale = jnp.minimum(jnp.float32(1.0), clip_norm / norm)
    new = adam(w, (grad * scale)[None], m, v, decay_rate) + adam(b, total * scale, bm, bv, 0.0)
    return (*new, loss_sum, loss_weight, norm)


def prepare_kernel(feats, ivecs, meta, spl, spl_t, rowm, rows, ivs):
    rows[...] = jnp.zeros_like(rows)
    frames = feats[...].astype(F32)
    columns = meta[...].T
    rowm[...] = jnp.zeros_like(rowm)
    first = 0
    for start, length in zip(START, SPAN):
        rows[8 + start : 8 + start + length, 0:FEAT] = frames[first : first + length]
        rowm[start : start + length, :] = columns[first : first + length]
        first = first + length
    ivs[...] = jnp.zeros_like(ivs)
    ivs[0:4, 0:IVEC] = ivecs[...].astype(F32)
    row = lax.broadcasted_iota(jnp.int32, (ROWS, 128), 0)
    lane = lax.broadcasted_iota(jnp.int32, (ROWS, 128), 1)
    iv = ivs[3:4, :]
    for k in (2, 1, 0):
        iv = jnp.where(row < START[k + 1], ivs[k : k + 1, :], iv)
    left = rows[7 : 7 + ROWS, :]
    left = jnp.where(lane < FEAT, left, pltpu.roll(rows[8 : 8 + ROWS, :], FEAT, 1))
    left = jnp.where(lane < 2 * FEAT, left, pltpu.roll(rows[9 : 9 + ROWS, :], 2 * FEAT, 1))
    left = jnp.where(lane < 3 * FEAT, left, pltpu.roll(iv, 3 * FEAT, 1))
    ones = 3 * FEAT + IVEC - 128
    right = jnp.where(lane < ones, pltpu.roll(iv, 3 * FEAT, 1), jnp.where(lane == ones, 1.0, 0.0))
    spl[:, 0:128] = left.astype(BF)
    spl[:, 128:256] = right.astype(BF)
    spl_t[0:128, :] = left.T.astype(BF)
    spl_t[128:256, :] = right.T.astype(BF)


def prepare(features, ivectors, frame_mask, labels, confidence):
    mask = frame_mask.astype(F32)
    meta = jnp.stack([mask, confidence * mask, jnp.ones_like(mask), labels.astype(F32)])
    meta = jnp.pad(meta, ((0, 4), (0, ROWS - mask.shape[0])))
    return kernel_call(
        prepare_kernel,
        [shape((ROWS, 256), BF), shape((256, ROWS), BF), shape((ROWS, 8))],
        "vvv",
        [vmem((ROWS + 16, 128)), vmem((8, 128))],
        name="prepare",
        us=2.0,
    )(features, ivectors, meta)


def on_device(
    features,
    ivectors,
    frame_mask,
    labels,
    confidence,
    weights,
    first_moment,
    second_moment,
    biases,
    bias_first,
    bias_second,
):
    n = lax.axis_size("dp")
    size = weights.shape[1]
    index = lax.axis_index("dp")
    fast = fits(n, size)
    me = index if fast else jnp.int32(0)
    place = me.reshape(1)
    blocks, (spliced, spl_t, rowm) = gather_blocks(
        weights, n, prepare, (features, ivectors, frame_mask, labels, confidence)
    )
    bias = biases[None]
    w_in = unpack_in(place, blocks)
    h1, gp1, st = layer_in(spliced, w_in, bias, rowm)
    if fast:
        tot1 = sum_core(st, n)
        w1a, w1b, w2a, w2b = unpack_mid(place, once(blocks, tot1))
        tot1 = sum_layers(tot1, n)
        tot1, w1a = lax.optimization_barrier((tot1, w1a))
        flat_out = flatten_out(place, once(blocks, tot1), 12, SPLIT - 1)
        tot1 = sum_plane(tot1, n)
        tot1, flat_out = lax.optimization_barrier((tot1, flat_out))
    else:
        tot1 = total(st, n)
        w1a, w1b, w2a, w2b = unpack_mid(place, blocks)
        flat_out = flatten_out(place, blocks, 12, SPLIT - 1)
        flat_two = flatten_out(place, blocks, SPLIT, 31)
    rounded, fac, fnext, h2, gp2, st = layer_mid(h1, tot1, w1a, w1b, w2a, w2b, bias, rowm)
    if fast:
        tot2 = sum_core(st, n)
        flat_two = flatten_out(place, once(blocks, tot2), SPLIT, 31)
        tot2 = sum_layers(tot2, n)
        tot2, flat_two = lax.optimization_barrier((tot2, flat_two))
        w_pre, w_out = unpack_out(flat_out, once(flat_two, tot2), h2)
        tot2 = sum_plane(tot2, n)
        tot2, w_pre = lax.optimization_barrier((tot2, w_pre))
    else:
        tot2 = total(st, n)
        w_pre, w_out = unpack_out(flat_out, flat_two, h2)
    summed, n2b, dpre, dsum, go, gbo, st, loss, pre = head(h1, tot1, h2, tot2, w_pre, w_out, bias, rowm)
    tot3 = sum_layers(sum_core(st, n), n) if fast else total(st, n)
    keep, send, edge, gbp = side_out(place, *once((summed, dpre, go), tot3))
    if fast:
        tot3 = sum_plane(tot3, n)
        tot3, keep = lax.optimization_barrier((tot3, keep))
    dact, dfac, dfnext, dn, st = back_mid(rounded, tot1, n2b, gp2, tot2, dsum, tot3, w1a, w1b, w2a, w2b, rowm)
    parts = (edge, fac, fnext, dact, rounded, dfac, dfnext, dn)
    if fast:
        tot4 = sum_core(st, n)
        keep, send, gbs = side_mid(place, keep, send, *once(parts, tot4))
        keep, send, tot4 = lax.optimization_barrier((keep, send, tot4))
        blocks = fold_core(keep, move(send, n, 1))
        tot4, blocks = lax.optimization_barrier((sum_plane(tot4, n), blocks))
        tot4 = sum_layers(tot4, n)
        a_keep, a_send, b_keep, b_send = blocks
        a_come, b_come = move(a_send, n, 2), move(b_send, n, 4)
    else:
        tot4 = total(st, n)
        keep, send, gbs = side_mid(place, keep, send, *parts)
    keep_in, send_in, gbi = back_in(place, rounded, gp1, tot1, dn, tot4, spl_t, rowm)
    if fast:
        first = fold_first(keep_in, move(send_in, n, 1))
        first = list(first)
        a_come, first[1] = lax.optimization_barrier((a_come, first[1]))
        first_keep, first_send, first_b = first
        first_a = (first_keep, move(first_send, n, 2))
        first_b = (first_b, move(first_b, n, 4, lambda t: (t & 4) == 0))
        a_keep, a_send, b_keep, b_send = fold_plane(place, a_keep, a_come, b_keep, b_come, *first_a, *first_b)
        parts = fold_layers(a_keep, move(a_send, n, 4), b_keep, move(b_send, n, 2))
        pre = once(pre, parts[0])
        parts = [parts[0]] + [move(parts[k], n, 8 * k) for k in (1, 2, 3)]
        loss = loss - picked_sum(pre, w_out, bias, rowm)
        grad, last = own_sums(place, *parts, gbi, gbs, gbp, gbo, loss, rowm)
        *new, loss_sum, loss_weight, norm = update(
            place, total(last, n), grad, weights, first_moment, second_moment, biases, bias_first, bias_second
        )
        return (*new, loss_sum.reshape(()), loss_weight.reshape(()), norm.reshape(()))
    in_order = lambda v: v.transpose(1, 0, 2, 3).reshape(16, BLK, 128)
    loss = loss - picked_sum(pre, w_out, bias, rowm)
    rows = to_rows(in_order(keep), in_order(send))
    rows = jnp.concatenate([rows[: 2 * CHIP] + to_rows(keep_in, send_in), rows[2 * CHIP :]], axis=0)
    grad = lax.psum_scatter(rows.astype(F32).reshape(n, size), "dp", scatter_dimension=0, tiled=True).reshape(-1)
    bias_grad = jnp.concatenate([gbi[4], gbs[0], gbp[0], gbo[0, :SEN]])
    extra = jnp.stack([jnp.sum(grad * grad), loss[0, 0], jnp.sum(rowm[:, 1])])
    last = total(jnp.concatenate([bias_grad, jnp.pad(extra, (0, 7 * 128 - 3))]).reshape(80, 128), n)
    return adam_all(last, grad, weights, first_moment, second_moment, biases, bias_first, bias_second)


def solution(mesh):
    return jax.shard_map(
        on_device,
        mesh=mesh,
        in_specs=(
            P("dp", None),
            P("dp", None),
            P("dp"),
            P("dp"),
            P("dp"),
            P("dp", None),
            P("dp", None),
            P("dp", None),
            P(),
            P(),
            P(),
        ),
        out_specs=(P("dp", None), P("dp", None), P("dp", None), P(), P(), P(), P(), P(), P()),
        check_vma=False,
    )
```

```python
import functools
import math

import jax
import jax.numpy as jnp
from jax import lax
from jax.experimental import pallas as pl
from jax.experimental.pallas import tpu as pltpu
from jax.sharding import PartitionSpec as P

FEAT = 40
IVEC = 100
HID = 1536
BOT = 160
PRE = 256
SEN = 6016
SPAN = (140, 140, 150, 300)
START = (0, 144, 288, 448)
ROWS = 768
SEGS = ((0, 288), (288, 448), (448, 768))
SENP = 6144
STEP = 10
NBIAS = 9344

bypass_scale = 0.66
norm_eps = 0.001
learn_rate = 0.05
beta_one = 0.9
beta_two = 0.999
adam_eps = 1e-08
decay_rate = 0.01
clip_norm = 1.0

F32 = jnp.float32
BF = jnp.bfloat16
VM = pl.BlockSpec(memory_space=pltpu.VMEM)
SM = pl.BlockSpec(memory_space=pltpu.SMEM)
HB = pl.BlockSpec(memory_space=pltpu.HBM)

CHIP = 1589
BLK = 800
GROUPS = ((0, (0, 2)), (1, (0, 2)), (0, (1, 3)), (1, (1, 3)))
OFF = (0, 2640, 6480, 10320, 13392)
ROWS_ALL = 16 * CHIP
TILE = 256
NT = HID // TILE
WIDE = 1024
NW = SENP // WIDE
FLAT = ROWS_ALL + 64
FROM = 2376
HALF = BLK // 2
BIG = 512
NB = HID // BIG
GELU_C = math.sqrt(2.0 / math.pi)


def shape(dims, kind=F32):
    return jax.ShapeDtypeStruct(dims, kind)


def params(mb):
    return pltpu.CompilerParams(vmem_limit_bytes=mb * 2**20)


def here(dims, kind=F32):
    return pltpu.VMEM(dims, kind)


def kernel_call(body, outs, ins, scratch=(), mb=12, name=None, us=1.0):
    spec = {"s": SM, "v": VM, "n": VM, "h": HB}
    call = pl.pallas_call(
        body,
        out_shape=tuple(outs),
        in_specs=[spec[k] for k in ins],
        out_specs=tuple(VM for _ in outs),
        scratch_shapes=list(scratch),
        compiler_params=params(mb),
        cost_estimate=pl.CostEstimate(flops=int(us * 1e9), bytes_accessed=int(us * 3e6), transcendentals=0),
        name=name,
    )
    return lambda *args: call(
        *(pltpu.with_memory_space_constraint(v, pltpu.VMEM) if k == "n" else v for k, v in zip(ins, args))
    )


def sems(n):
    return pltpu.SemaphoreType.DMA((n,))


def vmem(dims, kind=F32):
    return pltpu.VMEM(dims, kind)


def dot(a, b):
    return jnp.dot(a, b, preferred_element_type=F32)


def dot_nt(a, b):
    return lax.dot_general(a, b, (((1,), (1,)), ((), ())), preferred_element_type=F32)


def at(j, size):
    return slice(j * size, (j + 1) * size)


def unrolled(count):
    def run(body):
        for j in range(count):
            body(j)

    return run


def block_row(d):
    return (d >> 1) * CHIP + (d & 1) * 794


def own_rows_kernel(w, out, lines):
    whole = w.shape[1] // 128
    lines[whole:, :] = jnp.zeros((BLK - whole, 128), F32)
    for row in range(0, whole // 8 * 8, 72):
        count = min(72, whole // 8 * 8 - row)
        lines[row : row + count, :] = w[0:1, 128 * row : 128 * (row + count)].reshape(count, 128)
    for row in range(whole // 8 * 8, whole):
        lines[row : row + 1, :] = w[0:1, 128 * row : 128 * row + 128]
    lines[whole : whole + 1, 0:64] = w[0:1, 128 * whole :]
    out[...] = lines[...].astype(BF)


def own_rows(weights):
    return kernel_call(own_rows_kernel, [shape((BLK, 128), BF)], "v", [vmem((BLK, 128))], name="own_rows", us=1.0)(weights)[0]


def put_block(flat, d, v, start=0):
    first = block_row(d) - start
    v = v.astype(F32)
    if d % 2:
        v = pltpu.roll(v, 64, 1)
        low = lax.broadcasted_iota(jnp.int32, v.shape, 1) < 64
        flat[first : first + 1, :] = jnp.where(low[0:1], flat[first : first + 1, :], v[0:1])
        flat[first + 1 : first + 795, :] = jnp.where(low[:794], v[0:794], v[1:795])
    else:
        flat[first : first + 795, :] = v[:795]


def fetch_blocks(me, groups, first, last, stage, sem):
    for src, (core, layers) in zip(groups, GROUPS):
        for i in range(8):
            low, high = i & 1, (i >> 1) & 1
            x, y = (low, high) if i < 4 else (high, low)
            d = me[0] ^ (8 * layers[i // 4] + 4 * y + 2 * x + core)

            @pl.when((d >= first) & (d <= last))
            def _():
                pltpu.make_async_copy(src.at[i], stage.at[d - first], sem.at[d - first]).start()


def block_ready(src, d, stage, sem):
    pltpu.make_async_copy(src.at[0], stage.at[d], sem.at[d]).wait()


def unpack_in_kernel(me, g0, g1, g2, g3, win, stage, flat, sem):
    fetch_blocks(me, (g0, g1, g2, g3), 0, 3, stage, sem)
    for d in range(4):
        block_ready(g0, d, stage, sem)
        put_block(flat, d, stage[d])
    for j in range(12):
        v = flat[pl.ds(j, 224, stride=12), :]
        v = jnp.where(lax.broadcasted_iota(jnp.int32, (224, 128), 0) < 220, v, 0.0)
        win[0:224, 128 * j : 128 * j + 128] = v.astype(BF)
    win[224:256, :] = jnp.zeros((32, HID), BF)


def unpack_in(me, groups):
    return kernel_call(
        unpack_in_kernel,
        [here((256, HID), BF)],
        "shhhh",
        [vmem((4, BLK, 128), BF), vmem((2 * CHIP + 14, 128)), sems(4)],
        name="unpack_in",
        us=1.5,
    )(me, *groups)[0]


def unpack_mid_kernel(me, g0, g1, g2, g3, w1a, w1b, w2a, w2b, stage, flat, tall, tall2, sem):
    fetch_blocks(me, (g0, g1, g2, g3), 2, 12, stage, sem)
    start = block_row(2)
    first, second = OFF[1] - start, OFF[2] - start
    for d in range(2, 13):
        block_ready(g0, d - 2, stage, sem)
        put_block(flat, d, stage[d - 2], start)
    lane = lax.broadcasted_iota(jnp.int32, (768, 128), 1)
    a = [flat[pl.ds(first + q, 768, stride=5), :] for q in range(5)]

    def put(r, t0, t1):
        tall[pl.ds(r, 768, stride=4), :] = t0
        tall2[pl.ds(r, 768, stride=4), :] = jnp.where(lane < 32, t1, 0.0)

    put(0, a[0], a[1])
    for r in (1, 2, 3):
        turn = 128 - 32 * r
        low = pltpu.roll(a[r], turn, 1)
        high = pltpu.roll(a[r + 1], turn, 1)
        put(r, jnp.where(lane < turn, low, high), high)
    for out, row in ((w1a, 0), (w1b, 1536)):
        out[:, 0:128] = tall[row : row + 1536, :].astype(BF)
        out[:, 128:256] = tall2[row : row + 1536, :].astype(BF)
    for j in range(12):
        v = flat[pl.ds(second + j, 320, stride=12), :].astype(BF)
        w2a[0:160, 128 * j : 128 * j + 128] = v[:160]
        w2b[0:160, 128 * j : 128 * j + 128] = v[160:]
    w2a[160:256, :] = jnp.zeros((96, HID), BF)
    w2b[160:256, :] = jnp.zeros((96, HID), BF)


def unpack_mid(me, groups):
    return kernel_call(
        unpack_mid_kernel,
        [here((HID, 256), BF)] * 2 + [here((256, HID), BF)] * 2,
        "shhhh",
        [
            vmem((11, BLK, 128), BF),
            vmem((6 * CHIP, 128)),
            vmem((3072, 128)),
            vmem((3072, 128)),
            sems(11),
        ],
        mb=15,
        name="unpack_mid",
        us=5.2,
    )(me, *groups)


SPLIT = 22


def flatten_out_kernel(first, last, me, g0, g1, g2, g3, flat, stage, sem):
    fetch_blocks(me, (g0, g1, g2, g3), first, last, stage, sem)
    for d in range(first, last + 1):
        block_ready(g0, d - first, stage, sem)
        put_block(flat, d, stage[d - first], block_row(first))


def flatten_out(me, groups, first, last):
    count = last + 1 - first
    return kernel_call(
        functools.partial(flatten_out_kernel, first, last),
        [here((CHIP * count // 2, 128))],
        "shhhh",
        [vmem((count, BLK, 128), BF), sems(count)],
        name="flatten_out",
        us=3.0,
    )(me, *groups)[0]


def unpack_out_kernel(one, two, _, wp, wo, flat):
    pre, out = OFF[3] - block_row(12), OFF[4] - block_row(12)
    flat[0 : one.shape[0], :] = one[...]
    flat[one.shape[0] :, :] = two[...]
    for j in range(2):
        wp[:, 128 * j : 128 * j + 128] = flat[pl.ds(pre + j, 1536, stride=2), :].astype(BF)
    for j in range(47):
        wo[:, 128 * j : 128 * j + 128] = flat[pl.ds(out + j, 256, stride=47), :].astype(BF)
    wo[:, 6016:] = jnp.zeros((256, 128), BF)


def unpack_out(one, two, h2):
    return kernel_call(
        unpack_out_kernel,
        [here((HID, PRE), BF), here((PRE, SENP), BF)],
        "nnn",
        [vmem((10 * CHIP, 128))],
        mb=14,
        name="unpack_out",
        us=3.0,
    )(one, two, h2)


def put_columns(flat, first, grad, rows, width):
    for j in range(width // 128):
        flat[pl.ds(first + j, rows, stride=width // 128), :] = grad(128 * j)


def put_first(flat, first, tall, tall2):
    lane = lax.broadcasted_iota(jnp.int32, (768, 128), 1)
    t0 = [tall[pl.ds(r, 768, stride=4), :] for r in range(4)]
    t1 = [tall2[pl.ds(r, 768, stride=4), :] for r in range(4)]
    flat[pl.ds(first, 768, stride=5), :] = t0[0]
    for q in (1, 2, 3):
        shift = 32 * (q - 1)
        tail = t1[0]
        if q > 1:
            tail = jnp.where(lane < shift, pltpu.roll(t0[q - 1], shift, 1), pltpu.roll(t1[q - 1], shift, 1))
        flat[pl.ds(first + q, 768, stride=5), :] = jnp.where(lane < 32 * q, tail, pltpu.roll(t0[q], 32 * q, 1))
    flat[pl.ds(first + 4, 768, stride=5), :] = jnp.where(
        lane < 96, pltpu.roll(t0[3], 96, 1), pltpu.roll(t1[3], 96, 1)
    )


def gelu_parts(act):
    square = act * act
    t = jnp.tanh(GELU_C * act * (1.0 + 0.044715 * square))
    cdf = 0.5 + 0.5 * t
    slope = cdf + (0.5 * act) * (1.0 - t * t) * (GELU_C + (3 * 0.044715 * GELU_C) * square)
    return act * cdf, slope


def put_sums(st, first, v):
    for s, (a, b) in enumerate(SEGS):
        st[first + s : first + s + 1, :] = jnp.sum(v[a:b], axis=0, keepdims=True)


def norm_rows(tot, s, cols):
    count = tot[6:7, s : s + 1]
    mean = tot[s : s + 1, cols] / count
    var = tot[3 + s : 4 + s, cols] / count - mean * mean
    return mean, lax.rsqrt(var + norm_eps)


def put_stats(st, cols, hidden, mask):
    masked = hidden * mask
    square = masked * hidden
    for s, (a, b) in enumerate(SEGS):
        st[s : s + 1, cols] = jnp.sum(masked[a:b], axis=0, keepdims=True)
        st[3 + s : 4 + s, cols] = jnp.sum(square[a:b], axis=0, keepdims=True)


def put_counts(st, mask):
    lane = lax.broadcasted_iota(jnp.int32, (2, HID), 1)
    counts = [jnp.sum(mask[a:b], axis=0, keepdims=True) for a, b in SEGS]
    st[6:8, :] = jnp.where(lane == 0, counts[0], jnp.where(lane == 1, counts[1], counts[2]))


def put_grads(st, cols, s, grad, normed):
    st[s : s + 1, cols] = jnp.sum(grad, axis=0, keepdims=True)
    st[3 + s : 4 + s, cols] = jnp.sum(grad * normed, axis=0, keepdims=True)


def in_kernel(spl, w, b, rowm, h, gp, st):
    mask = rowm[:, 0:1]

    @unrolled(NB)
    def _(j):
        cols = at(j, BIG)
        hidden, slope = gelu_parts(dot(spl[...], w[:, cols]) + b[:, cols])
        h[:, cols] = hidden
        gp[:, cols] = slope.astype(BF)
        put_stats(st, cols, hidden, mask)

    put_counts(st, mask)


def layer_in(spliced, w_in, b_in, rowm):
    return kernel_call(
        in_kernel,
        [here((ROWS, HID)), here((ROWS, HID), BF), shape((8, HID))],
        "vnvv",
        name="layer_in",
        us=4.1,
    )(spliced, w_in, b_in, rowm)


def mid_kernel(h, tot, w1a, w1b, w2a, w2b, bias, rowm, rounded, fac, fnext, h2, gp2, st):
    valid = rowm[:, 2:3]
    mask = rowm[:, 0:1]

    @unrolled(NT)
    def _(j):
        cols = at(j, TILE)
        for s, (a, b) in enumerate(SEGS):
            mean, scale = norm_rows(tot, s, cols)
            rounded[a:b, cols] = ((h[a:b, cols] - mean) * scale).astype(BF)

    ua = dot(rounded[...], w1a[...])
    ub = dot(rounded[...], w1b[...])
    f = ((ub + pltpu.roll(ua * valid, 1, 0)) * valid).astype(BF)
    fac[...] = f
    fnext[...] = (pltpu.roll(f.astype(F32), ROWS - 1, 0) * valid).astype(BF)

    @unrolled(NB)
    def _(j):
        cols = at(j, BIG)
        act = dot(fac[...], w2a[:, cols]) + dot(fnext[...], w2b[:, cols]) + bias[:, at(j + HID // BIG, BIG)]
        hidden, slope = gelu_parts(act)
        h2[:, cols] = hidden
        gp2[:, cols] = slope.astype(BF)
        put_stats(st, cols, hidden, mask)

    put_counts(st, mask)


def layer_mid(h, tot, w1a, w1b, w2a, w2b, bias, rowm):
    return kernel_call(
        mid_kernel,
        [
            here((ROWS, HID), BF),
            here((ROWS, 256), BF),
            here((ROWS, 256), BF),
            here((ROWS, HID)),
            here((ROWS, HID), BF),
            shape((8, HID)),
        ],
        "nvnnnnvv",
        name="layer_mid",
        us=7.4,
    )(h, tot, w1a, w1b, w2a, w2b, bias, rowm)


def head_kernel(
    h1, tot1, h2, tot2, wp, wo, bias, rowm, summed, n2b, dpre, dsum, go, gb, st, loss, pre_out, acc
):
    @unrolled(NT)
    def _(j):
        cols = at(j, TILE)
        for s, (a, b) in enumerate(SEGS):
            mean1, scale1 = norm_rows(tot1, s, cols)
            mean2, scale2 = norm_rows(tot2, s, cols)
            n1 = (h1[a:b, cols] - mean1) * scale1
            n2 = (h2[a:b, cols] - mean2) * scale2
            summed[a:b, cols] = (n2 + bypass_scale * n1).astype(BF)
            n2b[a:b, cols] = n2.astype(BF)

    pre = (dot(summed[...], wp[...]) + bias[:, 2 * HID : 2 * HID + PRE]).astype(BF)
    lane = lax.broadcasted_iota(jnp.int32, (ROWS, 128), 1)
    where = rowm[:, 3:4].astype(jnp.int32) - lane
    weight = rowm[:, 1:2]

    bo = jnp.concatenate([bias[:, 2 * HID + PRE :], jnp.full((1, SENP - SEN), -1e30, F32)], axis=1)

    m = jnp.full((ROWS, 128), -1e30, F32)
    total = jnp.zeros((ROWS, 128), F32)
    for j in range(NW):
        cols = slice(WIDE * j, WIDE * j + WIDE)
        v = dot(pre, wo[:, cols]) + bo[:, cols]
        parts = [v[:, 128 * q : 128 * q + 128] for q in range(WIDE // 128)]
        old = m
        for p in parts:
            m = jnp.maximum(m, p)
        total = total * jnp.exp(old - m)
        for p in parts:
            total = total + jnp.exp(p - m)

    top = jnp.max(m, axis=1, keepdims=True)
    total = jnp.sum(total * jnp.exp(m - top), axis=1, keepdims=True)
    lse = jnp.log(total) + top
    less = lse - jnp.log(weight)
    acc[...] = jnp.zeros_like(acc)
    pre_t = jnp.concatenate([pre.astype(F32).T.astype(BF), jnp.ones((16, ROWS), BF)], axis=0)
    for j in range(NW):
        cols = slice(WIDE * j, WIDE * j + WIDE)
        v = dot(pre, wo[:, cols]) + bo[:, cols]
        parts = []
        for q in range(WIDE // 128):
            p = v[:, 128 * q : 128 * q + 128]
            hit = jnp.where(where == j * WIDE + 128 * q, weight, 0.0)
            parts.append((jnp.exp(p - less) - hit).astype(BF))
        d = jnp.concatenate(parts, axis=1)
        acc[...] += dot_nt(d, wo[:, cols])
        g = dot(pre_t, d)
        go[:, cols] = g[0:PRE].astype(BF)
        gb[:, cols] = g[PRE : PRE + 8]

    entropy = jnp.sum(weight * lse, axis=0, keepdims=True)
    loss[...] = jnp.zeros((8, 128), F32) + entropy
    pre_out[...] = pre
    dp = acc[...].astype(BF)
    dpre[...] = dp

    @unrolled(NT)
    def _(j):
        cols = at(j, TILE)
        ds = dot_nt(dp, wp[cols, :])
        dsum[:, cols] = ds
        for s, (a, b) in enumerate(SEGS):
            put_grads(st, cols, s, ds[a:b], n2b[a:b, cols].astype(F32))

    st[6:8, :] = jnp.zeros((2, HID), F32)


def head(h1, tot1, h2, tot2, wp, wo, bias, rowm):
    return kernel_call(
        head_kernel,
        [
            here((ROWS, HID), BF),
            here((ROWS, HID), BF),
            here((ROWS, PRE), BF),
            here((ROWS, HID)),
            here((PRE, SENP), BF),
            shape((8, SENP)),
            shape((8, HID)),
            shape((8, 128)),
            shape((ROWS, PRE), BF),
        ],
        "nvnvnnvv",
        [
            vmem((ROWS, PRE)),
        ],
        mb=14,
        name="head",
        us=20.0,
    )(h1, tot1, h2, tot2, wp, wo, bias, rowm)


def picked_kernel(pre, wo, bias, rowm, out):
    lane = lax.broadcasted_iota(jnp.int32, (ROWS, 128), 1)
    where = rowm[:, 3:4].astype(jnp.int32) - lane
    weight = rowm[:, 1:2]
    bo = jnp.concatenate([bias[:, 2 * HID + PRE :], jnp.zeros((1, SENP - SEN), F32)], axis=1)
    total = jnp.zeros((ROWS, 128), F32)
    for j in range(NW):
        cols = slice(WIDE * j, WIDE * j + WIDE)
        v = dot(pre[...], wo[:, cols]) + bo[:, cols]
        for q in range(WIDE // 128):
            total = total + jnp.where(where == j * WIDE + 128 * q, v[:, 128 * q : 128 * q + 128], 0.0)
    total = jnp.sum(total, axis=1, keepdims=True) * weight
    out[...] = jnp.zeros((8, 128), F32) + jnp.sum(total, axis=0, keepdims=True)


def picked_sum(pre, wo, bias, rowm):
    return kernel_call(picked_kernel, [shape((8, 128))], "vvvv", mb=14, name="picked_sum", us=5.0)(pre, wo, bias, rowm)[0]


def back_mid_kernel(
    n1b, tot1, n2b, gp2, tot2, dsum, tot3, w1a, w1b, w2a, w2b, rowm, dact, dfac, dfnext, dn, st
):
    valid = rowm[:, 2:3]

    @unrolled(NT)
    def _(j):
        cols = at(j, TILE)
        for s, (a, b) in enumerate(SEGS):
            mean, scale = norm_rows(tot2, s, cols)
            along = tot3[s : s + 1, cols]
            cross = tot3[3 + s : 4 + s, cols]
            part = rowm[a:b, 0:1] / tot1[6:7, s : s + 1]
            n2 = n2b[a:b, cols].astype(F32)
            back = scale * (dsum[a:b, cols] - part * (along + cross * n2))
            dact[a:b, cols] = (gp2[a:b, cols] * back).astype(BF)

    ua = dot_nt(dact[...], w2a[...])
    ub = dot_nt(dact[...], w2b[...])
    f = ((ua + pltpu.roll(ub, 1, 0)) * valid).astype(BF)
    dfac[...] = f
    dfnext[...] = (pltpu.roll(f.astype(F32), ROWS - 1, 0) * valid).astype(BF)

    @unrolled(NT)
    def _(j):
        cols = at(j, TILE)
        grad = bypass_scale * dsum[:, cols] + dot_nt(dfac[...], w1b[cols, :]) + dot_nt(dfnext[...], w1a[cols, :])
        dn[:, cols] = grad
        for s, (a, b) in enumerate(SEGS):
            put_grads(st, cols, s, grad[a:b], n1b[a:b, cols].astype(F32))

    st[6:8, :] = jnp.zeros((2, HID), F32)


def back_mid(n1b, tot1, n2b, gp2, tot2, dsum, tot3, w1a, w1b, w2a, w2b, rowm):
    return kernel_call(
        back_mid_kernel,
        [
            here((ROWS, HID), BF),
            here((ROWS, 256), BF),
            here((ROWS, 256), BF),
            here((ROWS, HID)),
            shape((8, HID)),
        ],
        "nvnnvnvnnnnv",
        name="back_mid",
        us=5.9,
    )(n1b, tot1, n2b, gp2, tot2, dsum, tot3, w1a, w1b, w2a, w2b, rowm)


def side_out_kernel(me, summed, dpre, go, keep, send, edge, gbp, flat):
    ones = jnp.ones((16, ROWS), BF)
    gbp[...] = dot(ones, dpre[...])[0:8]
    for j in range(NT):
        t = summed[:, TILE * j : TILE * j + TILE].astype(F32).T.astype(BF)
        g = dot(t, dpre[...])
        put_columns(flat, 2 * TILE * j, lambda c: g[:, c : c + 128], TILE, PRE)
    put_columns(flat, OFF[4] - OFF[3], lambda c: go[:, c : c + 128].astype(F32), PRE, SEN)
    flat[ROWS_ALL - OFF[3] :, :] = jnp.zeros((FLAT - ROWS_ALL, 128), F32)
    edge[...] = flat[0:16, :]
    for dc, out in ((0, keep), (1, send)):
        for k in range(4):
            for j in range(4):
                d = me[0] ^ (8 * k + 2 * j + dc)

                @pl.when(d > 12)
                def _():
                    out[j, k] = flat[pl.ds(block_row(d) - OFF[3], BLK), :].astype(BF)


def side_out(me, summed, dpre, go):
    return kernel_call(
        side_out_kernel,
        [here((4, 4, BLK, 128), BF), here((4, 4, BLK, 128), BF), shape((16, 128)), shape((8, PRE))],
        "snvn",
        [vmem((FLAT - OFF[3], 128))],
        mb=14,
        name="side_out",
        us=4.0,
    )(me, summed, dpre, go)


def side_mid_kernel(
    me, edge, fac, fnext, dact, rounded, dfac, dfnext, _, keep_in, send_in, keep, send, gbs, flat, tall, tall2
):
    fac_t = fac[...].astype(F32).T.astype(BF)
    next_t = fnext[...].astype(F32).T.astype(BF)
    ones = jnp.ones((16, ROWS), BF)
    flat[0 : OFF[1] - FROM, :] = jnp.zeros((OFF[1] - FROM, 128), F32)
    for j in range(NT):
        cols = slice(TILE * j, TILE * j + TILE)
        t = rounded[:, cols].astype(F32).T.astype(BF)
        for k, d in enumerate((dfnext, dfac)):
            g = dot(t, d[...])
            tall[HID * k + TILE * j : HID * k + TILE * j + TILE, :] = g[:, 0:128]
            tall2[HID * k + TILE * j : HID * k + TILE * j + TILE, :] = g[:, 128:256]
        for k, f in enumerate((fac_t, next_t)):
            g = dot(f, dact[:, cols])
            for q in range(TILE // 128):
                row = OFF[2] - FROM + 1920 * k + TILE // 128 * j + q
                flat[pl.ds(row, BOT, stride=12), :] = g[0:BOT, 128 * q : 128 * q + 128]
        gbs[:, cols] = dot(ones, dact[:, cols])[0:8]
    put_first(flat, OFF[1] - FROM, tall, tall2)
    flat[OFF[3] - FROM : OFF[3] - FROM + 16, :] = edge[...]
    flat[OFF[3] - FROM + 16 :, :] = jnp.zeros((7968 - (OFF[3] - FROM + 16), 128), F32)
    for dc, src, out in ((0, keep_in, keep), (1, send_in, send)):
        for k in range(4):
            for j in range(4):
                d = me[0] ^ (8 * k + 2 * j + dc)

                @pl.when(d > 12)
                def _():
                    out[j, k] = src[j, k]

                @pl.when((d > 2) & (d < 13))
                def _():
                    out[j, k] = flat[pl.ds(block_row(d) - FROM, BLK), :].astype(BF)

                @pl.when(d < 3)
                def _():
                    out[j, k] = jnp.zeros((BLK, 128), BF)


def side_mid(me, keep, send, *args):
    return kernel_call(
        side_mid_kernel,
        [here((4, 4, BLK, 128), BF), here((4, 4, BLK, 128), BF), shape((8, HID))],
        "svnnnnnnnnn",
        [vmem((7968, 128)), vmem((3072, 128)), vmem((3072, 128))],
        mb=14,
        name="side_mid",
        us=6.4,
    )(me, *args, keep, send)


def back_in_kernel(me, n1b, gp, tot1, dn, tot4, spl_t, rowm, keep, send, gb, d, flat):
    @unrolled(NT)
    def _(j):
        cols = at(j, TILE)
        for s, (a, b) in enumerate(SEGS):
            mean, scale = norm_rows(tot1, s, cols)
            along = tot4[s : s + 1, cols]
            cross = tot4[3 + s : 4 + s, cols]
            part = rowm[a:b, 0:1] / tot1[6:7, s : s + 1]
            n1 = n1b[a:b, cols].astype(F32)
            back = scale * (dn[a:b, cols] - part * (along + cross * n1))
            d[a:b, cols] = (gp[a:b, cols] * back).astype(BF)

    for j in range(NT):
        g = dot(spl_t[...], d[:, TILE * j : TILE * j + TILE])
        gb[:, TILE * j : TILE * j + TILE] = g[216:224]
        for q in range(TILE // 128):
            flat[pl.ds(TILE // 128 * j + q, 220, stride=12), :] = g[0:220, 128 * q : 128 * q + 128]
    flat[OFF[1] :, :] = jnp.zeros((2 * CHIP + 14 - OFF[1], 128), F32)
    for dc, out in ((0, keep), (1, send)):
        for dx in (0, 1):
            t = (me[0] & 3) ^ (2 * dx + dc)
            out[dx] = flat[pl.ds(block_row(t), BLK), :].astype(BF)


def back_in(me, n1b, gp, tot1, dn, tot4, spl_t, rowm):
    return kernel_call(
        back_in_kernel,
        [shape((2, BLK, 128), BF), shape((2, BLK, 128), BF), shape((8, HID))],
        "snnvnvvv",
        [vmem((ROWS, HID), BF), vmem((2 * CHIP + 14, 128))],
        name="back_in",
        us=2.8,
    )(me, n1b, gp, tot1, dn, tot4, spl_t, rowm)


def move(x, n, mask, to=None):
    return lax.ppermute(x, "dp", [(i, i ^ mask) for i in range(n) if to is None or to(i ^ mask)])


def exchange(x, n, masks):
    a, b, c = (move(x, n, k) for k in masks)
    return (x + a) + (b + c)


def sum_core(x, n):
    return x + move(x, n, 1)


def sum_layers(x, n):
    return exchange(x, n, (8, 16, 24))


def sum_plane(x, n):
    return exchange(x, n, (2, 4, 6))


def total(x, n):
    if n == 32:
        return sum_plane(sum_layers(sum_core(x, n), n), n)
    bit = 1
    while bit < n:
        x = x + move(x, n, bit)
        bit = 2 * bit
    return x


def fits(n, shard):
    return n == 32 and 2 * shard == CHIP * 128


def once(v, *earlier):
    return lax.optimization_barrier((v,) + earlier)[0]


def gather_blocks(weights, n, make, inputs):
    if fits(n, weights.shape[1]):
        own = own_rows(weights)
        own_x = move(own, n, 2)
        first, third, second = (move(own, n, 8 * k) for k in (1, 3, 2))
        meanwhile = make(*once(inputs, own_x))
        one = jnp.stack([own, own_x])
        one = jnp.concatenate([one, move(one, n, 4)])
        one, first, meanwhile = lax.optimization_barrier((one, first, meanwhile))
        three = jnp.stack([first, move(first, n, 2)])
        two = jnp.stack([second, move(second, n, 4)])
        four = jnp.stack([third, move(third, n, 4)])
        two, three = lax.optimization_barrier((two, three))
        left = jnp.concatenate([one, two, move(two, n, 2)])
        right = jnp.concatenate([three, move(three, n, 4), four, move(four, n, 2)])
        return [left, move(left, n, 1), right, move(right, n, 1)], meanwhile
    flat = lax.all_gather(weights.astype(BF), "dp", axis=0, tiled=True).reshape(32, -1)
    blocks = jnp.pad(flat, ((0, 0), (0, BLK * 128 - flat.shape[1]))).reshape(4, 2, 2, 2, BLK, 128)
    groups = []
    for core, layers in GROUPS:
        v = blocks[:, :, :, core]
        both = [v[layers[0]], v[layers[1]].transpose(1, 0, 2, 3)]
        groups.append(jnp.stack(both).reshape(8, BLK, 128))
    return groups, make(*inputs)


def add(a, b):
    return (a.astype(F32) + b.astype(F32)).astype(BF)


def fold_core_kernel(keep, come, ak, asend, bk, bsend):
    for j in range(4):
        for k in range(4):
            v = add(keep[j, k], come[j, k])
            (ak, asend)[j & 1][j >> 1, k] = v[:HALF]
            (bk, bsend)[j >> 1][j & 1, k] = v[HALF:]


def fold_core(keep, come):
    part = here((2, 4, HALF, 128), BF)
    return kernel_call(fold_core_kernel, [part] * 4, "vv", mb=16, name="fold_core", us=2.0)(keep, come)


def fold_first_kernel(keep, come, ak, asend, b):
    v = [add(keep[x], come[x]) for x in (0, 1)]
    ak[...] = v[0][:HALF]
    asend[...] = v[1][:HALF]
    for x in (0, 1):
        b[x] = v[x][HALF:]


def fold_first(keep, come):
    outs = [shape((HALF, 128), BF), shape((HALF, 128), BF), shape((2, HALF, 128), BF)]
    return kernel_call(fold_first_kernel, outs, "vv", name="fold_first", us=0.6)(keep, come)


def fold_plane_kernel(me, ak, acome, bk, bcome, fak, facome, fb, fbcome, ak2, asend2, bk2, bsend2):
    z, y = me[0] >> 3, (me[0] >> 2) & 1
    for i, (a, b) in enumerate(((ak2, bk2), (asend2, bsend2))):
        for k in range(4):
            a[k] = add(ak[i, k], acome[i, k])
            b[k] = add(bk[i, k], bcome[i, k])

        @pl.when(y == i)
        def _():
            a[z] = add(a[z], add(fak[...], facome[...]))

        @pl.when(y == 0)
        def _():
            b[z] = add(b[z], add(fb[i], fbcome[i]))


def fold_plane(me, *args):
    part = here((4, HALF, 128), BF)
    return kernel_call(fold_plane_kernel, [part] * 4, "s" + "v" * 8, name="fold_plane", us=1.0)(me, *args)


def fold_layers_kernel(ak, acome, bk, bcome, *outs):
    for k, out in enumerate(outs):
        out[0:HALF] = add(ak[k], acome[k])
        out[HALF:] = add(bk[k], bcome[k])


def fold_layers(*args):
    return kernel_call(fold_layers_kernel, [shape((BLK, 128), BF)] * 4, "vvvv", name="fold_layers", us=0.6)(*args)


def to_rows(even, odd):
    return jnp.concatenate([even[:, :794], odd[:, :795]], axis=1).reshape(-1, 128)


def own_kernel(me, v0, v1, v2, v3, gbi, gbs, gbp, gbo, loss, rowm, grad, last):
    g = (v0[...].astype(F32) + v1[...].astype(F32)) + (v2[...].astype(F32) + v3[...].astype(F32))
    grad[0:BLK, :] = g
    grad[BLK:, :] = jnp.zeros((8, 128), F32)
    row = lax.broadcasted_iota(jnp.int32, (BLK, 128), 0)
    lane = lax.broadcasted_iota(jnp.int32, (BLK, 128), 1)
    place = 128 * row + lane - 64 * (me[0] & 1)
    mine = jnp.where((place >= 0) & (place < 64 * CHIP), g, 0.0)
    square = jnp.sum(jnp.sum(mine * mine, axis=0, keepdims=True), axis=1, keepdims=True)
    weight = jnp.sum(rowm[:, 1:2], axis=0, keepdims=True)
    at_row = 0
    for src, line, count in ((gbi, 4, 12), (gbs, 0, 12), (gbp, 0, 2), (gbo, 0, 47)):
        for j in range(count):
            last[at_row : at_row + 1, :] = src[line : line + 1, 128 * j : 128 * j + 128]
            at_row = at_row + 1
    lane = lax.broadcasted_iota(jnp.int32, (1, 128), 1)
    extra = jnp.where(lane == 0, square, jnp.where(lane == 1, loss[0:1, :], jnp.where(lane == 2, weight, 0.0)))
    last[at_row : at_row + 1, :] = extra
    last[at_row + 1 :, :] = jnp.zeros((80 - at_row - 1, 128), F32)


def own_sums(me, *args):
    return kernel_call(
        own_kernel,
        [here((BLK + 8, 128)), shape((80, 128))],
        "s" + "v" * 10,
        name="own_sums",
        us=1.0,
    )(me, *args)


def adam(value, grad, first, second, decay):
    first = beta_one * first + (1.0 - beta_one) * grad
    second = beta_two * second + (1.0 - beta_two) * grad * grad
    first_hat = first * (1.0 / (1.0 - beta_one**STEP))
    second_hat = second * (1.0 / (1.0 - beta_two**STEP))
    value = value - learn_rate * (first_hat / (jnp.sqrt(second_hat) + adam_eps) + decay * value)
    return (value, first, second)


def update_kernel(me, last, grad, w, m, v, b, bm, bv, nw, nm, nv, nb, nbm, nbv, loss, weight, norm):
    rows = NBIAS // 128
    total = last[0:rows, :]
    squares = jnp.sum(jnp.sum(total * total, axis=0, keepdims=True), axis=1, keepdims=True)
    size = jnp.sqrt(squares + last[rows : rows + 1, 0:1])
    scale = jnp.minimum(1.0, clip_norm / size)
    norm[0, 0] = jnp.sum(size)
    loss[0, 0] = jnp.sum(last[rows : rows + 1, 1:2])
    weight[0, 0] = jnp.sum(last[rows : rows + 1, 2:3])
    odd = (me[0] & 1) == 1

    def weights(start, count):
        cols = pl.ds(start, 128 * count)
        row = start // 128
        low = grad[pl.ds(row, count), :]
        high = grad[pl.ds(row + 1, count), :]
        lane = lax.broadcasted_iota(jnp.int32, (count, 128), 1)
        turned = jnp.where(lane < 64, pltpu.roll(low, 64, 1), pltpu.roll(high, 64, 1))
        g = jnp.where(odd, turned, low) * scale
        load = lambda ref: ref[0:1, cols].reshape(count, 128)
        for ref, out in zip((nw, nm, nv), adam(load(w), g, load(m), load(v), decay_rate)):
            ref[0:1, cols] = out.reshape(1, 128 * count)

    wide = 72
    whole = w.shape[1] // 128
    for row in range(0, whole // 8 * 8, wide):
        weights(128 * row, min(wide, whole // 8 * 8 - row))
    for row in range(whole // 8 * 8, whole):
        weights(128 * row, 1)
    cols = slice(128 * whole, 128 * whole + 64)
    low, high = grad[whole : whole + 1, :], grad[whole + 1 : whole + 2, :]
    g = jnp.where(odd, pltpu.roll(low, 64, 1), low)[:, 0:64] * scale
    for ref, out in zip((nw, nm, nv), adam(w[0:1, cols], g, m[0:1, cols], v[0:1, cols], decay_rate)):
        ref[0:1, cols] = out
    for row in range(0, rows, 8):
        count = min(8, rows - row)
        cols = slice(128 * row, 128 * (row + count))
        load = lambda ref: ref[cols].reshape(count, 128)
        for ref, out in zip((nb, nbm, nbv), adam(load(b), total[row : row + count] * scale, load(bm), load(bv), 0.0)):
            ref[cols] = out.reshape(128 * count)


def update(me, last, grad, w, m, v, b, bm, bv):
    one = jax.ShapeDtypeStruct((1, 1), F32)
    return pl.pallas_call(
        update_kernel,
        out_shape=(shape(w.shape),) * 3 + (shape(b.shape),) * 3 + (one,) * 3,
        in_specs=[SM] + [VM] * 8,
        out_specs=(VM,) * 6 + (SM,) * 3,
        compiler_params=params(12),
        name="update",
    )(me, last, grad, w, m, v, b, bm, bv)


def adam_all(last, grad, w, m, v, b, bm, bv):
    total = last[: NBIAS // 128].reshape(-1)
    squares, loss_sum, loss_weight = (last[NBIAS // 128, k] for k in range(3))
    norm = jnp.sqrt(squares + jnp.sum(total * total))
    scale = jnp.minimum(jnp.float32(1.0), clip_norm / norm)
    new = adam(w, (grad * scale)[None], m, v, decay_rate) + adam(b, total * scale, bm, bv, 0.0)
    return (*new, loss_sum, loss_weight, norm)


def prepare_kernel(feats, ivecs, meta, spl, spl_t, rowm, rows, ivs):
    rows[...] = jnp.zeros_like(rows)
    frames = feats[...].astype(F32)
    columns = meta[...].T
    rowm[...] = jnp.zeros_like(rowm)
    first = 0
    for start, length in zip(START, SPAN):
        rows[8 + start : 8 + start + length, 0:FEAT] = frames[first : first + length]
        rowm[start : start + length, :] = columns[first : first + length]
        first = first + length
    ivs[...] = jnp.zeros_like(ivs)
    ivs[0:4, 0:IVEC] = ivecs[...].astype(F32)
    row = lax.broadcasted_iota(jnp.int32, (ROWS, 128), 0)
    lane = lax.broadcasted_iota(jnp.int32, (ROWS, 128), 1)
    iv = ivs[3:4, :]
    for k in (2, 1, 0):
        iv = jnp.where(row < START[k + 1], ivs[k : k + 1, :], iv)
    left = rows[7 : 7 + ROWS, :]
    left = jnp.where(lane < FEAT, left, pltpu.roll(rows[8 : 8 + ROWS, :], FEAT, 1))
    left = jnp.where(lane < 2 * FEAT, left, pltpu.roll(rows[9 : 9 + ROWS, :], 2 * FEAT, 1))
    left = jnp.where(lane < 3 * FEAT, left, pltpu.roll(iv, 3 * FEAT, 1))
    ones = 3 * FEAT + IVEC - 128
    right = jnp.where(lane < ones, pltpu.roll(iv, 3 * FEAT, 1), jnp.where(lane == ones, 1.0, 0.0))
    spl[:, 0:128] = left.astype(BF)
    spl[:, 128:256] = right.astype(BF)
    spl_t[0:128, :] = left.T.astype(BF)
    spl_t[128:256, :] = right.T.astype(BF)


def prepare(features, ivectors, frame_mask, labels, confidence):
    mask = frame_mask.astype(F32)
    meta = jnp.stack([mask, confidence * mask, jnp.ones_like(mask), labels.astype(F32)])
    meta = jnp.pad(meta, ((0, 4), (0, ROWS - mask.shape[0])))
    return kernel_call(
        prepare_kernel,
        [shape((ROWS, 256), BF), shape((256, ROWS), BF), shape((ROWS, 8))],
        "vvv",
        [vmem((ROWS + 16, 128)), vmem((8, 128))],
        name="prepare",
        us=2.0,
    )(features, ivectors, meta)


def on_device(
    features,
    ivectors,
    frame_mask,
    labels,
    confidence,
    weights,
    first_moment,
    second_moment,
    biases,
    bias_first,
    bias_second,
):
    n = lax.axis_size("dp")
    size = weights.shape[1]
    index = lax.axis_index("dp")
    fast = fits(n, size)
    me = index if fast else jnp.int32(0)
    place = me.reshape(1)
    blocks, (spliced, spl_t, rowm) = gather_blocks(
        weights, n, prepare, (features, ivectors, frame_mask, labels, confidence)
    )
    bias = biases[None]
    w_in = unpack_in(place, blocks)
    h1, gp1, st = layer_in(spliced, w_in, bias, rowm)
    if fast:
        tot1 = sum_core(st, n)
        w1a, w1b, w2a, w2b = unpack_mid(place, once(blocks, tot1))
        tot1 = sum_layers(tot1, n)
        tot1, w1a = lax.optimization_barrier((tot1, w1a))
        flat_out = flatten_out(place, once(blocks, tot1), 12, SPLIT - 1)
        tot1 = sum_plane(tot1, n)
        tot1, flat_out = lax.optimization_barrier((tot1, flat_out))
    else:
        tot1 = total(st, n)
        w1a, w1b, w2a, w2b = unpack_mid(place, blocks)
        flat_out = flatten_out(place, blocks, 12, SPLIT - 1)
        flat_two = flatten_out(place, blocks, SPLIT, 31)
    rounded, fac, fnext, h2, gp2, st = layer_mid(h1, tot1, w1a, w1b, w2a, w2b, bias, rowm)
    if fast:
        tot2 = sum_core(st, n)
        flat_two = flatten_out(place, once(blocks, tot2), SPLIT, 31)
        tot2 = sum_layers(tot2, n)
        tot2, flat_two = lax.optimization_barrier((tot2, flat_two))
        w_pre, w_out = unpack_out(flat_out, once(flat_two, tot2), h2)
        tot2 = sum_plane(tot2, n)
        tot2, w_pre = lax.optimization_barrier((tot2, w_pre))
    else:
        tot2 = total(st, n)
        w_pre, w_out = unpack_out(flat_out, flat_two, h2)
    summed, n2b, dpre, dsum, go, gbo, st, loss, pre = head(h1, tot1, h2, tot2, w_pre, w_out, bias, rowm)
    tot3 = sum_layers(sum_core(st, n), n) if fast else total(st, n)
    keep, send, edge, gbp = side_out(place, *once((summed, dpre, go), tot3))
    if fast:
        tot3 = sum_plane(tot3, n)
        tot3, keep = lax.optimization_barrier((tot3, keep))
    dact, dfac, dfnext, dn, st = back_mid(rounded, tot1, n2b, gp2, tot2, dsum, tot3, w1a, w1b, w2a, w2b, rowm)
    parts = (edge, fac, fnext, dact, rounded, dfac, dfnext, dn)
    if fast:
        tot4 = sum_core(st, n)
        keep, send, gbs = side_mid(place, keep, send, *once(parts, tot4))
        keep, send, tot4 = lax.optimization_barrier((keep, send, tot4))
        blocks = fold_core(keep, move(send, n, 1))
        tot4, blocks = lax.optimization_barrier((sum_plane(tot4, n), blocks))
        tot4 = sum_layers(tot4, n)
        a_keep, a_send, b_keep, b_send = blocks
        a_come, b_come = move(a_send, n, 2), move(b_send, n, 4)
    else:
        tot4 = total(st, n)
        keep, send, gbs = side_mid(place, keep, send, *parts)
    keep_in, send_in, gbi = back_in(place, rounded, gp1, tot1, dn, tot4, spl_t, rowm)
    if fast:
        first = fold_first(keep_in, move(send_in, n, 1))
        first = list(first)
        a_come, first[1] = lax.optimization_barrier((a_come, first[1]))
        first_keep, first_send, first_b = first
        first_a = (first_keep, move(first_send, n, 2))
        first_b = (first_b, move(first_b, n, 4, lambda t: (t & 4) == 0))
        a_keep, a_send, b_keep, b_send = fold_plane(place, a_keep, a_come, b_keep, b_come, *first_a, *first_b)
        parts = fold_layers(a_keep, move(a_send, n, 4), b_keep, move(b_send, n, 2))
        pre = once(pre, parts[0])
        parts = [parts[0]] + [move(parts[k], n, 8 * k) for k in (1, 2, 3)]
        loss = loss - picked_sum(pre, w_out, bias, rowm)
        grad, last = own_sums(place, *parts, gbi, gbs, gbp, gbo, loss, rowm)
        *new, loss_sum, loss_weight, norm = update(
            place, total(last, n), grad, weights, first_moment, second_moment, biases, bias_first, bias_second
        )
        return (*new, loss_sum.reshape(()), loss_weight.reshape(()), norm.reshape(()))
    in_order = lambda v: v.transpose(1, 0, 2, 3).reshape(16, BLK, 128)
    loss = loss - picked_sum(pre, w_out, bias, rowm)
    rows = to_rows(in_order(keep), in_order(send))
    rows = jnp.concatenate([rows[: 2 * CHIP] + to_rows(keep_in, send_in), rows[2 * CHIP :]], axis=0)
    grad = lax.psum_scatter(rows.astype(F32).reshape(n, size), "dp", scatter_dimension=0, tiled=True).reshape(-1)
    bias_grad = jnp.concatenate([gbi[4], gbs[0], gbp[0], gbo[0, :SEN]])
    extra = jnp.stack([jnp.sum(grad * grad), loss[0, 0], jnp.sum(rowm[:, 1])])
    last = total(jnp.concatenate([bias_grad, jnp.pad(extra, (0, 7 * 128 - 3))]).reshape(80, 128), n)
    return adam_all(last, grad, weights, first_moment, second_moment, biases, bias_first, bias_second)


def solution(mesh):
    return jax.shard_map(
        on_device,
        mesh=mesh,
        in_specs=(
            P("dp", None),
            P("dp", None),
            P("dp"),
            P("dp"),
            P("dp"),
            P("dp", None),
            P("dp", None),
            P("dp", None),
            P(),
            P(),
            P(),
        ),
        out_specs=(P("dp", None), P("dp", None), P("dp", None), P(), P(), P(), P(), P(), P()),
        check_vma=False,
    )
```

```python
import functools
import math

import jax
import jax.numpy as jnp
from jax import lax
from jax.experimental import pallas as pl
from jax.experimental.pallas import tpu as pltpu
from jax.sharding import PartitionSpec as P

FEAT = 40
IVEC = 100
HID = 1536
BOT = 160
PRE = 256
SEN = 6016
SPAN = (140, 140, 150, 300)
START = (0, 144, 288, 448)
ROWS = 768
SEGS = ((0, 288), (288, 448), (448, 768))
SENP = 6144
STEP = 10
NBIAS = 9344

bypass_scale = 0.66
norm_eps = 0.001
learn_rate = 0.05
beta_one = 0.9
beta_two = 0.999
adam_eps = 1e-08
decay_rate = 0.01
clip_norm = 1.0

F32 = jnp.float32
BF = jnp.bfloat16
VM = pl.BlockSpec(memory_space=pltpu.VMEM)
SM = pl.BlockSpec(memory_space=pltpu.SMEM)
HB = pl.BlockSpec(memory_space=pltpu.HBM)

CHIP = 1589
BLK = 800
GROUPS = ((0, (0, 2)), (1, (0, 2)), (0, (1, 3)), (1, (1, 3)))
OFF = (0, 2640, 6480, 10320, 13392)
ROWS_ALL = 16 * CHIP
TILE = 256
NT = HID // TILE
WIDE = 1024
NW = SENP // WIDE
FLAT = ROWS_ALL + 64
FROM = 2376
HALF = 416
BIG = 512
NB = HID // BIG
GELU_C = math.sqrt(2.0 / math.pi)


def shape(dims, kind=F32):
    return jax.ShapeDtypeStruct(dims, kind)


def params(mb):
    return pltpu.CompilerParams(vmem_limit_bytes=mb * 2**20)


def here(dims, kind=F32):
    return pltpu.VMEM(dims, kind)


def kernel_call(body, outs, ins, scratch=(), mb=12, name=None, us=1.0):
    spec = {"s": SM, "v": VM, "n": VM, "h": HB}
    call = pl.pallas_call(
        body,
        out_shape=tuple(outs),
        in_specs=[spec[k] for k in ins],
        out_specs=tuple(VM for _ in outs),
        scratch_shapes=list(scratch),
        compiler_params=params(mb),
        cost_estimate=pl.CostEstimate(flops=int(us * 1e9), bytes_accessed=int(us * 3e6), transcendentals=0),
        name=name,
    )
    return lambda *args: call(
        *(pltpu.with_memory_space_constraint(v, pltpu.VMEM) if k == "n" else v for k, v in zip(ins, args))
    )


def sems(n):
    return pltpu.SemaphoreType.DMA((n,))


def vmem(dims, kind=F32):
    return pltpu.VMEM(dims, kind)


def dot(a, b):
    return jnp.dot(a, b, preferred_element_type=F32)


def dot_nt(a, b):
    return lax.dot_general(a, b, (((1,), (1,)), ((), ())), preferred_element_type=F32)


def at(j, size):
    return slice(j * size, (j + 1) * size)


def unrolled(count):
    def run(body):
        for j in range(count):
            body(j)

    return run


def block_row(d):
    return (d >> 1) * CHIP + (d & 1) * 794


def own_rows_kernel(w, out, lines):
    whole = w.shape[1] // 128
    lines[whole:, :] = jnp.zeros((BLK - whole, 128), F32)
    for row in range(0, whole // 8 * 8, 72):
        count = min(72, whole // 8 * 8 - row)
        lines[row : row + count, :] = w[0:1, 128 * row : 128 * (row + count)].reshape(count, 128)
    for row in range(whole // 8 * 8, whole):
        lines[row : row + 1, :] = w[0:1, 128 * row : 128 * row + 128]
    lines[whole : whole + 1, 0:64] = w[0:1, 128 * whole :]
    out[...] = lines[...].astype(BF)


def own_rows(weights):
    return kernel_call(own_rows_kernel, [shape((BLK, 128), BF)], "v", [vmem((BLK, 128))], name="own_rows", us=1.0)(weights)[0]


def put_block(flat, d, v, start=0):
    first = block_row(d) - start
    v = v.astype(F32)
    if d % 2:
        v = pltpu.roll(v, 64, 1)
        low = lax.broadcasted_iota(jnp.int32, v.shape, 1) < 64
        flat[first : first + 1, :] = jnp.where(low[0:1], flat[first : first + 1, :], v[0:1])
        flat[first + 1 : first + 795, :] = jnp.where(low[:794], v[0:794], v[1:795])
    else:
        flat[first : first + 795, :] = v[:795]


def fetch_blocks(me, groups, first, last, stage, sem):
    for src, (core, layers) in zip(groups, GROUPS):
        for i in range(8):
            low, high = i & 1, (i >> 1) & 1
            x, y = (low, high) if i < 4 else (high, low)
            d = me[0] ^ (8 * layers[i // 4] + 4 * y + 2 * x + core)

            @pl.when((d >= first) & (d <= last))
            def _():
                pltpu.make_async_copy(src.at[i], stage.at[d - first], sem.at[d - first]).start()


def block_ready(src, d, stage, sem):
    pltpu.make_async_copy(src.at[0], stage.at[d], sem.at[d]).wait()


def unpack_in_kernel(me, g0, g1, g2, g3, win, stage, flat, sem):
    fetch_blocks(me, (g0, g1, g2, g3), 0, 3, stage, sem)
    for d in range(4):
        block_ready(g0, d, stage, sem)
        put_block(flat, d, stage[d])
    for j in range(12):
        v = flat[pl.ds(j, 224, stride=12), :]
        v = jnp.where(lax.broadcasted_iota(jnp.int32, (224, 128), 0) < 220, v, 0.0)
        win[0:224, 128 * j : 128 * j + 128] = v.astype(BF)
    win[224:256, :] = jnp.zeros((32, HID), BF)


def unpack_in(me, groups):
    return kernel_call(
        unpack_in_kernel,
        [here((256, HID), BF)],
        "shhhh",
        [vmem((4, BLK, 128), BF), vmem((2 * CHIP + 14, 128)), sems(4)],
        name="unpack_in",
        us=1.5,
    )(me, *groups)[0]


def unpack_mid_kernel(me, g0, g1, g2, g3, w1a, w1b, w2a, w2b, stage, flat, tall, tall2, sem):
    fetch_blocks(me, (g0, g1, g2, g3), 2, 12, stage, sem)
    start = block_row(2)
    first, second = OFF[1] - start, OFF[2] - start
    for d in range(2, 13):
        block_ready(g0, d - 2, stage, sem)
        put_block(flat, d, stage[d - 2], start)
    lane = lax.broadcasted_iota(jnp.int32, (768, 128), 1)
    a = [flat[pl.ds(first + q, 768, stride=5), :] for q in range(5)]

    def put(r, t0, t1):
        tall[pl.ds(r, 768, stride=4), :] = t0
        tall2[pl.ds(r, 768, stride=4), :] = jnp.where(lane < 32, t1, 0.0)

    put(0, a[0], a[1])
    for r in (1, 2, 3):
        turn = 128 - 32 * r
        low = pltpu.roll(a[r], turn, 1)
        high = pltpu.roll(a[r + 1], turn, 1)
        put(r, jnp.where(lane < turn, low, high), high)
    for out, row in ((w1a, 0), (w1b, 1536)):
        out[:, 0:128] = tall[row : row + 1536, :].astype(BF)
        out[:, 128:256] = tall2[row : row + 1536, :].astype(BF)
    for j in range(12):
        v = flat[pl.ds(second + j, 320, stride=12), :].astype(BF)
        w2a[0:160, 128 * j : 128 * j + 128] = v[:160]
        w2b[0:160, 128 * j : 128 * j + 128] = v[160:]
    w2a[160:256, :] = jnp.zeros((96, HID), BF)
    w2b[160:256, :] = jnp.zeros((96, HID), BF)


def unpack_mid(me, groups):
    return kernel_call(
        unpack_mid_kernel,
        [here((HID, 256), BF)] * 2 + [here((256, HID), BF)] * 2,
        "shhhh",
        [
            vmem((11, BLK, 128), BF),
            vmem((6 * CHIP, 128)),
            vmem((3072, 128)),
            vmem((3072, 128)),
            sems(11),
        ],
        mb=15,
        name="unpack_mid",
        us=5.2,
    )(me, *groups)


SPLIT = 22


def flatten_out_kernel(first, last, me, g0, g1, g2, g3, flat, stage, sem):
    fetch_blocks(me, (g0, g1, g2, g3), first, last, stage, sem)
    for d in range(first, last + 1):
        block_ready(g0, d - first, stage, sem)
        put_block(flat, d, stage[d - first], block_row(first))


def flatten_out(me, groups, first, last):
    count = last + 1 - first
    return kernel_call(
        functools.partial(flatten_out_kernel, first, last),
        [here((CHIP * count // 2, 128))],
        "shhhh",
        [vmem((count, BLK, 128), BF), sems(count)],
        name="flatten_out",
        us=3.0,
    )(me, *groups)[0]


def unpack_out_kernel(one, two, _, wp, wo, flat):
    pre, out = OFF[3] - block_row(12), OFF[4] - block_row(12)
    flat[0 : one.shape[0], :] = one[...]
    flat[one.shape[0] :, :] = two[...]
    for j in range(2):
        wp[:, 128 * j : 128 * j + 128] = flat[pl.ds(pre + j, 1536, stride=2), :].astype(BF)
    for j in range(47):
        wo[:, 128 * j : 128 * j + 128] = flat[pl.ds(out + j, 256, stride=47), :].astype(BF)
    wo[:, 6016:] = jnp.zeros((256, 128), BF)


def unpack_out(one, two, h2):
    return kernel_call(
        unpack_out_kernel,
        [here((HID, PRE), BF), here((PRE, SENP), BF)],
        "nnn",
        [vmem((10 * CHIP, 128))],
        mb=14,
        name="unpack_out",
        us=3.0,
    )(one, two, h2)


def put_columns(flat, first, grad, rows, width):
    for j in range(width // 128):
        flat[pl.ds(first + j, rows, stride=width // 128), :] = grad(128 * j)


def put_first(flat, first, tall, tall2):
    lane = lax.broadcasted_iota(jnp.int32, (768, 128), 1)
    t0 = [tall[pl.ds(r, 768, stride=4), :] for r in range(4)]
    t1 = [tall2[pl.ds(r, 768, stride=4), :] for r in range(4)]
    flat[pl.ds(first, 768, stride=5), :] = t0[0]
    for q in (1, 2, 3):
        shift = 32 * (q - 1)
        tail = t1[0]
        if q > 1:
            tail = jnp.where(lane < shift, pltpu.roll(t0[q - 1], shift, 1), pltpu.roll(t1[q - 1], shift, 1))
        flat[pl.ds(first + q, 768, stride=5), :] = jnp.where(lane < 32 * q, tail, pltpu.roll(t0[q], 32 * q, 1))
    flat[pl.ds(first + 4, 768, stride=5), :] = jnp.where(
        lane < 96, pltpu.roll(t0[3], 96, 1), pltpu.roll(t1[3], 96, 1)
    )


def gelu_parts(act):
    square = act * act
    t = jnp.tanh(GELU_C * act * (1.0 + 0.044715 * square))
    cdf = 0.5 + 0.5 * t
    slope = cdf + (0.5 * act) * (1.0 - t * t) * (GELU_C + (3 * 0.044715 * GELU_C) * square)
    return act * cdf, slope


def put_sums(st, first, v):
    for s, (a, b) in enumerate(SEGS):
        st[first + s : first + s + 1, :] = jnp.sum(v[a:b], axis=0, keepdims=True)


def norm_rows(tot, s, cols):
    count = tot[6:7, s : s + 1]
    mean = tot[s : s + 1, cols] / count
    var = tot[3 + s : 4 + s, cols] / count - mean * mean
    return mean, lax.rsqrt(var + norm_eps)


def put_stats(st, cols, hidden, mask):
    masked = hidden * mask
    square = masked * hidden
    for s, (a, b) in enumerate(SEGS):
        st[s : s + 1, cols] = jnp.sum(masked[a:b], axis=0, keepdims=True)
        st[3 + s : 4 + s, cols] = jnp.sum(square[a:b], axis=0, keepdims=True)


def put_counts(st, mask):
    lane = lax.broadcasted_iota(jnp.int32, (2, HID), 1)
    counts = [jnp.sum(mask[a:b], axis=0, keepdims=True) for a, b in SEGS]
    st[6:8, :] = jnp.where(lane == 0, counts[0], jnp.where(lane == 1, counts[1], counts[2]))


def put_grads(st, cols, s, grad, normed):
    st[s : s + 1, cols] = jnp.sum(grad, axis=0, keepdims=True)
    st[3 + s : 4 + s, cols] = jnp.sum(grad * normed, axis=0, keepdims=True)


def in_kernel(spl, w, b, rowm, h, gp, st):
    mask = rowm[:, 0:1]

    @unrolled(NB)
    def _(j):
        cols = at(j, BIG)
        hidden, slope = gelu_parts(dot(spl[...], w[:, cols]) + b[:, cols])
        h[:, cols] = hidden
        gp[:, cols] = slope.astype(BF)
        put_stats(st, cols, hidden, mask)

    put_counts(st, mask)


def layer_in(spliced, w_in, b_in, rowm):
    return kernel_call(
        in_kernel,
        [here((ROWS, HID)), here((ROWS, HID), BF), shape((8, HID))],
        "vnvv",
        name="layer_in",
        us=4.1,
    )(spliced, w_in, b_in, rowm)


def mid_kernel(h, tot, w1a, w1b, w2a, w2b, bias, rowm, rounded, fac, fnext, h2, gp2, st):
    valid = rowm[:, 2:3]
    mask = rowm[:, 0:1]

    @unrolled(NT)
    def _(j):
        cols = at(j, TILE)
        for s, (a, b) in enumerate(SEGS):
            mean, scale = norm_rows(tot, s, cols)
            rounded[a:b, cols] = ((h[a:b, cols] - mean) * scale).astype(BF)

    ua = dot(rounded[...], w1a[...])
    ub = dot(rounded[...], w1b[...])
    f = ((ub + pltpu.roll(ua * valid, 1, 0)) * valid).astype(BF)
    fac[...] = f
    fnext[...] = (pltpu.roll(f.astype(F32), ROWS - 1, 0) * valid).astype(BF)

    @unrolled(NB)
    def _(j):
        cols = at(j, BIG)
        act = dot(fac[...], w2a[:, cols]) + dot(fnext[...], w2b[:, cols]) + bias[:, at(j + HID // BIG, BIG)]
        hidden, slope = gelu_parts(act)
        h2[:, cols] = hidden
        gp2[:, cols] = slope.astype(BF)
        put_stats(st, cols, hidden, mask)

    put_counts(st, mask)


def layer_mid(h, tot, w1a, w1b, w2a, w2b, bias, rowm):
    return kernel_call(
        mid_kernel,
        [
            here((ROWS, HID), BF),
            here((ROWS, 256), BF),
            here((ROWS, 256), BF),
            here((ROWS, HID)),
            here((ROWS, HID), BF),
            shape((8, HID)),
        ],
        "nvnnnnvv",
        name="layer_mid",
        us=7.4,
    )(h, tot, w1a, w1b, w2a, w2b, bias, rowm)


def head_kernel(
    h1, tot1, h2, tot2, wp, wo, bias, rowm, summed, n2b, dpre, dsum, go, gb, st, loss, pre_out, acc
):
    @unrolled(NT)
    def _(j):
        cols = at(j, TILE)
        for s, (a, b) in enumerate(SEGS):
            mean1, scale1 = norm_rows(tot1, s, cols)
            mean2, scale2 = norm_rows(tot2, s, cols)
            n1 = (h1[a:b, cols] - mean1) * scale1
            n2 = (h2[a:b, cols] - mean2) * scale2
            summed[a:b, cols] = (n2 + bypass_scale * n1).astype(BF)
            n2b[a:b, cols] = n2.astype(BF)

    pre = (dot(summed[...], wp[...]) + bias[:, 2 * HID : 2 * HID + PRE]).astype(BF)
    lane = lax.broadcasted_iota(jnp.int32, (ROWS, 128), 1)
    where = rowm[:, 3:4].astype(jnp.int32) - lane
    weight = rowm[:, 1:2]

    bo = jnp.concatenate([bias[:, 2 * HID + PRE :], jnp.full((1, SENP - SEN), -1e30, F32)], axis=1)

    m = jnp.full((ROWS, 128), -1e30, F32)
    total = jnp.zeros((ROWS, 128), F32)
    for j in range(NW):
        cols = slice(WIDE * j, WIDE * j + WIDE)
        v = dot(pre, wo[:, cols]) + bo[:, cols]
        parts = [v[:, 128 * q : 128 * q + 128] for q in range(WIDE // 128)]
        old = m
        for p in parts:
            m = jnp.maximum(m, p)
        total = total * jnp.exp(old - m)
        for p in parts:
            total = total + jnp.exp(p - m)

    top = jnp.max(m, axis=1, keepdims=True)
    total = jnp.sum(total * jnp.exp(m - top), axis=1, keepdims=True)
    lse = jnp.log(total) + top
    less = lse - jnp.log(weight)
    acc[...] = jnp.zeros_like(acc)
    pre_t = jnp.concatenate([pre.astype(F32).T.astype(BF), jnp.ones((16, ROWS), BF)], axis=0)
    for j in range(NW):
        cols = slice(WIDE * j, WIDE * j + WIDE)
        v = dot(pre, wo[:, cols]) + bo[:, cols]
        parts = []
        for q in range(WIDE // 128):
            p = v[:, 128 * q : 128 * q + 128]
            hit = jnp.where(where == j * WIDE + 128 * q, weight, 0.0)
            parts.append((jnp.exp(p - less) - hit).astype(BF))
        d = jnp.concatenate(parts, axis=1)
        acc[...] += dot_nt(d, wo[:, cols])
        g = dot(pre_t, d)
        go[:, cols] = g[0:PRE].astype(BF)
        gb[:, cols] = g[PRE : PRE + 8]

    entropy = jnp.sum(weight * lse, axis=0, keepdims=True)
    loss[...] = jnp.zeros((8, 128), F32) + entropy
    pre_out[...] = pre
    dp = acc[...].astype(BF)
    dpre[...] = dp

    @unrolled(NT)
    def _(j):
        cols = at(j, TILE)
        ds = dot_nt(dp, wp[cols, :])
        dsum[:, cols] = ds
        for s, (a, b) in enumerate(SEGS):
            put_grads(st, cols, s, ds[a:b], n2b[a:b, cols].astype(F32))

    st[6:8, :] = jnp.zeros((2, HID), F32)


def head(h1, tot1, h2, tot2, wp, wo, bias, rowm):
    return kernel_call(
        head_kernel,
        [
            here((ROWS, HID), BF),
            here((ROWS, HID), BF),
            here((ROWS, PRE), BF),
            here((ROWS, HID)),
            here((PRE, SENP), BF),
            shape((8, SENP)),
            shape((8, HID)),
            shape((8, 128)),
            shape((ROWS, PRE), BF),
        ],
        "nvnvnnvv",
        [
            vmem((ROWS, PRE)),
        ],
        mb=14,
        name="head",
        us=20.0,
    )(h1, tot1, h2, tot2, wp, wo, bias, rowm)


def picked_kernel(pre, wo, bias, rowm, out):
    lane = lax.broadcasted_iota(jnp.int32, (ROWS, 128), 1)
    where = rowm[:, 3:4].astype(jnp.int32) - lane
    weight = rowm[:, 1:2]
    bo = jnp.concatenate([bias[:, 2 * HID + PRE :], jnp.zeros((1, SENP - SEN), F32)], axis=1)
    total = jnp.zeros((ROWS, 128), F32)
    for j in range(NW):
        cols = slice(WIDE * j, WIDE * j + WIDE)
        v = dot(pre[...], wo[:, cols]) + bo[:, cols]
        for q in range(WIDE // 128):
            total = total + jnp.where(where == j * WIDE + 128 * q, v[:, 128 * q : 128 * q + 128], 0.0)
    total = jnp.sum(total, axis=1, keepdims=True) * weight
    out[...] = jnp.zeros((8, 128), F32) + jnp.sum(total, axis=0, keepdims=True)


def picked_sum(pre, wo, bias, rowm):
    return kernel_call(picked_kernel, [shape((8, 128))], "vvvv", mb=14, name="picked_sum", us=5.0)(pre, wo, bias, rowm)[0]


def back_mid_kernel(
    n1b, tot1, n2b, gp2, tot2, dsum, tot3, w1a, w1b, w2a, w2b, rowm, dact, dfac, dfnext, dn, st
):
    valid = rowm[:, 2:3]

    @unrolled(NT)
    def _(j):
        cols = at(j, TILE)
        for s, (a, b) in enumerate(SEGS):
            mean, scale = norm_rows(tot2, s, cols)
            along = tot3[s : s + 1, cols]
            cross = tot3[3 + s : 4 + s, cols]
            part = rowm[a:b, 0:1] / tot1[6:7, s : s + 1]
            n2 = n2b[a:b, cols].astype(F32)
            back = scale * (dsum[a:b, cols] - part * (along + cross * n2))
            dact[a:b, cols] = (gp2[a:b, cols] * back).astype(BF)

    ua = dot_nt(dact[...], w2a[...])
    ub = dot_nt(dact[...], w2b[...])
    f = ((ua + pltpu.roll(ub, 1, 0)) * valid).astype(BF)
    dfac[...] = f
    dfnext[...] = (pltpu.roll(f.astype(F32), ROWS - 1, 0) * valid).astype(BF)

    @unrolled(NT)
    def _(j):
        cols = at(j, TILE)
        grad = bypass_scale * dsum[:, cols] + dot_nt(dfac[...], w1b[cols, :]) + dot_nt(dfnext[...], w1a[cols, :])
        dn[:, cols] = grad
        for s, (a, b) in enumerate(SEGS):
            put_grads(st, cols, s, grad[a:b], n1b[a:b, cols].astype(F32))

    st[6:8, :] = jnp.zeros((2, HID), F32)


def back_mid(n1b, tot1, n2b, gp2, tot2, dsum, tot3, w1a, w1b, w2a, w2b, rowm):
    return kernel_call(
        back_mid_kernel,
        [
            here((ROWS, HID), BF),
            here((ROWS, 256), BF),
            here((ROWS, 256), BF),
            here((ROWS, HID)),
            shape((8, HID)),
        ],
        "nvnnvnvnnnnv",
        name="back_mid",
        us=5.9,
    )(n1b, tot1, n2b, gp2, tot2, dsum, tot3, w1a, w1b, w2a, w2b, rowm)


def side_out_kernel(me, summed, dpre, go, keep, send, edge, gbp, flat):
    ones = jnp.ones((16, ROWS), BF)
    gbp[...] = dot(ones, dpre[...])[0:8]
    for j in range(NT):
        t = summed[:, TILE * j : TILE * j + TILE].astype(F32).T.astype(BF)
        g = dot(t, dpre[...])
        put_columns(flat, 2 * TILE * j, lambda c: g[:, c : c + 128], TILE, PRE)
    put_columns(flat, OFF[4] - OFF[3], lambda c: go[:, c : c + 128].astype(F32), PRE, SEN)
    flat[ROWS_ALL - OFF[3] :, :] = jnp.zeros((FLAT - ROWS_ALL, 128), F32)
    edge[...] = flat[0:16, :]
    for dc, out in ((0, keep), (1, send)):
        for k in range(4):
            for j in range(4):
                d = me[0] ^ (8 * k + 2 * j + dc)

                @pl.when(d > 12)
                def _():
                    out[j, k] = flat[pl.ds(block_row(d) - OFF[3], BLK), :].astype(BF)


def side_out(me, summed, dpre, go):
    return kernel_call(
        side_out_kernel,
        [here((4, 4, BLK, 128), BF), here((4, 4, BLK, 128), BF), shape((16, 128)), shape((8, PRE))],
        "snvn",
        [vmem((FLAT - OFF[3], 128))],
        mb=14,
        name="side_out",
        us=4.0,
    )(me, summed, dpre, go)


def side_mid_kernel(
    me, edge, fac, fnext, dact, rounded, dfac, dfnext, _, keep_in, send_in, keep, send, gbs, flat, tall, tall2
):
    fac_t = fac[...].astype(F32).T.astype(BF)
    next_t = fnext[...].astype(F32).T.astype(BF)
    ones = jnp.ones((16, ROWS), BF)
    flat[0 : OFF[1] - FROM, :] = jnp.zeros((OFF[1] - FROM, 128), F32)
    for j in range(NT):
        cols = slice(TILE * j, TILE * j + TILE)
        t = rounded[:, cols].astype(F32).T.astype(BF)
        for k, d in enumerate((dfnext, dfac)):
            g = dot(t, d[...])
            tall[HID * k + TILE * j : HID * k + TILE * j + TILE, :] = g[:, 0:128]
            tall2[HID * k + TILE * j : HID * k + TILE * j + TILE, :] = g[:, 128:256]
        for k, f in enumerate((fac_t, next_t)):
            g = dot(f, dact[:, cols])
            for q in range(TILE // 128):
                row = OFF[2] - FROM + 1920 * k + TILE // 128 * j + q
                flat[pl.ds(row, BOT, stride=12), :] = g[0:BOT, 128 * q : 128 * q + 128]
        gbs[:, cols] = dot(ones, dact[:, cols])[0:8]
    put_first(flat, OFF[1] - FROM, tall, tall2)
    flat[OFF[3] - FROM : OFF[3] - FROM + 16, :] = edge[...]
    flat[OFF[3] - FROM + 16 :, :] = jnp.zeros((7968 - (OFF[3] - FROM + 16), 128), F32)
    for dc, src, out in ((0, keep_in, keep), (1, send_in, send)):
        for k in range(4):
            for j in range(4):
                d = me[0] ^ (8 * k + 2 * j + dc)

                @pl.when(d > 12)
                def _():
                    out[j, k] = src[j, k]

                @pl.when((d > 2) & (d < 13))
                def _():
                    out[j, k] = flat[pl.ds(block_row(d) - FROM, BLK), :].astype(BF)

                @pl.when(d < 3)
                def _():
                    out[j, k] = jnp.zeros((BLK, 128), BF)


def side_mid(me, keep, send, *args):
    return kernel_call(
        side_mid_kernel,
        [here((4, 4, BLK, 128), BF), here((4, 4, BLK, 128), BF), shape((8, HID))],
        "svnnnnnnnnn",
        [vmem((7968, 128)), vmem((3072, 128)), vmem((3072, 128))],
        mb=14,
        name="side_mid",
        us=6.4,
    )(me, *args, keep, send)


def back_in_kernel(me, n1b, gp, tot1, dn, tot4, spl_t, rowm, keep, send, gb, d, flat):
    @unrolled(NT)
    def _(j):
        cols = at(j, TILE)
        for s, (a, b) in enumerate(SEGS):
            mean, scale = norm_rows(tot1, s, cols)
            along = tot4[s : s + 1, cols]
            cross = tot4[3 + s : 4 + s, cols]
            part = rowm[a:b, 0:1] / tot1[6:7, s : s + 1]
            n1 = n1b[a:b, cols].astype(F32)
            back = scale * (dn[a:b, cols] - part * (along + cross * n1))
            d[a:b, cols] = (gp[a:b, cols] * back).astype(BF)

    for j in range(NT):
        g = dot(spl_t[...], d[:, TILE * j : TILE * j + TILE])
        gb[:, TILE * j : TILE * j + TILE] = g[216:224]
        for q in range(TILE // 128):
            flat[pl.ds(TILE // 128 * j + q, 220, stride=12), :] = g[0:220, 128 * q : 128 * q + 128]
    flat[OFF[1] :, :] = jnp.zeros((2 * CHIP + 14 - OFF[1], 128), F32)
    for dc, out in ((0, keep), (1, send)):
        for dx in (0, 1):
            t = (me[0] & 3) ^ (2 * dx + dc)
            out[dx] = flat[pl.ds(block_row(t), BLK), :].astype(BF)


def back_in(me, n1b, gp, tot1, dn, tot4, spl_t, rowm):
    return kernel_call(
        back_in_kernel,
        [shape((2, BLK, 128), BF), shape((2, BLK, 128), BF), shape((8, HID))],
        "snnvnvvv",
        [vmem((ROWS, HID), BF), vmem((2 * CHIP + 14, 128))],
        name="back_in",
        us=2.8,
    )(me, n1b, gp, tot1, dn, tot4, spl_t, rowm)


def move(x, n, mask, to=None):
    return lax.ppermute(x, "dp", [(i, i ^ mask) for i in range(n) if to is None or to(i ^ mask)])


def exchange(x, n, masks):
    a, b, c = (move(x, n, k) for k in masks)
    return (x + a) + (b + c)


def sum_core(x, n):
    return x + move(x, n, 1)


def sum_layers(x, n):
    return exchange(x, n, (8, 16, 24))


def sum_plane(x, n):
    return exchange(x, n, (2, 4, 6))


def total(x, n):
    if n == 32:
        return sum_plane(sum_layers(sum_core(x, n), n), n)
    bit = 1
    while bit < n:
        x = x + move(x, n, bit)
        bit = 2 * bit
    return x


def fits(n, shard):
    return n == 32 and 2 * shard == CHIP * 128


def once(v, *earlier):
    return lax.optimization_barrier((v,) + earlier)[0]


def gather_blocks(weights, n, make, inputs):
    if fits(n, weights.shape[1]):
        own = own_rows(weights)
        own_x = move(own, n, 2)
        first, third, second = (move(own, n, 8 * k) for k in (1, 3, 2))
        meanwhile = make(*once(inputs, own_x))
        one = jnp.stack([own, own_x])
        one = jnp.concatenate([one, move(one, n, 4)])
        one, first, meanwhile = lax.optimization_barrier((one, first, meanwhile))
        three = jnp.stack([first, move(first, n, 2)])
        two = jnp.stack([second, move(second, n, 4)])
        four = jnp.stack([third, move(third, n, 4)])
        two, three = lax.optimization_barrier((two, three))
        left = jnp.concatenate([one, two, move(two, n, 2)])
        right = jnp.concatenate([three, move(three, n, 4), four, move(four, n, 2)])
        return [left, move(left, n, 1), right, move(right, n, 1)], meanwhile
    flat = lax.all_gather(weights.astype(BF), "dp", axis=0, tiled=True).reshape(32, -1)
    blocks = jnp.pad(flat, ((0, 0), (0, BLK * 128 - flat.shape[1]))).reshape(4, 2, 2, 2, BLK, 128)
    groups = []
    for core, layers in GROUPS:
        v = blocks[:, :, :, core]
        both = [v[layers[0]], v[layers[1]].transpose(1, 0, 2, 3)]
        groups.append(jnp.stack(both).reshape(8, BLK, 128))
    return groups, make(*inputs)


def add(a, b):
    return (a.astype(F32) + b.astype(F32)).astype(BF)


def fold_core_kernel(keep, come, ak, asend, bk, bsend):
    for j in range(4):
        for k in range(4):
            v = add(keep[j, k], come[j, k])
            (ak, asend)[j & 1][j >> 1, k] = v[:HALF]
            (bk, bsend)[j >> 1][j & 1, k] = v[HALF:]


def fold_core(keep, come):
    over_x, over_y = here((2, 4, HALF, 128), BF), here((2, 4, BLK - HALF, 128), BF)
    return kernel_call(fold_core_kernel, [over_x, over_x, over_y, over_y], "vv", mb=16, name="fold_core", us=2.0)(keep, come)


def fold_first_kernel(keep, come, ak, asend, b):
    v = [add(keep[x], come[x]) for x in (0, 1)]
    ak[...] = v[0][:HALF]
    asend[...] = v[1][:HALF]
    for x in (0, 1):
        b[x] = v[x][HALF:]


def fold_first(keep, come):
    outs = [shape((HALF, 128), BF), shape((HALF, 128), BF), shape((2, BLK - HALF, 128), BF)]
    return kernel_call(fold_first_kernel, outs, "vv", name="fold_first", us=0.6)(keep, come)


def fold_plane_kernel(me, ak, acome, bk, bcome, fak, facome, fb, fbcome, ak2, asend2, bk2, bsend2):
    z, y = me[0] >> 3, (me[0] >> 2) & 1
    for i, (a, b) in enumerate(((ak2, bk2), (asend2, bsend2))):
        for k in range(4):
            a[k] = add(ak[i, k], acome[i, k])
            b[k] = add(bk[i, k], bcome[i, k])

        @pl.when(y == i)
        def _():
            a[z] = add(a[z], add(fak[...], facome[...]))

        @pl.when(y == 0)
        def _():
            b[z] = add(b[z], add(fb[i], fbcome[i]))


def fold_plane(me, *args):
    over_y, over_x = here((4, HALF, 128), BF), here((4, BLK - HALF, 128), BF)
    return kernel_call(fold_plane_kernel, [over_y, over_y, over_x, over_x], "s" + "v" * 8, name="fold_plane", us=1.0)(me, *args)


def fold_layers_kernel(ak, acome, bk, bcome, *outs):
    for k, out in enumerate(outs):
        out[0:HALF] = add(ak[k], acome[k])
        out[HALF:] = add(bk[k], bcome[k])


def fold_layers(*args):
    return kernel_call(fold_layers_kernel, [shape((BLK, 128), BF)] * 4, "vvvv", name="fold_layers", us=0.6)(*args)


def to_rows(even, odd):
    return jnp.concatenate([even[:, :794], odd[:, :795]], axis=1).reshape(-1, 128)


def own_kernel(me, v0, v1, v2, v3, gbi, gbs, gbp, gbo, loss, rowm, grad, last):
    g = (v0[...].astype(F32) + v1[...].astype(F32)) + (v2[...].astype(F32) + v3[...].astype(F32))
    grad[0:BLK, :] = g
    grad[BLK:, :] = jnp.zeros((8, 128), F32)
    row = lax.broadcasted_iota(jnp.int32, (BLK, 128), 0)
    lane = lax.broadcasted_iota(jnp.int32, (BLK, 128), 1)
    place = 128 * row + lane - 64 * (me[0] & 1)
    mine = jnp.where((place >= 0) & (place < 64 * CHIP), g, 0.0)
    square = jnp.sum(jnp.sum(mine * mine, axis=0, keepdims=True), axis=1, keepdims=True)
    weight = jnp.sum(rowm[:, 1:2], axis=0, keepdims=True)
    at_row = 0
    for src, line, count in ((gbi, 4, 12), (gbs, 0, 12), (gbp, 0, 2), (gbo, 0, 47)):
        for j in range(count):
            last[at_row : at_row + 1, :] = src[line : line + 1, 128 * j : 128 * j + 128]
            at_row = at_row + 1
    lane = lax.broadcasted_iota(jnp.int32, (1, 128), 1)
    extra = jnp.where(lane == 0, square, jnp.where(lane == 1, loss[0:1, :], jnp.where(lane == 2, weight, 0.0)))
    last[at_row : at_row + 1, :] = extra
    last[at_row + 1 :, :] = jnp.zeros((80 - at_row - 1, 128), F32)


def own_sums(me, *args):
    return kernel_call(
        own_kernel,
        [here((BLK + 8, 128)), shape((80, 128))],
        "s" + "v" * 10,
        name="own_sums",
        us=1.0,
    )(me, *args)


def adam(value, grad, first, second, decay):
    first = beta_one * first + (1.0 - beta_one) * grad
    second = beta_two * second + (1.0 - beta_two) * grad * grad
    first_hat = first * (1.0 / (1.0 - beta_one**STEP))
    second_hat = second * (1.0 / (1.0 - beta_two**STEP))
    value = value - learn_rate * (first_hat / (jnp.sqrt(second_hat) + adam_eps) + decay * value)
    return (value, first, second)


def update_kernel(me, last, grad, w, m, v, b, bm, bv, nw, nm, nv, nb, nbm, nbv, loss, weight, norm):
    rows = NBIAS // 128
    total = last[0:rows, :]
    squares = jnp.sum(jnp.sum(total * total, axis=0, keepdims=True), axis=1, keepdims=True)
    size = jnp.sqrt(squares + last[rows : rows + 1, 0:1])
    scale = jnp.minimum(1.0, clip_norm / size)
    norm[0, 0] = jnp.sum(size)
    loss[0, 0] = jnp.sum(last[rows : rows + 1, 1:2])
    weight[0, 0] = jnp.sum(last[rows : rows + 1, 2:3])
    odd = (me[0] & 1) == 1

    def weights(start, count):
        cols = pl.ds(start, 128 * count)
        row = start // 128
        low = grad[pl.ds(row, count), :]
        high = grad[pl.ds(row + 1, count), :]
        lane = lax.broadcasted_iota(jnp.int32, (count, 128), 1)
        turned = jnp.where(lane < 64, pltpu.roll(low, 64, 1), pltpu.roll(high, 64, 1))
        g = jnp.where(odd, turned, low) * scale
        load = lambda ref: ref[0:1, cols].reshape(count, 128)
        for ref, out in zip((nw, nm, nv), adam(load(w), g, load(m), load(v), decay_rate)):
            ref[0:1, cols] = out.reshape(1, 128 * count)

    wide = 72
    whole = w.shape[1] // 128
    for row in range(0, whole // 8 * 8, wide):
        weights(128 * row, min(wide, whole // 8 * 8 - row))
    for row in range(whole // 8 * 8, whole):
        weights(128 * row, 1)
    cols = slice(128 * whole, 128 * whole + 64)
    low, high = grad[whole : whole + 1, :], grad[whole + 1 : whole + 2, :]
    g = jnp.where(odd, pltpu.roll(low, 64, 1), low)[:, 0:64] * scale
    for ref, out in zip((nw, nm, nv), adam(w[0:1, cols], g, m[0:1, cols], v[0:1, cols], decay_rate)):
        ref[0:1, cols] = out
    for row in range(0, rows, 8):
        count = min(8, rows - row)
        cols = slice(128 * row, 128 * (row + count))
        load = lambda ref: ref[cols].reshape(count, 128)
        for ref, out in zip((nb, nbm, nbv), adam(load(b), total[row : row + count] * scale, load(bm), load(bv), 0.0)):
            ref[cols] = out.reshape(128 * count)


def update(me, last, grad, w, m, v, b, bm, bv):
    one = jax.ShapeDtypeStruct((1, 1), F32)
    return pl.pallas_call(
        update_kernel,
        out_shape=(shape(w.shape),) * 3 + (shape(b.shape),) * 3 + (one,) * 3,
        in_specs=[SM] + [VM] * 8,
        out_specs=(VM,) * 6 + (SM,) * 3,
        compiler_params=params(12),
        name="update",
    )(me, last, grad, w, m, v, b, bm, bv)


def adam_all(last, grad, w, m, v, b, bm, bv):
    total = last[: NBIAS // 128].reshape(-1)
    squares, loss_sum, loss_weight = (last[NBIAS // 128, k] for k in range(3))
    norm = jnp.sqrt(squares + jnp.sum(total * total))
    scale = jnp.minimum(jnp.float32(1.0), clip_norm / norm)
    new = adam(w, (grad * scale)[None], m, v, decay_rate) + adam(b, total * scale, bm, bv, 0.0)
    return (*new, loss_sum, loss_weight, norm)


def prepare_kernel(feats, ivecs, meta, spl, spl_t, rowm, rows, ivs):
    rows[...] = jnp.zeros_like(rows)
    frames = feats[...].astype(F32)
    columns = meta[...].T
    rowm[...] = jnp.zeros_like(rowm)
    first = 0
    for start, length in zip(START, SPAN):
        rows[8 + start : 8 + start + length, 0:FEAT] = frames[first : first + length]
        rowm[start : start + length, :] = columns[first : first + length]
        first = first + length
    ivs[...] = jnp.zeros_like(ivs)
    ivs[0:4, 0:IVEC] = ivecs[...].astype(F32)
    row = lax.broadcasted_iota(jnp.int32, (ROWS, 128), 0)
    lane = lax.broadcasted_iota(jnp.int32, (ROWS, 128), 1)
    iv = ivs[3:4, :]
    for k in (2, 1, 0):
        iv = jnp.where(row < START[k + 1], ivs[k : k + 1, :], iv)
    left = rows[7 : 7 + ROWS, :]
    left = jnp.where(lane < FEAT, left, pltpu.roll(rows[8 : 8 + ROWS, :], FEAT, 1))
    left = jnp.where(lane < 2 * FEAT, left, pltpu.roll(rows[9 : 9 + ROWS, :], 2 * FEAT, 1))
    left = jnp.where(lane < 3 * FEAT, left, pltpu.roll(iv, 3 * FEAT, 1))
    ones = 3 * FEAT + IVEC - 128
    right = jnp.where(lane < ones, pltpu.roll(iv, 3 * FEAT, 1), jnp.where(lane == ones, 1.0, 0.0))
    spl[:, 0:128] = left.astype(BF)
    spl[:, 128:256] = right.astype(BF)
    spl_t[0:128, :] = left.T.astype(BF)
    spl_t[128:256, :] = right.T.astype(BF)


def prepare(features, ivectors, frame_mask, labels, confidence):
    mask = frame_mask.astype(F32)
    meta = jnp.stack([mask, confidence * mask, jnp.ones_like(mask), labels.astype(F32)])
    meta = jnp.pad(meta, ((0, 4), (0, ROWS - mask.shape[0])))
    return kernel_call(
        prepare_kernel,
        [shape((ROWS, 256), BF), shape((256, ROWS), BF), shape((ROWS, 8))],
        "vvv",
        [vmem((ROWS + 16, 128)), vmem((8, 128))],
        name="prepare",
        us=2.0,
    )(features, ivectors, meta)


def on_device(
    features,
    ivectors,
    frame_mask,
    labels,
    confidence,
    weights,
    first_moment,
    second_moment,
    biases,
    bias_first,
    bias_second,
):
    n = lax.axis_size("dp")
    size = weights.shape[1]
    index = lax.axis_index("dp")
    fast = fits(n, size)
    me = index if fast else jnp.int32(0)
    place = me.reshape(1)
    blocks, (spliced, spl_t, rowm) = gather_blocks(
        weights, n, prepare, (features, ivectors, frame_mask, labels, confidence)
    )
    bias = biases[None]
    w_in = unpack_in(place, blocks)
    h1, gp1, st = layer_in(spliced, w_in, bias, rowm)
    if fast:
        tot1 = sum_core(st, n)
        w1a, w1b, w2a, w2b = unpack_mid(place, once(blocks, tot1))
        tot1 = sum_layers(tot1, n)
        tot1, w1a = lax.optimization_barrier((tot1, w1a))
        flat_out = flatten_out(place, once(blocks, tot1), 12, SPLIT - 1)
        tot1 = sum_plane(tot1, n)
        tot1, flat_out = lax.optimization_barrier((tot1, flat_out))
    else:
        tot1 = total(st, n)
        w1a, w1b, w2a, w2b = unpack_mid(place, blocks)
        flat_out = flatten_out(place, blocks, 12, SPLIT - 1)
        flat_two = flatten_out(place, blocks, SPLIT, 31)
    rounded, fac, fnext, h2, gp2, st = layer_mid(h1, tot1, w1a, w1b, w2a, w2b, bias, rowm)
    if fast:
        tot2 = sum_core(st, n)
        flat_two = flatten_out(place, once(blocks, tot2), SPLIT, 31)
        tot2 = sum_layers(tot2, n)
        tot2, flat_two = lax.optimization_barrier((tot2, flat_two))
        w_pre, w_out = unpack_out(flat_out, once(flat_two, tot2), h2)
        tot2 = sum_plane(tot2, n)
        tot2, w_pre = lax.optimization_barrier((tot2, w_pre))
    else:
        tot2 = total(st, n)
        w_pre, w_out = unpack_out(flat_out, flat_two, h2)
    summed, n2b, dpre, dsum, go, gbo, st, loss, pre = head(h1, tot1, h2, tot2, w_pre, w_out, bias, rowm)
    tot3 = sum_layers(sum_core(st, n), n) if fast else total(st, n)
    keep, send, edge, gbp = side_out(place, *once((summed, dpre, go), tot3))
    if fast:
        tot3 = sum_plane(tot3, n)
        tot3, keep = lax.optimization_barrier((tot3, keep))
    dact, dfac, dfnext, dn, st = back_mid(rounded, tot1, n2b, gp2, tot2, dsum, tot3, w1a, w1b, w2a, w2b, rowm)
    parts = (edge, fac, fnext, dact, rounded, dfac, dfnext, dn)
    if fast:
        tot4 = sum_core(st, n)
        keep, send, gbs = side_mid(place, keep, send, *once(parts, tot4))
        keep, send, tot4 = lax.optimization_barrier((keep, send, tot4))
        blocks = fold_core(keep, move(send, n, 1))
        tot4, blocks = lax.optimization_barrier((sum_plane(tot4, n), blocks))
        tot4 = sum_layers(tot4, n)
        a_keep, a_send, b_keep, b_send = blocks
        a_come, b_come = move(a_send, n, 2), move(b_send, n, 4)
    else:
        tot4 = total(st, n)
        keep, send, gbs = side_mid(place, keep, send, *parts)
    keep_in, send_in, gbi = back_in(place, rounded, gp1, tot1, dn, tot4, spl_t, rowm)
    if fast:
        first = fold_first(keep_in, move(send_in, n, 1))
        first = list(first)
        a_come, first[1] = lax.optimization_barrier((a_come, first[1]))
        first_keep, first_send, first_b = first
        first_a = (first_keep, move(first_send, n, 2))
        first_b = (first_b, move(first_b, n, 4, lambda t: (t & 4) == 0))
        a_keep, a_send, b_keep, b_send = fold_plane(place, a_keep, a_come, b_keep, b_come, *first_a, *first_b)
        parts = fold_layers(a_keep, move(a_send, n, 4), b_keep, move(b_send, n, 2))
        pre = once(pre, parts[0])
        parts = [parts[0]] + [move(parts[k], n, 8 * k) for k in (1, 2, 3)]
        loss = loss - picked_sum(pre, w_out, bias, rowm)
        grad, last = own_sums(place, *parts, gbi, gbs, gbp, gbo, loss, rowm)
        *new, loss_sum, loss_weight, norm = update(
            place, total(last, n), grad, weights, first_moment, second_moment, biases, bias_first, bias_second
        )
        return (*new, loss_sum.reshape(()), loss_weight.reshape(()), norm.reshape(()))
    in_order = lambda v: v.transpose(1, 0, 2, 3).reshape(16, BLK, 128)
    loss = loss - picked_sum(pre, w_out, bias, rowm)
    rows = to_rows(in_order(keep), in_order(send))
    rows = jnp.concatenate([rows[: 2 * CHIP] + to_rows(keep_in, send_in), rows[2 * CHIP :]], axis=0)
    grad = lax.psum_scatter(rows.astype(F32).reshape(n, size), "dp", scatter_dimension=0, tiled=True).reshape(-1)
    bias_grad = jnp.concatenate([gbi[4], gbs[0], gbp[0], gbo[0, :SEN]])
    extra = jnp.stack([jnp.sum(grad * grad), loss[0, 0], jnp.sum(rowm[:, 1])])
    last = total(jnp.concatenate([bias_grad, jnp.pad(extra, (0, 7 * 128 - 3))]).reshape(80, 128), n)
    return adam_all(last, grad, weights, first_moment, second_moment, biases, bias_first, bias_second)


def solution(mesh):
    return jax.shard_map(
        on_device,
        mesh=mesh,
        in_specs=(
            P("dp", None),
            P("dp", None),
            P("dp"),
            P("dp"),
            P("dp"),
            P("dp", None),
            P("dp", None),
            P("dp", None),
            P(),
            P(),
            P(),
        ),
        out_specs=(P("dp", None), P("dp", None), P("dp", None), P(), P(), P(), P(), P(), P()),
        check_vma=False,
    )
```
